32 devices in a mesh: seq: 16 (over z, x, core), dp: 2 (over y).
Axes of the slice: x: 2, y: 2, z: 4, core: 2. Of those that a mesh axis runs over, the one named last changes fastest.
Arguments:
- tokens: bfloat16 [2, 6272, 1024], P('dp', 'seq'), may hold values from -6 to 6
- clip_start: int32 [2, 32], P('dp', 'seq'), may hold values from 0 to 28, as said below
- frames: int32 [2, 32], P('dp', 'seq'), may hold values from 8 to 32, as said below
- positions: int32 [2, 3, 6272], P('dp', None, 'seq'), may hold values from 0 to 15, as said below
- first_gain: float32 [1024], replicated, may hold values from 0.5 to 1.5
- first_offset: float32 [1024], replicated, may hold values from -3 to 3
- triple_weight: bfloat16 [1024, 3072], replicated, may hold values from -0.1875 to 0.1875
- triple_bias: float32 [3072], replicated, may hold values from -0.75 to 0.75
- output_weight: bfloat16 [1024, 1024], replicated, may hold values from -3 to 3
- output_bias: float32 [1024], replicated, may hold values from -1.5 to 1.5
- second_gain: float32 [1024], replicated, may hold values from 0.5 to 1.5
- second_offset: float32 [1024], replicated, may hold values from -3 to 3
- expand_weight: bfloat16 [1024, 4096], replicated, may hold values from -0.1875 to 0.1875
- expand_bias: float32 [4096], replicated, may hold values from -3 to 3
- reduce_weight: bfloat16 [4096, 1024], replicated, may hold values from -0.09375 to 0.09375
- reduce_bias: float32 [1024], replicated, may hold values from -1.5 to 1.5
- cotangent: bfloat16 [2, 6272, 1024], P('dp', 'seq'), may hold values from -6 to 6
Outputs:
- result: bfloat16 [2, 6272, 1024], P('dp', 'seq')
- input_grad: float32 [2, 6272, 1024], P('dp', 'seq')
- grad_first_gain: float32 [1024], P(('seq', 'dp'))
- grad_first_offset: float32 [1024], P(('seq', 'dp'))
- grad_triple_weight: float32 [1024, 3072], P(('seq', 'dp'))
- grad_query_key_bias: float32 [2048], P(('seq', 'dp'))
- grad_value_bias: float32 [1024], P(('seq', 'dp'))
- grad_output_weight: float32 [1024, 1024], P(('seq', 'dp'))
- grad_output_bias: float32 [1024], P(('seq', 'dp'))
- grad_second_gain: float32 [1024], P(('seq', 'dp'))
- grad_second_offset: float32 [1024], P(('seq', 'dp'))
- grad_expand_weight: float32 [1024, 4096], P(('seq', 'dp'))
- grad_expand_bias: float32 [4096], P(('seq', 'dp'))
- grad_reduce_weight: float32 [4096, 1024], P(('seq', 'dp'))
- grad_reduce_bias: float32 [1024], P(('seq', 'dp'))
The draws below stay inside these ranges and needn't reach their ends.
Inputs may be any that keep to these rules, and one draw needn't show every extreme that they name: `clip_start`: each group's 32 slabs are split into whole clips of 4, 8 or 16 slabs that begin at multiples of 4; every slab of a clip holds the clip's first slab, and every group has a clip of 16 slabs. `frames`: twice the number of slabs of the slab's clip. `positions`: row 0 is the token's slab minus its clip's first slab; rows 1 and 2 are the token's row and column in its 14 x 14 frame plus an offset of 0 to 2 that is one for each clip and direction.
All inputs are finite; a program needn't handle non-finite values.
Results may differ from the reference program's by a relative error of at most 0.023.
Values may be sent and summed in bfloat16 or wider, within the bound.
No kernel may reach another device: no remote copies, remote signals or barrier semaphores. Data moves between devices by JAX's collectives and lax.ppermute only.
A program may use at most 384 MiB of HBM per device.

```python
import jax
import jax.numpy as jnp
from jax import lax

D = 1024
HEADS = 16
HEAD_DIM = 64
FF = 4096
GRID = 14
CLIP_MIN = 4
CLIP_MAX = 16
S_DEV = 2
SLAB = 196
GROUP_SLABS = 32
GROUP_TOKENS = 6272
N_DP = 2


def clip_layout(key):
    unit_count = GROUP_SLABS // CLIP_MIN
    long_units = CLIP_MAX // CLIP_MIN
    stride = max(S_DEV // CLIP_MIN, 1)
    first_unit = stride - 1
    spot_count = (unit_count - long_units - first_unit) // stride + 1
    token_ids = jnp.arange(GROUP_TOKENS, dtype=jnp.int32)

    def one_group(group_key):
        long_place = first_unit + stride * jax.random.randint(jax.random.fold_in(group_key, 1), (), 0, spot_count)
        pick_draw = jax.random.randint(jax.random.fold_in(group_key, 2), (unit_count,), 0, 3)
        wanted = jnp.where(pick_draw == 0, 1, jnp.where(pick_draw == 1, long_units // 2, long_units))
        row_offsets = jax.random.randint(jax.random.fold_in(group_key, 3), (unit_count,), 0, 3)
        col_offsets = jax.random.randint(jax.random.fold_in(group_key, 4), (unit_count,), 0, 3)

        def advance(state_in, scan_item):
            left_units, begin_unit, size_units = state_in
            unit_id, want_units = scan_item
            room_units = jnp.where(unit_id < long_place, long_place - unit_id, unit_count - unit_id)
            capped = jnp.minimum(want_units, room_units)
            capped = jnp.where(capped >= long_units, long_units, jnp.where(capped >= long_units // 2, long_units // 2, 1))
            at_place = unit_id == long_place
            starts_new = (left_units == 0) | at_place
            size_units = jnp.where(at_place, long_units, jnp.where(starts_new, capped, size_units))
            begin_unit = jnp.where(starts_new, unit_id, begin_unit)
            left_units = jnp.where(starts_new, size_units, left_units) - 1
            return ((left_units, begin_unit, size_units), (begin_unit, size_units))
        start_state = (jnp.int32(0), jnp.int32(0), jnp.int32(1))
        final_state, (begins, size_list) = lax.scan(advance, start_state, (jnp.arange(unit_count, dtype=jnp.int32), wanted))
        slab_start = jnp.repeat(begins * CLIP_MIN, CLIP_MIN)
        frame_count = jnp.repeat(size_list * CLIP_MIN * 2, CLIP_MIN)
        row_shift = jnp.repeat(row_offsets[begins], CLIP_MIN)
        col_shift = jnp.repeat(col_offsets[begins], CLIP_MIN)
        slab_of = token_ids // SLAB
        inside = token_ids % SLAB
        time_place = slab_of - slab_start[slab_of]
        row_place = inside // GRID + row_shift[slab_of]
        col_place = inside % GRID + col_shift[slab_of]
        return (slab_start, frame_count, jnp.stack([time_place, row_place, col_place]))
    starts_all = []
    frames_all = []
    places_all = []
    for group_id in range(N_DP):
        slab_start, frame_count, places = one_group(jax.random.fold_in(key, 100 + group_id))
        starts_all.append(slab_start)
        frames_all.append(frame_count)
        places_all.append(places)
    return (jnp.stack(starts_all).astype(jnp.int32), jnp.stack(frames_all).astype(jnp.int32), jnp.stack(places_all).astype(jnp.int32))


def draw_clip_start(key, part):
    return clip_layout(key)[0]


def draw_frames(key, part):
    return clip_layout(key)[1]


def draw_positions(key, part):
    return clip_layout(key)[2]


def block_scale(own_key, dims, shards, least, high):
    loudness = 1.0
    for axis_at, blocks in shards:
        steps = jax.random.uniform(jax.random.fold_in(jax.random.fold_in(own_key, 6), axis_at), (blocks,), jnp.float32, least / len(shards), high / len(shards))
        loudness = loudness * jnp.repeat(jnp.exp(steps), dims[axis_at] // blocks).reshape((-1,) + (1,) * (len(dims) - 1 - axis_at))
    return loudness


def normal_values(stream_key, shape, width, bound, split=(), kind=jnp.bfloat16):
    result = jax.random.normal(stream_key, shape, jnp.float32) * width
    if len(split) > 0:
        result = block_scale(stream_key, shape, split, -0.22, 0.18) * result
    return jnp.clip(result, min=-bound, max=bound).astype(kind)


def setup_inputs(seed: int = 0) -> dict:
    keys = jax.random.split(jax.random.key(seed), 18)
    tokens = normal_values(keys[0], (N_DP, GROUP_TOKENS, D), 1.0, 6.0, ((0, 2), (1, 16)))
    clip_start = draw_clip_start(jax.random.fold_in(keys[17], 71), 0)
    frames = draw_frames(jax.random.fold_in(keys[17], 71), 0)
    positions = draw_positions(jax.random.fold_in(keys[17], 71), 0)
    first_gain = jnp.clip(1.0 + 0.1 * jax.random.normal(keys[4], (D,), jnp.float32), 0.5, 1.5)
    first_offset = normal_values(keys[5], (D,), 0.2, 3.0, (), jnp.float32)
    triple_weight = normal_values(keys[6], (D, 3 * D), D ** -0.5, 0.1875)
    triple_bias = normal_values(keys[7], (3 * D,), 0.05, 0.75, (), jnp.float32)
    output_weight = normal_values(keys[8], (D, D), 4 ** -0.5, 3.0)
    output_bias = normal_values(keys[9], (D,), 0.1, 1.5, (), jnp.float32)
    second_gain = jnp.clip(1.0 + 0.1 * jax.random.normal(keys[10], (D,), jnp.float32), 0.5, 1.5)
    second_offset = normal_values(keys[11], (D,), 0.2, 3.0, (), jnp.float32)
    expand_weight = normal_values(keys[12], (D, FF), D ** -0.5, 0.1875)
    expand_bias = normal_values(keys[13], (FF,), 0.2, 3.0, (), jnp.float32)
    reduce_weight = normal_values(keys[14], (FF, D), FF ** -0.5, 0.09375)
    reduce_bias = normal_values(keys[15], (D,), 0.1, 1.5, (), jnp.float32)
    cotangent = normal_values(keys[16], (N_DP, GROUP_TOKENS, D), 1.0, 6.0, ((0, 2), (1, 16)))
    return {"tokens": tokens, "clip_start": clip_start, "frames": frames, "positions": positions, "first_gain": first_gain, "first_offset": first_offset, "triple_weight": triple_weight, "triple_bias": triple_bias, "output_weight": output_weight, "output_bias": output_bias, "second_gain": second_gain, "second_offset": second_offset, "expand_weight": expand_weight, "expand_bias": expand_bias, "reduce_weight": reduce_weight, "reduce_bias": reduce_bias, "cotangent": cotangent}


EPSILON = 1e-06
NEGATIVE = -1e+30
SECTIONS = ((0, 10, 0), (20, 11, 10), (42, 11, 21))
HIGHEST = lax.Precision.HIGHEST

@jax.custom_vjp
def low(v):
    return lax.optimization_barrier(v.astype(jnp.bfloat16)).astype(jnp.float32)

@jax.custom_vjp
def low_back(v):
    return v

def low_keep(v):
    return (low(v), None)

def low_pass(kept, grad):
    return (grad,)

def back_keep(v):
    return (v, None)

def back_low(kept, grad):
    return (low(grad),)
low.defvjp(low_keep, low_pass)
low_back.defvjp(back_keep, back_low)

def layer_norm(inputs, norm_gain, norm_offset):
    centred = inputs - lax.optimization_barrier(jnp.mean(inputs, axis=-1, keepdims=True))
    spread = lax.optimization_barrier(jnp.mean(centred * centred, axis=-1, keepdims=True))
    return centred * lax.rsqrt(spread + EPSILON) * norm_gain + norm_offset

def rotary_tables(positions):
    angles = []
    for section, (begin_at, pair_count, first_pair) in enumerate(SECTIONS):
        frequency = jnp.power(10000.0, -jnp.arange(pair_count, dtype=jnp.float32) / pair_count)
        angles.append(positions[..., section, :].astype(jnp.float32)[..., None] * frequency)
    joined = jnp.concatenate(angles, axis=-1)
    return (jnp.cos(joined), jnp.sin(joined))

def rotate(inputs, cos_table, sin_table):
    pieces = []
    for begin_at, pair_count, first_pair in SECTIONS:
        low_half = inputs[..., begin_at:begin_at + pair_count]
        high_half = inputs[..., begin_at + pair_count:begin_at + 2 * pair_count]
        cos_part = cos_table[..., None, first_pair:first_pair + pair_count]
        sin_part = sin_table[..., None, first_pair:first_pair + pair_count]
        pieces.append(low_half * cos_part - high_half * sin_part)
        pieces.append(high_half * cos_part + low_half * sin_part)
    return jnp.concatenate(pieces, axis=-1)

def slab_bounds(clip_start, frames, first_slab, group_slabs):
    slab_index = first_slab + jnp.arange(clip_start.shape[-1], dtype=jnp.int32)
    unit_base = slab_index // CLIP_MIN * CLIP_MIN
    lower_slab = jnp.maximum(jnp.maximum(jnp.minimum(clip_start, slab_index), unit_base - (CLIP_MAX - CLIP_MIN)), 0)
    upper_slab = jnp.minimum(jnp.minimum(jnp.maximum(clip_start + frames // 2, slab_index + 1), unit_base + CLIP_MAX), group_slabs)
    return (lower_slab, upper_slab, slab_index)

def reference(tokens, clip_start, frames, positions, first_gain, first_offset, triple_weight, triple_bias, output_weight, output_bias, second_gain, second_offset, expand_weight, expand_bias, reduce_weight, reduce_bias, cotangent):
    group_count, group_tokens, model_width = tokens.shape
    lower_slab, upper_slab, slab_index = slab_bounds(clip_start, frames, 0, GROUP_SLABS)
    query_lower = jnp.repeat(lower_slab, SLAB, axis=1)
    query_upper = jnp.repeat(upper_slab, SLAB, axis=1)
    cos_table, sin_table = rotary_tables(positions)
    unit_count = GROUP_SLABS // CLIP_MIN
    block_rows = CLIP_MIN * SLAB
    margin = (CLIP_MAX - CLIP_MIN) * SLAB
    window = (2 * CLIP_MAX - CLIP_MIN) * SLAB
    window_slabs = jnp.repeat(jnp.arange(2 * CLIP_MAX - CLIP_MIN, dtype=jnp.int32), SLAB)

    def attend(queries, keys_all, values_all):
        keys_pad = jnp.pad(keys_all, ((0, 0), (margin, margin), (0, 0), (0, 0)))
        values_pad = jnp.pad(values_all, ((0, 0), (margin, margin), (0, 0), (0, 0)))

        def one_block(block_id):
            group_id = block_id // unit_count
            unit_id = block_id % unit_count
            first_row = unit_id * block_rows
            anchor = jnp.zeros((), jnp.int32)
            block_query = lax.dynamic_slice(queries, (group_id, first_row, anchor, anchor), (1, block_rows, HEADS, HEAD_DIM))[0]
            block_keys = lax.dynamic_slice(keys_pad, (group_id, first_row, anchor, anchor), (1, window, HEADS, HEAD_DIM))[0]
            block_values = lax.dynamic_slice(values_pad, (group_id, first_row, anchor, anchor), (1, window, HEADS, HEAD_DIM))[0]
            lower_row = lax.dynamic_slice(query_lower, (group_id, first_row), (1, block_rows))[0]
            upper_row = lax.dynamic_slice(query_upper, (group_id, first_row), (1, block_rows))[0]
            key_slab = unit_id * CLIP_MIN - (CLIP_MAX - CLIP_MIN) + window_slabs
            allowed = (lower_row[:, None] <= key_slab[None, :]) & (key_slab[None, :] < upper_row[:, None])
            scores = low_back(jnp.einsum('qhd,khd->hqk', block_query, block_keys, precision=HIGHEST) * 0.125)
            attend_prob = jax.nn.softmax(jnp.where(allowed[None], scores, NEGATIVE), axis=-1)
            return jnp.einsum('hqk,khd->qhd', low(attend_prob), block_values, precision=HIGHEST)
        blocks = lax.map(jax.checkpoint(one_block), jnp.arange(group_count * unit_count, dtype=jnp.int32))
        return blocks.reshape(group_count, group_tokens, HEADS, HEAD_DIM)

    def forward(inputs, gain_one, offset_one, weight_triple, bias_triple, weight_output, bias_output, gain_two, offset_two, weight_expand, bias_expand, weight_reduce, bias_reduce):
        flat = inputs.reshape(-1, model_width)
        normed = low(layer_norm(flat, gain_one, offset_one))
        triple = low_back(jnp.dot(normed, weight_triple, precision=HIGHEST) + bias_triple)
        shaped = triple.reshape(group_count, group_tokens, 3, HEADS, HEAD_DIM)
        query_rot = low(rotate(shaped[:, :, 0], cos_table, sin_table))
        key_rot = low(rotate(shaped[:, :, 1], cos_table, sin_table))
        value_low = low(shaped[:, :, 2])
        attended = low_back(low(attend(query_rot, key_rot, value_low).reshape(-1, model_width)))
        hidden = flat + low_back(jnp.dot(attended, weight_output, precision=HIGHEST) + bias_output)

        def feed_forward(hidden_block):
            normed_two = low(layer_norm(hidden_block, gain_two, offset_two))
            expanded = low_back(jnp.dot(normed_two, weight_expand, precision=HIGHEST) + bias_expand)
            activated = low(jax.nn.gelu(expanded, approximate=False))
            return hidden_block + low_back(jnp.dot(activated, weight_reduce, precision=HIGHEST) + bias_reduce)
        outcome = lax.map(jax.checkpoint(feed_forward), hidden.reshape(-1, block_rows, model_width))
        return outcome.reshape(group_count, group_tokens, model_width)
    outcome, pull_back = jax.vjp(forward, tokens.astype(jnp.float32), first_gain, first_offset, triple_weight.astype(jnp.float32), triple_bias, output_weight.astype(jnp.float32), output_bias, second_gain, second_offset, expand_weight.astype(jnp.float32), expand_bias, reduce_weight.astype(jnp.float32), reduce_bias)
    grads = pull_back(cotangent.astype(jnp.float32))
    bias_grad = grads[4]
    return (outcome.astype(jnp.bfloat16), grads[0], grads[1], grads[2], grads[3], bias_grad[:2 * model_width], bias_grad[2 * model_width:], grads[5], grads[6], grads[7], grads[8], grads[9], grads[10], grads[11], grads[12])
```

```python
import jax
import jax.numpy as jnp
from jax import lax
from jax.experimental import pallas as pl
from jax.experimental.pallas import tpu as pltpu
from jax.sharding import PartitionSpec as P

HEAD_DIM = 64
CLIP_MIN = 4
CLIP_MAX = 16
EPSILON = 1e-06
MASKED = 1e30
SECTIONS = ((0, 10), (20, 11), (42, 11))
LANES = 128
F32 = jnp.float32
BF16 = jnp.bfloat16
VMEM_LIMIT = 63 * 2**20
Q_TILE = 256
SAFE_ABOVE = 60.0
BACK_SHARE = (3, 4)


def dot(left, right):
    return jnp.dot(left, right, preferred_element_type=F32)


def dot_cols(left, right):
    return lax.dot_general(left, right, (((1,), (1,)), ((), ())), preferred_element_type=F32)


def dot_rows(left, right):
    return lax.dot_general(left, right, (((0,), (0,)), ((), ())), preferred_element_type=F32)


def cost(micros):
    return pl.CostEstimate(flops=int(micros * 1.15e9), bytes_accessed=2**20, transcendentals=0)


def params(**more):
    return pltpu.CompilerParams(vmem_limit_bytes=VMEM_LIMIT, **more)


def lane_index(shape):
    return lax.broadcasted_iota(jnp.int32, shape, len(shape) - 1)


def swap_halves(pair):
    return pltpu.roll(pair, HEAD_DIM, 1)


def rotate_pair(pair, cos_lanes, sin_lanes, inverse):
    lane = lane_index((1, LANES)) % HEAD_DIM
    sign = -1.0 if inverse else 1.0
    total = pair * cos_lanes
    for half in (10, 11):
        first = jnp.zeros(lane.shape, jnp.bool_)
        second = jnp.zeros(lane.shape, jnp.bool_)
        for begin_at, count in SECTIONS:
            if count == half:
                first = first | ((lane >= begin_at) & (lane < begin_at + half))
                second = second | ((lane >= begin_at + half) & (lane < begin_at + 2 * half))
        minus = jnp.where(first, -sign, 0.0)
        plus = jnp.where(second, sign, 0.0)
        total = total + pltpu.roll(pair, LANES - half, 1) * (sin_lanes * minus)
        total = total + pltpu.roll(pair, half, 1) * (sin_lanes * plus)
    return total


def lane_tables(positions):
    angles = jnp.zeros((positions.shape[1], LANES), F32)
    for section, (begin_at, count) in enumerate(SECTIONS):
        frequency = jnp.power(10000.0, -jnp.arange(count, dtype=F32) / count)
        in_head = jnp.zeros((HEAD_DIM,), F32)
        in_head = in_head.at[begin_at : begin_at + count].set(frequency)
        in_head = in_head.at[begin_at + count : begin_at + 2 * count].set(frequency)
        lanes = jnp.tile(in_head, LANES // HEAD_DIM)
        angles = angles + positions[section].astype(F32)[:, None] * lanes[None, :]
    return jnp.cos(angles), jnp.sin(angles)


def all_turns(places):
    spots = jnp.arange(16)
    table = []
    for section in range(len(SECTIONS)):
        only = jnp.where(jnp.arange(len(SECTIONS))[:, None] == section, spots[None, :], 0)
        cos, sin = lane_tables(only)
        lane = jnp.arange(LANES)
        begin_at, count = SECTIONS[section]
        inside = (lane % HEAD_DIM >= begin_at) & (lane % HEAD_DIM < begin_at + 2 * count)
        table.append(jnp.where(inside, jnp.where(lane < HEAD_DIM, cos, sin), 0.0))
    table = jnp.concatenate(table, axis=0)
    hit = places.astype(jnp.int32).transpose(0, 2, 1)[..., None] == spots
    hit = hit.reshape(hit.shape[:2] + table.shape[:1]).astype(F32)
    hit = jnp.pad(hit, ((0, 0), (0, -hit.shape[1] % 16), (0, 0))).reshape(-1, table.shape[0])
    return jnp.dot(hit, table, precision=lax.Precision.HIGHEST)


def slab_bounds(clip_start, frames, first_slab, group_slabs):
    slab_index = first_slab + jnp.arange(clip_start.shape[-1], dtype=jnp.int32)
    unit_base = slab_index // CLIP_MIN * CLIP_MIN
    lower_slab = jnp.maximum(
        jnp.maximum(jnp.minimum(clip_start, slab_index), unit_base - (CLIP_MAX - CLIP_MIN)), 0
    )
    upper_slab = jnp.minimum(
        jnp.minimum(jnp.maximum(clip_start + frames // 2, slab_index + 1), unit_base + CLIP_MAX),
        group_slabs,
    )
    return lower_slab, upper_slab


def norm_parts(rows):
    centred = rows - jnp.mean(rows, axis=-1, keepdims=True)
    spread = jnp.mean(centred * centred, axis=-1, keepdims=True)
    scale = lax.rsqrt(spread + EPSILON)
    return centred * scale, scale


def norm_back(grad, rows, gain):
    unit, scale = norm_parts(rows)
    inner = grad * gain
    part = scale * (
        inner
        - jnp.mean(inner, axis=-1, keepdims=True)
        - unit * jnp.mean(inner * unit, axis=-1, keepdims=True)
    )
    return part, jnp.sum(grad * unit, axis=0, keepdims=True), jnp.sum(grad, axis=0, keepdims=True)


class Sizes:
    def __init__(self, rows, width, ff, n, m, slabs):
        self.rows = rows
        self.width = width
        self.ff = ff
        self.n = n
        self.m = m
        self.heads = width // HEAD_DIM
        self.rep = n // self.heads
        self.shards = n * m
        self.per_unit = CLIP_MIN // slabs
        self.units = n // self.per_unit
        self.slot = (rows + 15) // 16 * 16
        self.unit_rows = self.slot * self.per_unit
        self.tokens = self.slot * n
        self.fold = (rows // 2 + 15) // 16 * 16
        self.rest = rows - self.fold
        self.msg = self.slot + self.fold


def pad_rows(block, count):
    if block.shape[0] == count:
        return block
    return jnp.concatenate([block, jnp.zeros((count - block.shape[0], block.shape[1]), F32)], axis=0)


def fold_head(block, sz, right):
    low = block[: sz.fold]
    high = pad_rows(block[sz.fold :], sz.fold)
    left = lane_index(low.shape) < HEAD_DIM
    if right:
        folded = jnp.where(left, swap_halves(low), high)
    else:
        folded = jnp.where(left, low, swap_halves(high))
    return folded


def project_kernel(sz, tok, gain, offset, wq, wk, wv, bq, bk, bv, cos, sin, meta, msg, normed_out):
    step = pl.program_id(0)

    @pl.when(step == 0)
    def _():
        unit, _ = norm_parts(tok[...].astype(F32))
        normed_out[...] = (unit * gain[...] + offset[...]).astype(BF16)

    normed = normed_out[...]
    query = dot(normed, wq[...]) + bq[...]
    key = dot(normed, wk[...]) + bk[...]
    value = dot(normed, wv[...]) + bv[...]
    left = lane_index((sz.rows, LANES)) < HEAD_DIM
    spare = sz.slot - sz.rows
    facts = jnp.concatenate([jnp.zeros((sz.fold - 8, LANES), F32), meta[...]], axis=0)
    for pair in range(query.shape[1] // LANES):
        cols = slice(pair * LANES, (pair + 1) * LANES)
        q_pair = rotate_pair(query[:, cols], cos[...], sin[...], False) * 0.125
        k_pair = rotate_pair(key[:, cols], cos[...], sin[...], False)
        v_pair = value[:, cols]
        both = (jnp.where(left, k_pair, swap_halves(v_pair)), jnp.where(left, swap_halves(k_pair), v_pair))
        for head in range(2):
            tail = jnp.where(left[:spare], both[head][sz.rows - spare :], 0.0)
            folded = fold_head(q_pair, sz, head == 1) + facts
            rows = jnp.concatenate([both[head], tail, folded], axis=0)
            msg[2 * pair + head] = rows.astype(BF16)


def project(sz, tokens, gain, offset, weight, bias, cos, sin, meta):
    cols = 256
    steps = sz.width // cols
    whole = lambda shape: pl.BlockSpec(shape, lambda j: (0,) * len(shape))
    part = lambda k: pl.BlockSpec((sz.width, cols), lambda j: (0, k * steps + j))
    part_bias = lambda k: pl.BlockSpec((1, cols), lambda j: (0, k * steps + j))
    heads = cols // HEAD_DIM
    return pl.pallas_call(
        lambda *refs: project_kernel(sz, *refs),
        grid=(steps,),
        in_specs=[whole((sz.rows, sz.width)), whole((1, sz.width)), whole((1, sz.width))]
        + [part(0), part(1), part(2), part_bias(0), part_bias(1), part_bias(2)]
        + [whole((sz.rows, LANES)), whole((sz.rows, LANES)), whole((8, LANES))],
        out_specs=[
            pl.BlockSpec((heads, sz.msg, LANES), lambda j: (j, 0, 0)),
            whole((sz.rows, sz.width)),
        ],
        out_shape=[
            jax.ShapeDtypeStruct((sz.heads, sz.msg, LANES), BF16),
            jax.ShapeDtypeStruct((sz.rows, sz.width), BF16),
        ],
        compiler_params=params(),
        cost_estimate=cost(8),
        name="project",
    )(tokens, gain, offset, weight, weight, weight, bias, bias, bias, cos, sin, meta)


def unfold_slot(folded, sz, right):
    wide = folded.astype(F32)
    left = lane_index(wide.shape) < HEAD_DIM
    keep = ~left if right else left
    swapped = swap_halves(wide)
    low, high = (swapped, wide) if right else (wide, swapped)
    return (
        jnp.where(keep, low, 0.0).astype(BF16),
        jnp.where(keep, high, 0.0)[: sz.slot - sz.fold].astype(BF16),
    )


def unfold_into(target, at, folded, sz, right):
    low, high = unfold_slot(folded, sz, right)
    target[pl.ds(at, sz.fold), :] = low
    target[pl.ds(at + sz.fold, sz.slot - sz.fold), :] = high


def loop(count, body):
    def step(index, carry):
        body(index)
        return carry

    lax.fori_loop(0, count, step, 0)


def attend_kernel(sz, first, count, recv, out, kept, qs, kvs, ones_v):
    def unpack(src):
        at = pl.multiple_of(src * sz.slot, 16)
        unfold_into(qs, at, recv[src, sz.slot :, :], sz, False)
        kv = recv[src, 0 : sz.slot, :]
        kvs[pl.ds(at, sz.slot), :] = kv
        left = lane_index((1, LANES)) < HEAD_DIM
        real = lax.broadcasted_iota(jnp.int32, (sz.slot, 1), 0) < sz.rows
        one = jnp.where(real, 1.0, 0.0)
        ones_v[pl.ds(at, sz.slot), :] = jnp.where(left, one, kv.astype(F32)).astype(BF16)

    loop(sz.n, unpack)
    qs[sz.tokens :, :] = jnp.zeros((Q_TILE, LANES), BF16)
    kept[sz.tokens :, :] = jnp.zeros((Q_TILE, LANES), F32)

    def one(unit):
        rows = pl.ds(pl.multiple_of(unit * sz.unit_rows, 16), sz.unit_rows)
        begin = pl.multiple_of(first[unit] * sz.unit_rows, 16)

        def keep(shift, mixed):
            total = mixed[:, 0:1]
            left = lane_index((1, LANES)) < HEAD_DIM
            kept[rows, :] = jnp.where(left, shift + jnp.log(total), mixed * (1.0 / total))

        for span in (1, 2, 4):

            @pl.when(count[unit] == span)
            def _():
                clip = pl.ds(begin, span * sz.unit_rows)
                some = dot_cols(qs[rows, :], kvs[pl.ds(begin, 2 * LANES), :])
                shift = jnp.max(some, axis=1, keepdims=True)
                scores = dot_cols(qs[rows, :], kvs[clip, :])
                prob = jnp.exp(scores - shift).astype(BF16)
                keep(shift, dot(prob, ones_v[clip, :]))
                above = jnp.max(jnp.max(scores, axis=1, keepdims=True) - shift)

                @pl.when(above > SAFE_ABOVE)
                def _():
                    scores = dot_cols(qs[rows, :], kvs[clip, :])
                    peak = jnp.max(scores, axis=1, keepdims=True)
                    prob = jnp.exp(scores - peak).astype(BF16)
                    keep(peak, dot(prob, ones_v[clip, :]))

    loop(sz.units, one)

    def pack(src):
        at = pl.multiple_of(src * sz.slot, 16)
        out[src] = fold_head(kept[pl.ds(at, sz.slot), :][: sz.rows], sz, True).astype(BF16)
        left = lane_index((sz.slot - sz.rows, LANES)) < HEAD_DIM
        kept[pl.ds(at + sz.rows, sz.slot - sz.rows), :] = jnp.where(left, MASKED, 0.0)

    loop(sz.n, pack)


def attend(sz, first, count, recv):
    smem = pl.BlockSpec(memory_space=pltpu.SMEM)
    vmem = pl.BlockSpec(memory_space=pltpu.VMEM)
    shape = jax.ShapeDtypeStruct
    return pl.pallas_call(
        lambda *refs: attend_kernel(sz, *refs),
        in_specs=[smem, smem, vmem],
        out_specs=[vmem] * 4,
        out_shape=[
            shape((sz.n, sz.fold, LANES), BF16),
            shape((sz.tokens + Q_TILE, LANES), F32),
            shape((sz.tokens + Q_TILE, LANES), BF16),
            shape((sz.tokens, LANES), BF16),
        ],
        scratch_shapes=[pltpu.VMEM((sz.tokens, LANES), BF16)],
        compiler_params=params(),
        cost_estimate=cost(32),
        name="attend",
    )(first, count, recv)


def back_tiles(sz, part, first, count, qs, kvs, dos, kept, grad_q, grad_kv, key_t):
    def one(unit):
        begin = pl.multiple_of(unit * sz.unit_rows, 16)
        for span in (1, 2, 4):

            @pl.when((count[unit] == span) & (first[unit] == unit))
            def _():
                length = span * sz.unit_rows
                clip = pl.ds(begin, length)
                turned = kvs[clip, :].astype(F32).T[:HEAD_DIM]
                real = lax.rem(lane_index((1, length)), sz.slot) < sz.rows
                key_t[:, 0:length] = jnp.where(real, turned, 0.0).astype(BF16)

                def q_tile(t, carry):
                    rows = pl.ds(pl.multiple_of(begin + t * Q_TILE, 16), Q_TILE)
                    query = qs[rows, :]
                    grad = dos[rows, :]
                    kept_rows = kept[rows, :]
                    left = lane_index((Q_TILE, LANES)) < HEAD_DIM
                    turned = jnp.where(left, kept_rows, kept_rows * grad.astype(F32)).T
                    inside = lane_index((1, Q_TILE)) < length - t * Q_TILE
                    log_total = jnp.where(inside, turned[0:1, :], MASKED)
                    delta = jnp.sum(turned[HEAD_DIM:, :], axis=0, keepdims=True)
                    keys = kvs[clip, :]
                    prob = jnp.exp(dot_cols(keys, query) - log_total)
                    grad_prob = dot_cols(keys, grad)
                    grad_scores = (prob * (grad_prob - delta)).astype(BF16)
                    grad_kv[clip, :] += dot(grad_scores, query) + dot(prob.astype(BF16), grad)
                    grad_query = dot(key_t[:, 0:length], grad_scores) * 0.125
                    grad_query = jnp.concatenate([grad_query, jnp.zeros_like(grad_query)], axis=0).T
                    if part == 1:
                        own = lax.broadcasted_iota(jnp.int32, (Q_TILE, 1), 0) < length - t * Q_TILE
                        grad_query = jnp.where(own, grad_query, grad_q[rows, :])
                    grad_q[rows, :] = grad_query
                    return carry

                tiles = (length + Q_TILE - 1) // Q_TILE
                middle = (tiles * BACK_SHARE[0] + BACK_SHARE[1] - 1) // BACK_SHARE[1]
                lax.fori_loop(*((0, middle) if part == 0 else (middle, tiles)), q_tile, 0)

    loop(sz.units, one)


def back_first_kernel(sz, first, count, recv_grad, qs, kvs, kept, dos, grad_q, grad_kv, key_t):
    dos[sz.tokens :, :] = jnp.zeros((Q_TILE, LANES), BF16)

    def unpack(src):
        at = pl.multiple_of(src * sz.slot, 16)
        unfold_into(dos, at, recv_grad[src], sz, True)
        grad_kv[pl.ds(at, sz.slot), :] = jnp.zeros((sz.slot, LANES), F32)

    loop(sz.n, unpack)
    back_tiles(sz, 0, first, count, qs, kvs, dos, kept, grad_q, grad_kv, key_t)


def back_last_kernel(
    sz, first, count, dos, qs, kvs, kept, grad_q_in, grad_kv_in, turns, out, grad_q, grad_kv, key_t
):
    def copy(src):
        rows = pl.ds(pl.multiple_of(src * sz.slot, 16), sz.slot)
        grad_q[rows, :] = grad_q_in[rows, :]
        grad_kv[rows, :] = grad_kv_in[rows, :]

    loop(sz.n, copy)
    back_tiles(sz, 1, first, count, qs, kvs, dos, kept, grad_q, grad_kv, key_t)

    def pack(src):
        rows = pl.ds(pl.multiple_of(src * sz.slot, 16), sz.slot)
        kv = grad_kv[rows, :]
        left = lane_index((1, LANES)) < HEAD_DIM
        real = lax.broadcasted_iota(jnp.int32, (sz.slot, 1), 0) < sz.rows
        both = jnp.where(left, grad_q[rows, :], swap_halves(kv))
        table = turns[rows, :]
        other = swap_halves(table)
        both = rotate_pair(both, jnp.where(left, table, other), jnp.where(left, other, table), True)
        out[src, 0 : sz.slot, :] = jnp.where(real, jnp.where(left, swap_halves(both), kv), 0.0).astype(BF16)
        out[src, sz.slot :, :] = fold_head(both[: sz.rows], sz, False).astype(BF16)

    loop(sz.n, pack)


def attend_back_first(sz, first, count, recv_grad, qs, kvs, kept):
    smem = pl.BlockSpec(memory_space=pltpu.SMEM)
    vmem = pl.BlockSpec(memory_space=pltpu.VMEM)
    shape = jax.ShapeDtypeStruct
    return pl.pallas_call(
        lambda *refs: back_first_kernel(sz, *refs),
        in_specs=[smem, smem] + [vmem] * 4,
        out_specs=[vmem] * 3,
        out_shape=[
            shape((sz.tokens + Q_TILE, LANES), BF16),
            shape((sz.tokens + Q_TILE, LANES), F32),
            shape((sz.tokens, LANES), F32),
        ],
        scratch_shapes=[pltpu.VMEM((HEAD_DIM, CLIP_MAX // CLIP_MIN * sz.unit_rows), BF16)],
        compiler_params=params(),
        cost_estimate=cost(40),
        name="attend_back_first",
    )(first, count, recv_grad, qs, kvs, kept)


def attend_back_last(sz, first, count, dos, qs, kvs, kept, grad_q, grad_kv, turns):
    smem = pl.BlockSpec(memory_space=pltpu.SMEM)
    vmem = pl.BlockSpec(memory_space=pltpu.VMEM)
    shape = jax.ShapeDtypeStruct
    return pl.pallas_call(
        lambda *refs: back_last_kernel(sz, *refs),
        in_specs=[smem, smem] + [vmem] * 7,
        out_specs=vmem,
        out_shape=shape((sz.n, sz.msg, LANES), BF16),
        scratch_shapes=[
            pltpu.VMEM((sz.tokens + Q_TILE, LANES), F32),
            pltpu.VMEM((sz.tokens, LANES), F32),
            pltpu.VMEM((HEAD_DIM, CLIP_MAX // CLIP_MIN * sz.unit_rows), BF16),
        ],
        compiler_params=params(),
        cost_estimate=cost(20),
        name="attend_back_last",
    )(first, count, dos, qs, kvs, kept, grad_q, grad_kv, turns)


def triple_grad_kernel(sz, grads, normed, out, total):
    step = pl.program_id(0)
    high = sz.slot - sz.fold
    part_kv = jnp.zeros((LANES, sz.width), F32)
    part_q = jnp.zeros((HEAD_DIM, sz.width), F32)
    sums = jnp.zeros((1, 2 * LANES), F32)
    for src in range(grads.shape[0]):
        key_value = grads[src, 0 : sz.slot, :]
        query = grads[src, sz.slot :, :]
        part_kv = part_kv + dot_rows(key_value, normed[src])
        part_q = part_q + dot_rows(query, normed[src, 0 : sz.fold, :])[:HEAD_DIM]
        part_q = part_q + dot_rows(query[:high], normed[src, sz.fold :, :])[HEAD_DIM:]
        sum_kv = jnp.sum(key_value.astype(F32), axis=0, keepdims=True)
        sum_q = jnp.sum(query.astype(F32), axis=0, keepdims=True)
        sums = sums + jnp.concatenate([sum_kv, sum_q + swap_halves(sum_q)], axis=1)

    @pl.when(step == 0)
    def _():
        total[...] = jnp.zeros_like(total)

    total[0:LANES, :] += part_kv
    total[LANES : LANES + HEAD_DIM, :] += part_q
    total[2 * LANES :, 0 : 2 * LANES] += jnp.broadcast_to(sums, (8, 2 * LANES))

    @pl.when(step == pl.num_programs(0) - 1)
    def _():
        few = sz.width // sz.shards
        bias = total[2 * LANES : 2 * LANES + 1, 0 : 2 * LANES]
        place = lax.broadcasted_iota(jnp.int32, (sz.width, 1), 0) % few
        left = lane_index((1, LANES)) < HEAD_DIM
        out[:, 0:LANES] = total[0:LANES, :].T
        queries = total[LANES : 2 * LANES, :].T
        kv_row, q_row = bias[:, 0:LANES], bias[:, LANES:]
        side = jnp.where(place == 0, swap_halves(kv_row), jnp.where(place == 1, kv_row, q_row))
        out[:, LANES:] = jnp.where(left, queries, side)


def triple_grad(sz, grads, normed_all):
    shape = jax.ShapeDtypeStruct
    last = sz.n // 2 - 1
    return pl.pallas_call(
        lambda *refs: triple_grad_kernel(sz, *refs),
        grid=(sz.n // 2,),
        in_specs=[
            pl.BlockSpec((2, sz.msg, LANES), lambda j: (j, 0, 0)),
            pl.BlockSpec((2, sz.slot, sz.width), lambda j: (jnp.where(j % 2 == 0, j // 2, last - j // 2), 0, 0)),
        ],
        out_specs=pl.BlockSpec((sz.width, 2 * LANES), lambda j: (0, 0)),
        out_shape=shape((sz.width, 2 * LANES), F32),
        scratch_shapes=[pltpu.VMEM((2 * LANES + 8, sz.width), F32)],
        compiler_params=params(),
        cost_estimate=cost(1),
        name="triple_grad",
    )(grads, normed_all)


def choose(pieces, index):
    picked = pieces[0]
    for at in range(1, len(pieces)):
        picked = jnp.where(index == at, pieces[at], picked)
    return picked


def core_cols(block, width, side):
    count = block.shape[1] // (2 * width)
    groups = [block[:, g * width : (g + 1) * width] for g in range(2 * count)]
    return jnp.concatenate([choose(groups[2 * g : 2 * g + 2], side) for g in range(count)], axis=1)


def feed_kernel(sz, place, tok, heads_in, wo, bo, gain, offset, we, be, wr, br, cot, *refs):
    result, grad_hidden, msg, shared, act_own, grad_be, grad_gain, grad_offset, grad_bo, grad_br = refs[:10]
    hidden, reduced, grad_normed = refs[10:]
    step = pl.program_id(0)
    core = place[0]
    left = lane_index((sz.fold, LANES)) < HEAD_DIM
    normed = shared.at[:, sz.ff : sz.ff + sz.width]
    attended = shared.at[:, sz.ff + sz.width : sz.ff + 2 * sz.width]

    @pl.when(step == 0)
    def _():
        for pair in range(sz.heads // 2):
            a = heads_in[2 * pair, 0 : sz.fold, :].astype(F32)
            b = heads_in[2 * pair + 1, 0 : sz.fold, :].astype(F32)
            low = jnp.where(left, a, swap_halves(b))
            high = jnp.where(left, swap_halves(a), b)[: sz.rest]
            both = jnp.concatenate([low, high], axis=0)
            attended[:, pair * LANES : (pair + 1) * LANES] = both.astype(BF16)
        rows = tok[...].astype(F32) + (dot(attended[...], wo[...]) + bo[...])
        hidden[...] = rows
        unit, _ = norm_parts(rows)
        normed[...] = (unit * gain[...] + offset[...]).astype(BF16)
        reduced[...] = jnp.zeros_like(reduced)
        grad_normed[...] = jnp.zeros_like(grad_normed)

    expanded = dot(normed[...], we[...]) + be[...]
    below = 0.5 * (1.0 + lax.erf(expanded * 0.7071067811865476))
    bell = jnp.exp(expanded * expanded * -0.5) * 0.3989422804014327
    activated = expanded * below
    slope = below + expanded * bell
    act_low = activated.astype(BF16)
    reduced[...] += dot(act_low, wr[...])
    grad_expanded = (dot_cols(cot[...], wr[...]) * slope).astype(BF16)
    grad_be[...] = jnp.sum(grad_expanded.astype(F32), axis=0, keepdims=True)
    grad_normed[...] += dot_cols(grad_expanded, we[...])
    span = act_low.shape[1]
    act_own[...] = core_cols(activated, sz.ff // sz.n, core).astype(BF16)
    sent_at = sz.ff + 3 * sz.width
    shared[:, pl.ds(pl.multiple_of(sent_at + step * (span // 2), LANES), span // 2)] = core_cols(
        activated, sz.ff // sz.n, 1 - core
    ).astype(BF16)
    shared[:, pl.ds(pl.multiple_of(step * span, LANES), span)] = grad_expanded

    @pl.when(step == pl.num_programs(0) - 1)
    def _():
        rows = hidden[...]
        out_grad = cot[...].astype(F32)
        result[...] = (rows + (reduced[...] + br[...])).astype(BF16)
        part, gain_part, offset_part = norm_back(grad_normed[...], rows, gain[...])
        total = out_grad + part
        grad_hidden[...] = total
        grad_gain[...] = gain_part
        grad_offset[...] = offset_part
        grad_br[...] = jnp.sum(out_grad, axis=0, keepdims=True)
        low = total.astype(BF16)
        shared[:, sz.ff + 2 * sz.width : sz.ff + 3 * sz.width] = low
        grad_bo[...] = jnp.sum(low.astype(F32), axis=0, keepdims=True)
        for quarter in range(4):
            wide = sz.width // 4
            grad_attended = dot_cols(low, wo[quarter * wide : (quarter + 1) * wide, :])
            for pair in range(wide // LANES):
                both = grad_attended[:, pair * LANES : (pair + 1) * LANES]
                head = 2 * (quarter * (wide // LANES) + pair)
                msg[head] = fold_head(both, sz, False).astype(BF16)
                msg[head + 1] = fold_head(both, sz, True).astype(BF16)


def feed(sz, place, tokens, heads_in, wo, bo, gain, offset, we, be, wr, br, cot):
    span = 512
    steps = sz.ff // span
    whole = lambda *shape: pl.BlockSpec(shape, lambda j: (0,) * len(shape))
    shape = jax.ShapeDtypeStruct
    vector = whole(1, sz.width)
    vector_out = shape((1, sz.width), F32)
    shared = sz.ff + 3 * sz.width + sz.ff // 2
    return pl.pallas_call(
        lambda *refs: feed_kernel(sz, *refs),
        grid=(steps,),
        in_specs=[
            pl.BlockSpec(memory_space=pltpu.SMEM),
            whole(sz.rows, sz.width),
            whole(sz.heads, sz.fold, LANES),
            whole(sz.width, sz.width),
            vector,
            vector,
            vector,
            pl.BlockSpec((sz.width, span), lambda j: (0, j)),
            pl.BlockSpec((1, span), lambda j: (0, j)),
            pl.BlockSpec((span, sz.width), lambda j: (j, 0)),
            vector,
            whole(sz.rows, sz.width),
        ],
        out_specs=[
            whole(sz.rows, sz.width),
            whole(sz.rows, sz.width),
            whole(sz.heads, sz.fold, LANES),
            whole(sz.rows, shared),
            pl.BlockSpec((sz.rows, span // 2), lambda j: (0, j)),
            pl.BlockSpec((1, span), lambda j: (0, j)),
            vector,
            vector,
            vector,
            vector,
        ],
        out_shape=[
            shape((sz.rows, sz.width), BF16),
            shape((sz.rows, sz.width), F32),
            shape((sz.heads, sz.fold, LANES), BF16),
            shape((sz.rows, shared), BF16),
            shape((sz.rows, sz.ff // 2), BF16),
            shape((1, sz.ff), F32),
            vector_out,
            vector_out,
            vector_out,
            vector_out,
        ],
        scratch_shapes=[pltpu.VMEM((sz.rows, sz.width), F32)] * 3,
        compiler_params=params(),
        cost_estimate=cost(28),
        name="feed",
    )(place, tokens, heads_in, wo, bo, gain, offset, we, be, wr, br, cot)


def weights_kernel(sz, place, act, act_got, cot, cot_got, back, back_got, norm, norm_got, *refs):
    att, att_got, low, low_got = refs[:4]
    wr_own, wr_sent, wo_own, wo_sent = refs[4:8]
    we_out = refs[8 : 8 + sz.m]
    norm_t, norm_t_got = refs[8 + sz.m :]
    step = pl.program_id(0)
    core, low_bit, next_bit, mine_dp = place[0], place[1], place[2], place[3]
    per = sz.width // sz.n

    def core_rows(block):
        turned = block[...].astype(F32).T.reshape(sz.n // 2, 2, per, sz.rows)
        return choose([turned[:, 0], turned[:, 1]], core).reshape(sz.width // 2, sz.rows).astype(BF16)

    @pl.when(step == 0)
    def _():
        norm_t[...] = core_rows(norm)
        norm_t_got[...] = core_rows(norm_got)
        grad_wo = dot(core_rows(att), low[...]) + dot(core_rows(att_got), low_got[...])
        grad_wo = grad_wo.reshape(sz.n // 8, 2, 2 * per, sz.width)
        sides = [grad_wo[:, 0], grad_wo[:, 1]]
        wo_own[...] = choose(sides, next_bit).astype(BF16)
        wo_sent[...] = choose(sides, 1 - next_bit).astype(BF16)

    groups = act.shape[1] // (sz.ff // sz.n)
    grad_wr = (dot_rows(act[...], cot[...]) + dot_rows(act_got[...], cot_got[...])).astype(BF16)
    grad_wr = grad_wr.reshape(groups, sz.ff // sz.n, sz.width)
    if groups == 1:

        @pl.when(step % 2 == low_bit)
        def _():
            wr_own[...] = grad_wr

        @pl.when(step % 2 != low_bit)
        def _():
            wr_sent[...] = grad_wr

    else:
        wr_own[...] = choose([grad_wr[0:1], grad_wr[1:2]], low_bit)
        wr_sent[...] = choose([grad_wr[0:1], grad_wr[1:2]], 1 - low_bit)
    grad_we = dot(norm_t[...], back[...]) + dot(norm_t_got[...], back_got[...])
    grad_we = grad_we.reshape(sz.n // 2, sz.m, per // sz.m, grad_we.shape[1])
    sides = [grad_we[:, q] for q in range(sz.m)]
    for by in range(sz.m):
        piece = choose(sides, lax.rem(mine_dp + by, sz.m))
        we_out[by][...] = piece.astype(BF16).reshape(we_out[by].shape)


def weights(sz, place, act, cot, cot_got, shared, shared_got):
    span = 512
    steps = sz.ff // span
    per = sz.width // span
    fan = sz.ff // sz.width
    half = sz.n // 2
    few = sz.width // sz.shards
    whole = lambda *shape: pl.BlockSpec(shape, lambda j: (0,) * len(shape))
    column = lambda k: pl.BlockSpec((sz.rows, sz.width), lambda j: (0, sz.ff // sz.width + k))
    block = pl.BlockSpec((sz.rows, span), lambda j: (0, j))
    act_block = pl.BlockSpec((sz.rows, span // 2), lambda j: (0, j))
    got_at = (sz.ff + 3 * sz.width) // (span // 2)
    got_block = pl.BlockSpec((sz.rows, span // 2), lambda j: (0, got_at + j))
    shape = jax.ShapeDtypeStruct
    groups = half // steps
    wr_block = pl.BlockSpec((1, sz.ff // sz.n, sz.width), lambda j: (j * groups // 2, 0, 0))
    wr_out = shape((half // 2, sz.ff // sz.n, sz.width), BF16)
    wo_dims = (sz.n // 8, 2 * sz.width // sz.n, sz.width)
    we_block = pl.BlockSpec((half, 1, few, span), lambda j: (0, j // per, 0, j % per))
    we_out = shape((half, fan, few, sz.width), BF16)
    return pl.pallas_call(
        lambda *refs: weights_kernel(sz, *refs),
        grid=(steps,),
        in_specs=[
            pl.BlockSpec(memory_space=pltpu.SMEM),
            act_block,
            got_block,
            whole(sz.rows, sz.width),
            whole(sz.rows, sz.width),
            block,
            block,
        ]
        + [column(k // 2) for k in range(6)],
        out_specs=[wr_block, wr_block, whole(*wo_dims), whole(*wo_dims)] + [we_block] * sz.m,
        out_shape=[wr_out, wr_out, shape(wo_dims, BF16), shape(wo_dims, BF16)] + [we_out] * sz.m,
        scratch_shapes=[pltpu.VMEM((sz.width // 2, sz.rows), BF16)] * 2,
        compiler_params=params(),
        cost_estimate=cost(10),
        name="weights",
    )(place, act, shared_got, cot, cot_got, shared, shared_got, *([shared, shared_got] * 3))


def finish_kernel(sz, back, wq, wk, wv, tok, gain, grad_hidden, input_grad, grad_normed):
    step = pl.program_id(0)
    left = lane_index((sz.rows, LANES)) < HEAD_DIM
    left_fold = lane_index((sz.fold, LANES)) < HEAD_DIM
    queries, keys, values = [], [], []
    for pair in range(wq.shape[1] // LANES):
        kv_a = back[2 * pair, 0 : sz.rows, :].astype(F32)
        kv_b = back[2 * pair + 1, 0 : sz.rows, :].astype(F32)
        q_a = back[2 * pair, sz.slot : sz.slot + sz.fold, :].astype(F32)
        q_b = back[2 * pair + 1, sz.slot : sz.slot + sz.fold, :].astype(F32)
        low = jnp.where(left_fold, q_a, swap_halves(q_b))
        high = jnp.where(left_fold, swap_halves(q_a), q_b)[: sz.rest]
        queries.append(jnp.concatenate([low, high], axis=0).astype(BF16))
        keys.append(jnp.where(left, kv_a, swap_halves(kv_b)).astype(BF16))
        values.append(jnp.where(left, swap_halves(kv_a), kv_b).astype(BF16))
    total = jnp.zeros((sz.rows, sz.width), F32)
    for parts, weight in ((queries, wq), (keys, wk), (values, wv)):
        total = total + dot_cols(jnp.concatenate(parts, axis=1), weight[...])

    @pl.when(step == 0)
    def _():
        grad_normed[...] = total

    @pl.when(step > 0)
    def _():
        grad_normed[...] += total

    @pl.when(step == pl.num_programs(0) - 1)
    def _():
        part, _, _ = norm_back(grad_normed[...], tok[...].astype(F32), gain[...])
        input_grad[...] = grad_hidden[...] + part


def finish(sz, back, weight, tokens, gain, grad_hidden):
    cols = 256
    steps = sz.width // cols
    whole = lambda *shape: pl.BlockSpec(shape, lambda j: (0,) * len(shape))
    part = lambda k: pl.BlockSpec((sz.width, cols), lambda j: (0, k * steps + j))
    return pl.pallas_call(
        lambda *refs: finish_kernel(sz, *refs),
        grid=(steps,),
        in_specs=[
            pl.BlockSpec((cols // HEAD_DIM, sz.msg, LANES), lambda j: (j, 0, 0)),
            part(0),
            part(1),
            part(2),
            whole(sz.rows, sz.width),
            whole(1, sz.width),
            whole(sz.rows, sz.width),
        ],
        out_specs=whole(sz.rows, sz.width),
        out_shape=jax.ShapeDtypeStruct((sz.rows, sz.width), F32),
        scratch_shapes=[pltpu.VMEM((sz.rows, sz.width), F32)],
        compiler_params=params(),
        cost_estimate=cost(10),
        name="finish",
    )(back, weight, weight, weight, tokens, gain, grad_hidden)


def pick(array, axis, index):
    return lax.dynamic_index_in_dim(array, index, axis, keepdims=False)


def after(value, *others):
    return lax.optimization_barrier((value,) + others)[0]


class Halving:
    def __init__(self, sz, value, labels):
        self.sz = sz
        self.labels = list(labels)
        self.parts = [value]

    def picked(self, axis, index):
        return sum(pick(part, axis, index).astype(F32) for part in self.parts)

    def send(self, label):
        sz = self.sz
        axis = self.labels.index(label)
        self.labels.remove(label)
        if label == "dp":
            mine = lax.axis_index("dp")
            outs = [self.picked(axis, (mine + by) % sz.m).astype(BF16) for by in range(1, sz.m)]
        else:
            mine = (lax.axis_index("seq") // (2 << label)) % 2
            outs = [self.picked(axis, 1 - mine).astype(BF16)]
        self.parts = [self.picked(axis, mine)]
        return outs

    def move(self, label, outs):
        sz = self.sz
        if label == "dp":
            return [
                lax.ppermute(block, "dp", [(i, (i + by + 1) % sz.m) for i in range(sz.m)])
                for by, block in enumerate(outs)
            ]
        bit = 2 << label
        return [lax.ppermute(block, "seq", [(i, i ^ bit) for i in range(sz.n)]) for block in outs]

    def add(self, got):
        self.parts = self.parts + list(got)

    def value(self):
        return sum(part.astype(F32) for part in self.parts)

    def stage(self, label):
        self.add(self.move(label, self.send(label)))


def per_device(
    tokens,
    clip_start,
    frames,
    positions,
    first_gain,
    first_offset,
    triple_weight,
    triple_bias,
    output_weight,
    output_bias,
    second_gain,
    second_offset,
    expand_weight,
    expand_bias,
    reduce_weight,
    reduce_bias,
    cotangent,
):
    rows, width = tokens.shape[1:]
    ff = expand_weight.shape[1]
    n = lax.axis_size("seq")
    m = lax.axis_size("dp")
    slabs = clip_start.shape[1]
    sz = Sizes(rows, width, ff, n, m, slabs)
    shards = n * m
    group_slabs = n * slabs
    lower, upper = slab_bounds(clip_start[0], frames[0], lax.axis_index("seq") * slabs, group_slabs)
    first_unit = lower[0] // CLIP_MIN
    unit_count = (upper[0] - lower[0]) // CLIP_MIN
    meta_rows = jnp.arange(8)[:, None]
    meta = jnp.where(meta_rows == 0, first_unit, jnp.where(meta_rows == 1, unit_count, 0))
    meta = jnp.where(jnp.arange(LANES) < HEAD_DIM, 0, meta).astype(F32)
    cos, sin = lane_tables(positions[0])
    row = lambda vector: vector.reshape(1, -1)
    me, mine_dp = lax.axis_index("seq"), lax.axis_index("dp")
    place = jnp.stack([me % 2, me // 2 % 2, me // 4 % 2, mine_dp])
    swap_core = lambda block: lax.ppermute(block, "seq", [(i, i ^ 1) for i in range(n)])

    def exchange(message):
        if sz.rep > 1:
            message = jnp.repeat(message, sz.rep, axis=0)
        return lax.all_to_all(message, "seq", 0, 0, tiled=True)

    cot_got = swap_core(cotangent[0])
    message, normed = project(
        sz, tokens[0], row(first_gain), row(first_offset), triple_weight, row(triple_bias), cos, sin, meta
    )
    recv = exchange(message)
    places = jnp.pad(positions[0].astype(BF16), ((0, sz.slot - rows - 3), (0, width - rows)))
    normed_all = jnp.concatenate([normed, places], axis=0)
    chips = list(range(0, n // 2, 2)) + list(range(n // 2 - 1, 0, -2))
    ring = [2 * chip + core for chip in chips for core in range(2)]
    normed_all = lax.all_gather(after(normed_all, recv), "seq", axis=0, tiled=False, axis_index_groups=[ring])
    back_order = [ring.index(src) for src in range(n)]
    turns = all_turns(normed_all[:, rows : rows + 3, :rows][jnp.array(back_order)])
    facts = recv[:: sz.per_unit, sz.msg - 8 : sz.msg - 6, LANES - 1].astype(jnp.int32)
    unit_first, unit_span = facts[:, 0], facts[:, 1]
    out_message, kept, qs, kvs = attend(sz, unit_first, unit_span, recv)
    heads_in = lax.all_to_all(out_message, "seq", 0, 0, tiled=True)[:: sz.rep]
    (
        result,
        grad_hidden,
        grad_message,
        shared,
        act_own,
        grad_be,
        grad_second_gain,
        grad_second_offset,
        grad_bo,
        grad_br,
    ) = feed(
        sz,
        place,
        tokens[0],
        heads_in,
        output_weight,
        row(output_bias),
        row(second_gain),
        row(second_offset),
        expand_weight,
        row(expand_bias),
        reduce_weight,
        row(reduce_bias),
        cotangent[0],
    )
    recv_grad = exchange(grad_message)
    half = n // 2
    fan = ff // width
    few = width // shards
    many = ff // shards
    columns = [
        grad_bo.reshape(width, 1),
        grad_second_gain.reshape(width, 1),
        grad_second_offset.reshape(width, 1),
        grad_be.reshape(width, fan),
        grad_br.reshape(width, 1),
    ]
    small = jnp.concatenate(columns, axis=1)
    shared_got = swap_core(shared)
    wr_own, wr_sent, wo_own, wo_sent, *we_parts = weights(
        sz, place, act_own, cotangent[0], cot_got, shared, shared_got
    )
    bits = list(range(half.bit_length() - 2, -1, -1))
    twos = lambda count: (2,) * count
    wr_shape = twos(len(bits) - 1) + (m, many, width)
    we_shape = twos(len(bits)) + (many, width)
    wo_shape = twos(len(bits) - 1) + (m, few, width)
    side_r = Halving(sz, wr_own.reshape(wr_shape), bits[:-1] + ["dp"])
    side_e = Halving(sz, we_parts[0].reshape(we_shape), bits)
    side_o = Halving(sz, wo_own.reshape(wo_shape), bits[:-2] + [0, "dp"])
    small = small.reshape(twos(len(bits)) + (2, m, -1))
    small_got = swap_core(pick(small, len(bits), 1 - me % 2))
    side_s = Halving(sz, pick(small, len(bits), me % 2), bits + ["dp"])
    side_s.add([small_got])
    recv_grad = after(recv_grad, wr_sent, turns)
    got_r = side_r.move(0, [wr_sent.reshape(wr_shape)])
    got_e = side_e.move("dp", [part.reshape(we_shape) for part in we_parts[1:]])
    got_o = side_o.move(1, [wo_sent.reshape(wo_shape)])
    out_s = side_s.send(1)
    got_s = side_s.move(1, out_s)
    dos, grad_q, grad_kv = attend_back_first(sz, unit_first, unit_span, recv_grad, qs, kvs, kept)
    side_r.add(after(got_r, grad_kv))
    side_e.add(after(got_e, grad_kv))
    side_o.add(after(got_o, grad_kv))
    side_s.add(after(got_s, grad_kv))
    small_sum = side_s.value()
    small_sum = jnp.pad(
        small_sum[..., None, :], [(0, 0)] * small_sum.ndim + [(0, width - small_sum.shape[-1])]
    )
    small_sum = jnp.pad(small_sum, [(0, 0)] * (small_sum.ndim - 2) + [(0, 7), (0, 0)])
    side_o.parts = [jnp.concatenate([side_o.value(), small_sum], axis=-2)]
    out_r, out_e, out_o = side_r.send("dp"), side_e.send(0), side_o.send("dp")
    got_r, got_e, got_o = side_r.move("dp", out_r), side_e.move(0, out_e), side_o.move("dp", out_o)
    back_message = attend_back_last(
        sz, unit_first, unit_span, after(dos, out_r, out_e, out_o), qs, kvs, kept, grad_q, grad_kv, turns
    )
    got_r, got_e, got_o = after((got_r, got_e, got_o), back_message)
    side_r.add(got_r)
    side_e.add(got_e)
    side_o.add(got_o)
    out_r, out_e, out_o = side_r.send(1), side_e.send(1), side_o.send(0)
    got_r, got_e, got_o = side_r.move(1, out_r), side_e.move(1, out_e), side_o.move(0, out_o)
    back = lax.all_to_all(after(back_message, out_r, out_e, out_o), "seq", 0, 0, tiled=True)[:: sz.rep]
    head_grad = triple_grad(sz, after(back_message, out_r, out_e, out_o), normed_all)
    side_r.add(after(got_r, head_grad))
    side_e.add(after(got_e, head_grad))
    side_o.add(after(got_o, head_grad))
    out_r, out_e, out_o = side_r.send(2), side_e.send(2), side_o.send(2)
    got_r, got_e, got_o = side_r.move(2, out_r), side_e.move(2, out_e), side_o.move(2, out_o)
    input_grad = finish(sz, back, triple_weight, tokens[0], row(first_gain), grad_hidden)
    side_r.add(after(got_r, input_grad))
    side_e.add(after(got_e, input_grad))
    side_o.add(after(got_o, input_grad))
    for bit in range(3, len(bits)):
        side_r.stage(bit)
        side_e.stage(bit)
        side_o.stage(bit)
    head_parts = head_grad.reshape(n, m, few, 2 * LANES)
    head_sum = pick(head_parts, 1, mine_dp)
    for by in range(1, m):
        block = pick(head_parts, 1, (mine_dp + by) % m)
        head_sum = head_sum + lax.ppermute(block, "dp", [(i, (i + by) % m) for i in range(m)])
    head_rows = lax.all_to_all(after(head_sum, back), "seq", 0, 0, tiled=True)[:: sz.rep]
    parts = [head_rows[:, :, k * HEAD_DIM : (k + 1) * HEAD_DIM] for k in (2, 0, 1)]
    out_wt = jnp.concatenate([part.transpose(1, 0, 2).reshape(few, width) for part in parts], axis=1)
    bias_all = jnp.concatenate([head_rows[:, k, 3 * HEAD_DIM :].reshape(width) for k in (2, 0, 1)])
    shard = lax.axis_index("seq") * m + mine_dp
    bias_qk = lax.dynamic_slice(bias_all, (shard * 2 * few,), (2 * few,))
    bias_v = lax.dynamic_slice(bias_all, (2 * width + shard * few,), (few,))
    weight_rows = lax.dynamic_slice(triple_weight, (shard * few, 0), (few, 3 * width)).astype(F32)
    gain_rows = lax.dynamic_slice(first_gain, (shard * few,), (few,))
    offset_rows = lax.dynamic_slice(first_offset, (shard * few,), (few,))
    offset_one = jnp.sum(weight_rows * bias_all, axis=1)
    gain_one = (jnp.sum(weight_rows * out_wt, axis=1) - offset_rows * offset_one) / gain_rows
    out_wr = side_r.value()
    out_we = side_e.value().reshape(fan, few, width).transpose(1, 0, 2).reshape(few, ff)
    last_o = side_o.value()
    out_wo = last_o[:few]
    vectors = last_o[few, : small.shape[-1]].reshape(few, -1)
    begin = 0
    outs = []
    for column in columns:
        wide = column.shape[1]
        outs.append(vectors[:, begin : begin + wide].reshape(-1))
        begin += wide
    bias_o, gain_two, offset_two, bias_e, bias_r = outs
    return (
        result[None],
        input_grad[None],
        gain_one,
        offset_one,
        out_wt,
        bias_qk,
        bias_v,
        out_wo,
        bias_o,
        gain_two,
        offset_two,
        out_we,
        bias_e,
        out_wr,
        bias_r,
    )


def solution(mesh):
    sharded = P("dp", "seq", None)
    placed = (
        (sharded, P("dp", "seq"), P("dp", "seq"), P("dp", None, "seq"))
        + (P(),) * 12
        + (sharded,)
    )
    vector = P(("seq", "dp"))
    matrix = P(("seq", "dp"), None)
    return jax.shard_map(
        per_device,
        mesh=mesh,
        in_specs=placed,
        out_specs=(sharded, sharded, vector, vector, matrix, vector, vector, matrix, vector)
        + (vector, vector, matrix, vector, matrix, vector),
        check_vma=False,
    )
```

```python
import jax
import jax.numpy as jnp
from jax import lax
from jax.experimental import pallas as pl
from jax.experimental.pallas import tpu as pltpu
from jax.sharding import PartitionSpec as P

HEAD_DIM = 64
CLIP_MIN = 4
CLIP_MAX = 16
EPSILON = 1e-06
MASKED = 1e30
SECTIONS = ((0, 10), (20, 11), (42, 11))
LANES = 128
F32 = jnp.float32
BF16 = jnp.bfloat16
VMEM_LIMIT = 63 * 2**20
Q_TILE = 256
SAFE_ABOVE = 60.0
BACK_SHARE = (3, 4)


def dot(left, right):
    return jnp.dot(left, right, preferred_element_type=F32)


def dot_cols(left, right):
    return lax.dot_general(left, right, (((1,), (1,)), ((), ())), preferred_element_type=F32)


def dot_rows(left, right):
    return lax.dot_general(left, right, (((0,), (0,)), ((), ())), preferred_element_type=F32)


def cost(micros):
    return pl.CostEstimate(flops=int(micros * 1.15e9), bytes_accessed=2**20, transcendentals=0)


def params(sz=None, mib=0):
    if sz is not None and sz.n <= 16:
        return pltpu.CompilerParams(vmem_limit_bytes=mib * 2**20)
    return pltpu.CompilerParams(vmem_limit_bytes=VMEM_LIMIT)


def lane_index(shape):
    return lax.broadcasted_iota(jnp.int32, shape, len(shape) - 1)


def swap_halves(pair):
    return pltpu.roll(pair, HEAD_DIM, 1)


def rotate_pair(pair, cos_lanes, sin_lanes, inverse):
    lane = lane_index((1, LANES)) % HEAD_DIM
    sign = -1.0 if inverse else 1.0
    total = pair * cos_lanes
    for half in (10, 11):
        first = jnp.zeros(lane.shape, jnp.bool_)
        second = jnp.zeros(lane.shape, jnp.bool_)
        for begin_at, count in SECTIONS:
            if count == half:
                first = first | ((lane >= begin_at) & (lane < begin_at + half))
                second = second | ((lane >= begin_at + half) & (lane < begin_at + 2 * half))
        minus = jnp.where(first, -sign, 0.0)
        plus = jnp.where(second, sign, 0.0)
        total = total + pltpu.roll(pair, LANES - half, 1) * (sin_lanes * minus)
        total = total + pltpu.roll(pair, half, 1) * (sin_lanes * plus)
    return total


def lane_tables(positions):
    angles = jnp.zeros((positions.shape[1], LANES), F32)
    for section, (begin_at, count) in enumerate(SECTIONS):
        frequency = jnp.power(10000.0, -jnp.arange(count, dtype=F32) / count)
        in_head = jnp.zeros((HEAD_DIM,), F32)
        in_head = in_head.at[begin_at : begin_at + count].set(frequency)
        in_head = in_head.at[begin_at + count : begin_at + 2 * count].set(frequency)
        lanes = jnp.tile(in_head, LANES // HEAD_DIM)
        angles = angles + positions[section].astype(F32)[:, None] * lanes[None, :]
    return jnp.cos(angles), jnp.sin(angles)


def all_places(sz, corners):
    slabs = corners.shape[1] // 3
    per_slab = sz.rows // slabs
    side = int(round(per_slab**0.5))
    inside = jnp.arange(per_slab)
    steps = jnp.stack([jnp.zeros_like(inside), inside // side, inside % side])
    places = corners.reshape(sz.n, slabs, 3).transpose(0, 2, 1)[..., None] + steps[None, :, None, :]
    return places.reshape(sz.n, 3, sz.rows)


def all_turns(places):
    spots = jnp.arange(16)
    table = []
    for section in range(len(SECTIONS)):
        only = jnp.where(jnp.arange(len(SECTIONS))[:, None] == section, spots[None, :], 0)
        cos, sin = lane_tables(only)
        lane = jnp.arange(LANES)
        begin_at, count = SECTIONS[section]
        inside = (lane % HEAD_DIM >= begin_at) & (lane % HEAD_DIM < begin_at + 2 * count)
        table.append(jnp.where(inside, jnp.where(lane < HEAD_DIM, cos, sin), 0.0))
    table = jnp.concatenate(table, axis=0)
    hit = places.transpose(0, 2, 1)[..., None] == spots
    hit = hit.reshape(hit.shape[:2] + table.shape[:1]).astype(F32)
    hit = jnp.pad(hit, ((0, 0), (0, -hit.shape[1] % 16), (0, 0))).reshape(-1, table.shape[0])
    return jnp.dot(hit, table, precision=lax.Precision.HIGHEST)


def slab_bounds(clip_start, frames, first_slab, group_slabs):
    slab_index = first_slab + jnp.arange(clip_start.shape[-1], dtype=jnp.int32)
    unit_base = slab_index // CLIP_MIN * CLIP_MIN
    lower_slab = jnp.maximum(
        jnp.maximum(jnp.minimum(clip_start, slab_index), unit_base - (CLIP_MAX - CLIP_MIN)), 0
    )
    upper_slab = jnp.minimum(
        jnp.minimum(jnp.maximum(clip_start + frames // 2, slab_index + 1), unit_base + CLIP_MAX),
        group_slabs,
    )
    return lower_slab, upper_slab


def norm_parts(rows):
    centred = rows - jnp.mean(rows, axis=-1, keepdims=True)
    spread = jnp.mean(centred * centred, axis=-1, keepdims=True)
    scale = lax.rsqrt(spread + EPSILON)
    return centred * scale, scale


def norm_back(grad, rows, gain):
    unit, scale = norm_parts(rows)
    inner = grad * gain
    part = scale * (
        inner
        - jnp.mean(inner, axis=-1, keepdims=True)
        - unit * jnp.mean(inner * unit, axis=-1, keepdims=True)
    )
    return part, jnp.sum(grad * unit, axis=0, keepdims=True), jnp.sum(grad, axis=0, keepdims=True)


class Sizes:
    def __init__(self, rows, width, ff, n, m, slabs):
        self.rows = rows
        self.width = width
        self.ff = ff
        self.n = n
        self.m = m
        self.heads = width // HEAD_DIM
        self.rep = n // self.heads
        self.shards = n * m
        self.bits = (n // 2).bit_length() - 1
        self.per_unit = CLIP_MIN // slabs
        self.units = n // self.per_unit
        self.slot = (rows + 15) // 16 * 16
        self.unit_rows = self.slot * self.per_unit
        self.tokens = self.slot * n
        self.fold = (rows // 2 + 15) // 16 * 16
        self.rest = rows - self.fold
        self.msg = self.slot + self.fold


def pad_rows(block, count):
    if block.shape[0] == count:
        return block
    return jnp.concatenate([block, jnp.zeros((count - block.shape[0], block.shape[1]), F32)], axis=0)


def fold_head(block, sz, right):
    low = block[: sz.fold]
    high = pad_rows(block[sz.fold :], sz.fold)
    left = lane_index(low.shape) < HEAD_DIM
    if right:
        folded = jnp.where(left, swap_halves(low), high)
    else:
        folded = jnp.where(left, low, swap_halves(high))
    return folded


def project_kernel(sz, tok, gain, offset, wq, wk, wv, bq, bk, bv, cos, sin, meta, msg, normed_out):
    step = pl.program_id(0)

    @pl.when(step == 0)
    def _():
        unit, _ = norm_parts(tok[...].astype(F32))
        rows = (unit * gain[...] + offset[...]).astype(BF16)
        normed_out[0 : sz.rows, :] = rows
        normed_out[sz.rows :, :] = jnp.zeros((sz.slot - sz.rows, sz.width), BF16)

    normed = normed_out[0 : sz.rows, :]
    query = dot(normed, wq[...]) + bq[...]
    key = dot(normed, wk[...]) + bk[...]
    value = dot(normed, wv[...]) + bv[...]
    left = lane_index((sz.rows, LANES)) < HEAD_DIM
    spare = sz.slot - sz.rows
    facts = jnp.concatenate([jnp.zeros((sz.fold - 8, LANES), F32), meta[...]], axis=0)
    for pair in range(query.shape[1] // LANES):
        cols = slice(pair * LANES, (pair + 1) * LANES)
        q_pair = rotate_pair(query[:, cols], cos[...], sin[...], False) * 0.125
        k_pair = rotate_pair(key[:, cols], cos[...], sin[...], False)
        v_pair = value[:, cols]
        both = (jnp.where(left, k_pair, swap_halves(v_pair)), jnp.where(left, swap_halves(k_pair), v_pair))
        for head in range(2):
            tail = jnp.where(left[:spare], both[head][sz.rows - spare :], 0.0)
            folded = fold_head(q_pair, sz, head == 1) + facts
            rows = jnp.concatenate([both[head], tail, folded], axis=0)
            msg[2 * pair + head] = rows.astype(BF16)


def project(sz, tokens, gain, offset, weight, bias, cos, sin, meta):
    cols = 256
    steps = sz.width // cols
    whole = lambda shape: pl.BlockSpec(shape, lambda j: (0,) * len(shape))
    part = lambda k: pl.BlockSpec((sz.width, cols), lambda j: (0, k * steps + j))
    part_bias = lambda k: pl.BlockSpec((1, cols), lambda j: (0, k * steps + j))
    heads = cols // HEAD_DIM
    return pl.pallas_call(
        lambda *refs: project_kernel(sz, *refs),
        grid=(steps,),
        in_specs=[whole((sz.rows, sz.width)), whole((1, sz.width)), whole((1, sz.width))]
        + [part(0), part(1), part(2), part_bias(0), part_bias(1), part_bias(2)]
        + [whole((sz.rows, LANES)), whole((sz.rows, LANES)), whole((8, LANES))],
        out_specs=[
            pl.BlockSpec((heads, sz.msg, LANES), lambda j: (j, 0, 0)),
            whole((sz.slot, sz.width)),
        ],
        out_shape=[
            jax.ShapeDtypeStruct((sz.heads, sz.msg, LANES), BF16),
            jax.ShapeDtypeStruct((sz.slot, sz.width), BF16),
        ],
        compiler_params=params(),
        cost_estimate=cost(8),
        name="project",
    )(tokens, gain, offset, weight, weight, weight, bias, bias, bias, cos, sin, meta)


def unfold_slot(folded, sz, right):
    wide = folded.astype(F32)
    left = lane_index(wide.shape) < HEAD_DIM
    keep = ~left if right else left
    swapped = swap_halves(wide)
    low, high = (swapped, wide) if right else (wide, swapped)
    return (
        jnp.where(keep, low, 0.0).astype(BF16),
        jnp.where(keep, high, 0.0)[: sz.slot - sz.fold].astype(BF16),
    )


def unfold_into(target, at, folded, sz, right):
    low, high = unfold_slot(folded, sz, right)
    target[pl.ds(at, sz.fold), :] = low
    target[pl.ds(at + sz.fold, sz.slot - sz.fold), :] = high


def loop(count, body):
    def step(index, carry):
        body(index)
        return carry

    lax.fori_loop(0, count, step, 0)


def attend_kernel(sz, first, count, recv, out, kept, qs, kvs, ones_v):
    def unpack(src):
        at = pl.multiple_of(src * sz.slot, 16)
        unfold_into(qs, at, recv[src, sz.slot :, :], sz, False)
        kv = recv[src, 0 : sz.slot, :]
        kvs[pl.ds(at, sz.slot), :] = kv
        left = lane_index((1, LANES)) < HEAD_DIM
        real = lax.broadcasted_iota(jnp.int32, (sz.slot, 1), 0) < sz.rows
        one = jnp.where(real, 1.0, 0.0)
        ones_v[pl.ds(at, sz.slot), :] = jnp.where(left, one, kv.astype(F32)).astype(BF16)

    loop(sz.n, unpack)
    qs[sz.tokens :, :] = jnp.zeros((Q_TILE, LANES), BF16)
    kept[sz.tokens :, :] = jnp.zeros((Q_TILE, LANES), F32)

    def one(unit):
        rows = pl.ds(pl.multiple_of(unit * sz.unit_rows, 16), sz.unit_rows)
        begin = pl.multiple_of(first[unit] * sz.unit_rows, 16)

        def keep(shift, mixed):
            total = mixed[:, 0:1]
            left = lane_index((1, LANES)) < HEAD_DIM
            kept[rows, :] = jnp.where(left, shift + jnp.log(total), mixed * (1.0 / total))

        for span in (1, 2, 4):

            @pl.when(count[unit] == span)
            def _():
                clip = pl.ds(begin, span * sz.unit_rows)
                some = dot_cols(qs[rows, :], kvs[pl.ds(begin, 2 * LANES), :])
                shift = jnp.max(some, axis=1, keepdims=True)
                scores = dot_cols(qs[rows, :], kvs[clip, :])
                prob = jnp.exp(scores - shift).astype(BF16)
                keep(shift, dot(prob, ones_v[clip, :]))
                above = jnp.max(jnp.max(scores, axis=1, keepdims=True) - shift)

                @pl.when(above > SAFE_ABOVE)
                def _():
                    scores = dot_cols(qs[rows, :], kvs[clip, :])
                    peak = jnp.max(scores, axis=1, keepdims=True)
                    prob = jnp.exp(scores - peak).astype(BF16)
                    keep(peak, dot(prob, ones_v[clip, :]))

    loop(sz.units, one)

    def pack(src):
        at = pl.multiple_of(src * sz.slot, 16)
        out[src] = fold_head(kept[pl.ds(at, sz.slot), :][: sz.rows], sz, True).astype(BF16)
        left = lane_index((sz.slot - sz.rows, LANES)) < HEAD_DIM
        kept[pl.ds(at + sz.rows, sz.slot - sz.rows), :] = jnp.where(left, MASKED, 0.0)

    loop(sz.n, pack)


def attend(sz, first, count, recv):
    smem = pl.BlockSpec(memory_space=pltpu.SMEM)
    vmem = pl.BlockSpec(memory_space=pltpu.VMEM)
    shape = jax.ShapeDtypeStruct
    return pl.pallas_call(
        lambda *refs: attend_kernel(sz, *refs),
        in_specs=[smem, smem, vmem],
        out_specs=[vmem] * 4,
        out_shape=[
            shape((sz.n, sz.fold, LANES), BF16),
            shape((sz.tokens + Q_TILE, LANES), F32),
            shape((sz.tokens + Q_TILE, LANES), BF16),
            shape((sz.tokens, LANES), BF16),
        ],
        scratch_shapes=[pltpu.VMEM((sz.tokens, LANES), BF16)],
        compiler_params=params(),
        cost_estimate=cost(32),
        name="attend",
    )(first, count, recv)


def back_tiles(sz, part, first, count, qs, kvs, dos, kept, grad_q, grad_kv, key_t):
    def one(unit):
        begin = pl.multiple_of(unit * sz.unit_rows, 16)
        for span in (1, 2, 4):

            @pl.when((count[unit] == span) & (first[unit] == unit))
            def _():
                length = span * sz.unit_rows
                clip = pl.ds(begin, length)
                turned = kvs[clip, :].astype(F32).T[:HEAD_DIM]
                real = lax.rem(lane_index((1, length)), sz.slot) < sz.rows
                key_t[:, 0:length] = jnp.where(real, turned, 0.0).astype(BF16)

                def q_tile(t, carry):
                    rows = pl.ds(pl.multiple_of(begin + t * Q_TILE, 16), Q_TILE)
                    query = qs[rows, :]
                    grad = dos[rows, :]
                    kept_rows = kept[rows, :]
                    left = lane_index((Q_TILE, LANES)) < HEAD_DIM
                    turned = jnp.where(left, kept_rows, kept_rows * grad.astype(F32)).T
                    inside = lane_index((1, Q_TILE)) < length - t * Q_TILE
                    log_total = jnp.where(inside, turned[0:1, :], MASKED)
                    delta = jnp.sum(turned[HEAD_DIM:, :], axis=0, keepdims=True)
                    keys = kvs[clip, :]
                    prob = jnp.exp(dot_cols(keys, query) - log_total)
                    grad_prob = dot_cols(keys, grad)
                    grad_scores = (prob * (grad_prob - delta)).astype(BF16)
                    grad_kv[clip, :] += dot(grad_scores, query) + dot(prob.astype(BF16), grad)
                    grad_query = dot(key_t[:, 0:length], grad_scores) * 0.125
                    grad_query = jnp.concatenate([grad_query, jnp.zeros_like(grad_query)], axis=0).T
                    if part == 1:
                        own = lax.broadcasted_iota(jnp.int32, (Q_TILE, 1), 0) < length - t * Q_TILE
                        grad_query = jnp.where(own, grad_query, grad_q[rows, :])
                    grad_q[rows, :] = grad_query
                    return carry

                tiles = (length + Q_TILE - 1) // Q_TILE
                middle = (tiles * BACK_SHARE[0] + BACK_SHARE[1] - 1) // BACK_SHARE[1]
                lax.fori_loop(*((0, middle) if part == 0 else (middle, tiles)), q_tile, 0)

    loop(sz.units, one)


def back_first_kernel(sz, first, count, recv_grad, qs, kvs, kept, dos, grad_q, grad_kv, key_t):
    dos[sz.tokens :, :] = jnp.zeros((Q_TILE, LANES), BF16)

    def unpack(src):
        at = pl.multiple_of(src * sz.slot, 16)
        unfold_into(dos, at, recv_grad[src], sz, True)
        grad_kv[pl.ds(at, sz.slot), :] = jnp.zeros((sz.slot, LANES), F32)

    loop(sz.n, unpack)
    back_tiles(sz, 0, first, count, qs, kvs, dos, kept, grad_q, grad_kv, key_t)


def back_last_kernel(
    sz, first, count, dos, qs, kvs, kept, grad_q_in, grad_kv_in, turns, out, grad_q, grad_kv, key_t
):
    def copy(src):
        rows = pl.ds(pl.multiple_of(src * sz.slot, 16), sz.slot)
        grad_q[rows, :] = grad_q_in[rows, :]
        grad_kv[rows, :] = grad_kv_in[rows, :]

    loop(sz.n, copy)
    back_tiles(sz, 1, first, count, qs, kvs, dos, kept, grad_q, grad_kv, key_t)

    def pack(src):
        rows = pl.ds(pl.multiple_of(src * sz.slot, 16), sz.slot)
        kv = grad_kv[rows, :]
        left = lane_index((1, LANES)) < HEAD_DIM
        real = lax.broadcasted_iota(jnp.int32, (sz.slot, 1), 0) < sz.rows
        both = jnp.where(left, grad_q[rows, :], swap_halves(kv))
        table = turns[rows, :]
        other = swap_halves(table)
        both = rotate_pair(both, jnp.where(left, table, other), jnp.where(left, other, table), True)
        out[src, 0 : sz.slot, :] = jnp.where(real, jnp.where(left, swap_halves(both), kv), 0.0).astype(BF16)
        out[src, sz.slot :, :] = fold_head(both[: sz.rows], sz, False).astype(BF16)

    loop(sz.n, pack)


def attend_back_first(sz, first, count, recv_grad, qs, kvs, kept):
    smem = pl.BlockSpec(memory_space=pltpu.SMEM)
    vmem = pl.BlockSpec(memory_space=pltpu.VMEM)
    shape = jax.ShapeDtypeStruct
    return pl.pallas_call(
        lambda *refs: back_first_kernel(sz, *refs),
        in_specs=[smem, smem] + [vmem] * 4,
        out_specs=[vmem] * 3,
        out_shape=[
            shape((sz.tokens + Q_TILE, LANES), BF16),
            shape((sz.tokens + Q_TILE, LANES), F32),
            shape((sz.tokens, LANES), F32),
        ],
        scratch_shapes=[pltpu.VMEM((HEAD_DIM, CLIP_MAX // CLIP_MIN * sz.unit_rows), BF16)],
        compiler_params=params(sz, 18),
        cost_estimate=cost(40),
        name="attend_back_first",
    )(first, count, recv_grad, qs, kvs, kept)


def attend_back_last(sz, first, count, dos, qs, kvs, kept, grad_q, grad_kv, turns):
    smem = pl.BlockSpec(memory_space=pltpu.SMEM)
    vmem = pl.BlockSpec(memory_space=pltpu.VMEM)
    shape = jax.ShapeDtypeStruct
    return pl.pallas_call(
        lambda *refs: back_last_kernel(sz, *refs),
        in_specs=[smem, smem] + [vmem] * 7,
        out_specs=vmem,
        out_shape=shape((sz.n, sz.msg, LANES), BF16),
        scratch_shapes=[
            pltpu.VMEM((sz.tokens + Q_TILE, LANES), F32),
            pltpu.VMEM((sz.tokens, LANES), F32),
            pltpu.VMEM((HEAD_DIM, CLIP_MAX // CLIP_MIN * sz.unit_rows), BF16),
        ],
        compiler_params=params(sz, 18),
        cost_estimate=cost(20),
        name="attend_back_last",
    )(first, count, dos, qs, kvs, kept, grad_q, grad_kv, turns)


def triple_grad_kernel(sz, grads, normed, out, total):
    step = pl.program_id(0)
    high = sz.slot - sz.fold
    part_kv = jnp.zeros((LANES, sz.width), F32)
    part_q = jnp.zeros((HEAD_DIM, sz.width), F32)
    sums = jnp.zeros((1, 2 * LANES), F32)
    for src in range(grads.shape[0]):
        key_value = grads[src, 0 : sz.slot, :]
        query = grads[src, sz.slot :, :]
        part_kv = part_kv + dot_rows(key_value, normed[src])
        part_q = part_q + dot_rows(query, normed[src, 0 : sz.fold, :])[:HEAD_DIM]
        part_q = part_q + dot_rows(query[:high], normed[src, sz.fold :, :])[HEAD_DIM:]
        sum_kv = jnp.sum(key_value.astype(F32), axis=0, keepdims=True)
        sum_q = jnp.sum(query.astype(F32), axis=0, keepdims=True)
        sums = sums + jnp.concatenate([sum_kv, sum_q + swap_halves(sum_q)], axis=1)

    @pl.when(step == 0)
    def _():
        total[...] = jnp.zeros_like(total)

    total[0:LANES, :] += part_kv
    total[LANES : LANES + HEAD_DIM, :] += part_q
    total[2 * LANES :, 0 : 2 * LANES] += jnp.broadcast_to(sums, (8, 2 * LANES))

    @pl.when(step == pl.num_programs(0) - 1)
    def _():
        few = sz.width // sz.shards
        bias = total[2 * LANES : 2 * LANES + 1, 0 : 2 * LANES]
        place = lax.broadcasted_iota(jnp.int32, (sz.width, 1), 0) % few
        left = lane_index((1, LANES)) < HEAD_DIM
        out[:, 0:LANES] = total[0:LANES, :].T
        queries = total[LANES : 2 * LANES, :].T
        kv_row, q_row = bias[:, 0:LANES], bias[:, LANES:]
        side = jnp.where(place == 0, swap_halves(kv_row), jnp.where(place == 1, kv_row, q_row))
        out[:, LANES:] = jnp.where(left, queries, side)


def triple_grad(sz, grads, normed_all):
    shape = jax.ShapeDtypeStruct
    last = sz.n // 2 - 1
    return pl.pallas_call(
        lambda *refs: triple_grad_kernel(sz, *refs),
        grid=(sz.n // 2,),
        in_specs=[
            pl.BlockSpec((2, sz.msg, LANES), lambda j: (j, 0, 0)),
            pl.BlockSpec((2, sz.slot, sz.width), lambda j: (jnp.where(j % 2 == 0, j // 2, last - j // 2), 0, 0)),
        ],
        out_specs=pl.BlockSpec((sz.width, 2 * LANES), lambda j: (0, 0)),
        out_shape=shape((sz.width, 2 * LANES), F32),
        scratch_shapes=[pltpu.VMEM((2 * LANES + 8, sz.width), F32)],
        compiler_params=params(),
        cost_estimate=cost(1),
        name="triple_grad",
    )(grads, normed_all)


def choose(pieces, index):
    picked = pieces[0]
    for at in range(1, len(pieces)):
        picked = jnp.where(index == at, pieces[at], picked)
    return picked


def core_cols(block, width, side):
    count = block.shape[1] // (2 * width)
    groups = [block[:, g * width : (g + 1) * width] for g in range(2 * count)]
    return jnp.concatenate([choose(groups[2 * g : 2 * g + 2], side) for g in range(count)], axis=1)


def feed_kernel(sz, place, tok, heads_in, wo, bo, gain, offset, we, be, wr, br, cot, *refs):
    result, grad_hidden, msg, shared, act_own, grad_be, grad_gain, grad_offset, grad_bo, grad_br = refs[:10]
    hidden, reduced, grad_normed = refs[10:]
    step = pl.program_id(0)
    core = place[0]
    left = lane_index((sz.fold, LANES)) < HEAD_DIM
    normed = shared.at[:, sz.ff : sz.ff + sz.width]
    attended = shared.at[:, sz.ff + sz.width : sz.ff + 2 * sz.width]

    @pl.when(step == 0)
    def _():
        for pair in range(sz.heads // 2):
            a = heads_in[2 * pair, 0 : sz.fold, :].astype(F32)
            b = heads_in[2 * pair + 1, 0 : sz.fold, :].astype(F32)
            low = jnp.where(left, a, swap_halves(b))
            high = jnp.where(left, swap_halves(a), b)[: sz.rest]
            both = jnp.concatenate([low, high], axis=0)
            attended[:, pair * LANES : (pair + 1) * LANES] = both.astype(BF16)
        rows = tok[...].astype(F32) + (dot(attended[...], wo[...]) + bo[...])
        hidden[...] = rows
        unit, _ = norm_parts(rows)
        normed[...] = (unit * gain[...] + offset[...]).astype(BF16)
        reduced[...] = jnp.zeros_like(reduced)
        grad_normed[...] = jnp.zeros_like(grad_normed)

    expanded = dot(normed[...], we[...]) + be[...]
    below = 0.5 * (1.0 + lax.erf(expanded * 0.7071067811865476))
    bell = jnp.exp(expanded * expanded * -0.5) * 0.3989422804014327
    activated = expanded * below
    slope = below + expanded * bell
    act_low = activated.astype(BF16)
    reduced[...] += dot(act_low, wr[...])
    grad_expanded = (dot_cols(cot[...], wr[...]) * slope).astype(BF16)
    grad_be[...] = jnp.sum(grad_expanded.astype(F32), axis=0, keepdims=True)
    grad_normed[...] += dot_cols(grad_expanded, we[...])
    span = act_low.shape[1]
    act_own[...] = core_cols(activated, sz.ff // sz.n, core).astype(BF16)
    sent_at = sz.ff + 3 * sz.width
    shared[:, pl.ds(pl.multiple_of(sent_at + step * (span // 2), LANES), span // 2)] = core_cols(
        activated, sz.ff // sz.n, 1 - core
    ).astype(BF16)
    shared[:, pl.ds(pl.multiple_of(step * span, LANES), span)] = grad_expanded

    @pl.when(step == pl.num_programs(0) - 1)
    def _():
        rows = hidden[...]
        out_grad = cot[...].astype(F32)
        result[...] = (rows + (reduced[...] + br[...])).astype(BF16)
        part, gain_part, offset_part = norm_back(grad_normed[...], rows, gain[...])
        total = out_grad + part
        grad_hidden[...] = total
        grad_gain[...] = gain_part
        grad_offset[...] = offset_part
        grad_br[...] = jnp.sum(out_grad, axis=0, keepdims=True)
        low = total.astype(BF16)
        shared[:, sz.ff + 2 * sz.width : sz.ff + 3 * sz.width] = low
        grad_bo[...] = jnp.sum(low.astype(F32), axis=0, keepdims=True)
        for quarter in range(4):
            wide = sz.width // 4
            grad_attended = dot_cols(low, wo[quarter * wide : (quarter + 1) * wide, :])
            for pair in range(wide // LANES):
                both = grad_attended[:, pair * LANES : (pair + 1) * LANES]
                head = 2 * (quarter * (wide // LANES) + pair)
                msg[head] = fold_head(both, sz, False).astype(BF16)
                msg[head + 1] = fold_head(both, sz, True).astype(BF16)


def feed(sz, place, tokens, heads_in, wo, bo, gain, offset, we, be, wr, br, cot):
    span = 512
    steps = sz.ff // span
    whole = lambda *shape: pl.BlockSpec(shape, lambda j: (0,) * len(shape))
    shape = jax.ShapeDtypeStruct
    vector = whole(1, sz.width)
    vector_out = shape((1, sz.width), F32)
    shared = sz.ff + 3 * sz.width + sz.ff // 2
    return pl.pallas_call(
        lambda *refs: feed_kernel(sz, *refs),
        grid=(steps,),
        in_specs=[
            pl.BlockSpec(memory_space=pltpu.SMEM),
            whole(sz.rows, sz.width),
            whole(sz.heads, sz.fold, LANES),
            whole(sz.width, sz.width),
            vector,
            vector,
            vector,
            pl.BlockSpec((sz.width, span), lambda j: (0, j)),
            pl.BlockSpec((1, span), lambda j: (0, j)),
            pl.BlockSpec((span, sz.width), lambda j: (j, 0)),
            vector,
            whole(sz.rows, sz.width),
        ],
        out_specs=[
            whole(sz.rows, sz.width),
            whole(sz.rows, sz.width),
            whole(sz.heads, sz.fold, LANES),
            whole(sz.rows, shared),
            pl.BlockSpec((sz.rows, span // 2), lambda j: (0, j)),
            pl.BlockSpec((1, span), lambda j: (0, j)),
            vector,
            vector,
            vector,
            vector,
        ],
        out_shape=[
            shape((sz.rows, sz.width), BF16),
            shape((sz.rows, sz.width), F32),
            shape((sz.heads, sz.fold, LANES), BF16),
            shape((sz.rows, shared), BF16),
            shape((sz.rows, sz.ff // 2), BF16),
            shape((1, sz.ff), F32),
            vector_out,
            vector_out,
            vector_out,
            vector_out,
        ],
        scratch_shapes=[pltpu.VMEM((sz.rows, sz.width), F32)] * 3,
        compiler_params=params(),
        cost_estimate=cost(28),
        name="feed",
    )(place, tokens, heads_in, wo, bo, gain, offset, we, be, wr, br, cot)


def weights_kernel(sz, place, act, act_got, cot, cot_got, back, back_got, norm, norm_got, *refs):
    att, att_got, low, low_got = refs[:4]
    wr_own, wr_sent, we_own, we_sent = refs[4:8]
    wo_out = refs[8 : 8 + sz.m]
    norm_t, norm_t_got = refs[8 + sz.m :]
    step = pl.program_id(0)
    core, low_bit, next_bit, mine_dp = place[0], place[1], place[2], place[1 + sz.bits]
    per = sz.width // sz.n

    def core_rows(block):
        turned = block[...].astype(F32).T.reshape(sz.n // 2, 2, per, sz.rows)
        return choose([turned[:, 0], turned[:, 1]], core).reshape(sz.width // 2, sz.rows).astype(BF16)

    @pl.when(step == 0)
    def _():
        norm_t[...] = core_rows(norm)
        norm_t_got[...] = core_rows(norm_got)
        grad_wo = dot(core_rows(att), low[...]) + dot(core_rows(att_got), low_got[...])
        grad_wo = grad_wo.reshape(sz.n // 2, sz.m, per // sz.m, sz.width)
        sides = [grad_wo[:, q] for q in range(sz.m)]
        for by in range(sz.m):
            wo_out[by][...] = choose(sides, lax.rem(mine_dp + by, sz.m)).astype(BF16)

    groups = act.shape[1] // (sz.ff // sz.n)
    grad_wr = (dot_rows(act[...], cot[...]) + dot_rows(act_got[...], cot_got[...])).astype(BF16)
    grad_wr = grad_wr.reshape(groups, sz.ff // sz.n, sz.width)
    if groups == 1:

        @pl.when(step % 2 == low_bit)
        def _():
            wr_own[...] = grad_wr

        @pl.when(step % 2 != low_bit)
        def _():
            wr_sent[...] = grad_wr

    else:
        wr_own[...] = choose([grad_wr[0:1], grad_wr[1:2]], low_bit)
        wr_sent[...] = choose([grad_wr[0:1], grad_wr[1:2]], 1 - low_bit)
    grad_we = dot(norm_t[...], back[...]) + dot(norm_t_got[...], back_got[...])
    grad_we = grad_we.reshape(sz.n // 8, 2, 2 * sz.m, per // sz.m, grad_we.shape[1])
    sides = [grad_we[:, 0], grad_we[:, 1]]
    we_own[...] = choose(sides, next_bit).astype(BF16).reshape(we_own.shape)
    we_sent[...] = choose(sides, 1 - next_bit).astype(BF16).reshape(we_sent.shape)


def weights(sz, place, act, cot, cot_got, shared, shared_got):
    span = 512
    steps = sz.ff // span
    per = sz.width // span
    fan = sz.ff // sz.width
    half = sz.n // 2
    few = sz.width // sz.shards
    whole = lambda *shape: pl.BlockSpec(shape, lambda j: (0,) * len(shape))
    column = lambda k: pl.BlockSpec((sz.rows, sz.width), lambda j: (0, sz.ff // sz.width + k))
    block = pl.BlockSpec((sz.rows, span), lambda j: (0, j))
    act_block = pl.BlockSpec((sz.rows, span // 2), lambda j: (0, j))
    got_at = (sz.ff + 3 * sz.width) // (span // 2)
    got_block = pl.BlockSpec((sz.rows, span // 2), lambda j: (0, got_at + j))
    shape = jax.ShapeDtypeStruct
    groups = half // steps
    wr_block = pl.BlockSpec((1, sz.ff // sz.n, sz.width), lambda j: (j * groups // 2, 0, 0))
    wr_out = shape((half // 2, sz.ff // sz.n, sz.width), BF16)
    wo_dims = (half, few, sz.width)
    we_block = pl.BlockSpec((half // 2 * sz.m, 1, few, span), lambda j: (0, j // per, 0, j % per))
    we_out = shape((half // 2 * sz.m, fan, few, sz.width), BF16)
    return pl.pallas_call(
        lambda *refs: weights_kernel(sz, *refs),
        grid=(steps,),
        in_specs=[
            pl.BlockSpec(memory_space=pltpu.SMEM),
            act_block,
            got_block,
            whole(sz.rows, sz.width),
            whole(sz.rows, sz.width),
            block,
            block,
        ]
        + [column(k // 2) for k in range(6)],
        out_specs=[wr_block, wr_block, we_block, we_block] + [whole(*wo_dims)] * sz.m,
        out_shape=[wr_out, wr_out, we_out, we_out] + [shape(wo_dims, BF16)] * sz.m,
        scratch_shapes=[pltpu.VMEM((sz.width // 2, sz.rows), BF16)] * 2,
        compiler_params=params(),
        cost_estimate=cost(10),
        name="weights",
    )(place, act, shared_got, cot, cot_got, shared, shared_got, *([shared, shared_got] * 3))


def finish_kernel(sz, back, wq, wk, wv, tok, gain, grad_hidden, input_grad, grad_normed):
    step = pl.program_id(0)
    left = lane_index((sz.rows, LANES)) < HEAD_DIM
    left_fold = lane_index((sz.fold, LANES)) < HEAD_DIM
    queries, keys, values = [], [], []
    for pair in range(wq.shape[1] // LANES):
        kv_a = back[2 * pair, 0 : sz.rows, :].astype(F32)
        kv_b = back[2 * pair + 1, 0 : sz.rows, :].astype(F32)
        q_a = back[2 * pair, sz.slot : sz.slot + sz.fold, :].astype(F32)
        q_b = back[2 * pair + 1, sz.slot : sz.slot + sz.fold, :].astype(F32)
        low = jnp.where(left_fold, q_a, swap_halves(q_b))
        high = jnp.where(left_fold, swap_halves(q_a), q_b)[: sz.rest]
        queries.append(jnp.concatenate([low, high], axis=0).astype(BF16))
        keys.append(jnp.where(left, kv_a, swap_halves(kv_b)).astype(BF16))
        values.append(jnp.where(left, swap_halves(kv_a), kv_b).astype(BF16))
    total = jnp.zeros((sz.rows, sz.width), F32)
    for parts, weight in ((queries, wq), (keys, wk), (values, wv)):
        total = total + dot_cols(jnp.concatenate(parts, axis=1), weight[...])

    @pl.when(step == 0)
    def _():
        grad_normed[...] = total

    @pl.when(step > 0)
    def _():
        grad_normed[...] += total

    @pl.when(step == pl.num_programs(0) - 1)
    def _():
        part, _, _ = norm_back(grad_normed[...], tok[...].astype(F32), gain[...])
        input_grad[...] = grad_hidden[...] + part


def finish(sz, back, weight, tokens, gain, grad_hidden):
    cols = 256
    steps = sz.width // cols
    whole = lambda *shape: pl.BlockSpec(shape, lambda j: (0,) * len(shape))
    part = lambda k: pl.BlockSpec((sz.width, cols), lambda j: (0, k * steps + j))
    return pl.pallas_call(
        lambda *refs: finish_kernel(sz, *refs),
        grid=(steps,),
        in_specs=[
            pl.BlockSpec((cols // HEAD_DIM, sz.msg, LANES), lambda j: (j, 0, 0)),
            part(0),
            part(1),
            part(2),
            whole(sz.rows, sz.width),
            whole(1, sz.width),
            whole(sz.rows, sz.width),
        ],
        out_specs=whole(sz.rows, sz.width),
        out_shape=jax.ShapeDtypeStruct((sz.rows, sz.width), F32),
        scratch_shapes=[pltpu.VMEM((sz.rows, sz.width), F32)],
        compiler_params=params(),
        cost_estimate=cost(10),
        name="finish",
    )(back, weight, weight, weight, tokens, gain, grad_hidden)


def pick(array, axis, index):
    return lax.dynamic_index_in_dim(array, index, axis, keepdims=False)


def after(value, *others):
    return lax.optimization_barrier((value,) + others)[0]


class Side:
    def __init__(self, sz, labels, rows, arrays):
        self.dims = [(label, sz.m if label == "dp" else 2) for label in labels]
        self.rows = rows
        self.width = sz.width
        self.arrays = list(arrays)

    def split(self, label):
        at = [name for name, _ in self.dims].index(label)
        before, after_it = 1, self.rows
        for _, size in self.dims[:at]:
            before *= size
        for _, size in self.dims[at + 1 :]:
            after_it *= size
        count = self.dims[at][1]
        self.dims = self.dims[:at] + self.dims[at + 1 :]
        return before, count, after_it

    def total(self):
        return sum(array.astype(F32) for array in self.arrays).reshape(self.rows, self.width)


def halve_kernel(shapes, place, *refs):
    at = 0
    outs = sum(adds * count for adds, count in shapes)
    for adds, count in shapes:
        for _ in range(count):
            total = refs[at][:, 0].astype(F32)
            for more in range(1, adds):
                total = total + refs[at + more][:, 0].astype(F32)
            refs[outs][...] = total.astype(BF16)
            at += adds
            outs += 1


def halve(sz, place, sides, labels):
    parts = [side.split(label) for side, label in zip(sides, labels)]
    grid = 2 if all(before % 2 == 0 for before, _, _ in parts) else 1
    ins, in_specs, out_specs, out_shape = [], [], [], []
    for side, label, (before, count, rest) in zip(sides, labels, parts):
        which = 1 + sz.bits if label == "dp" else 1 + label
        for by in range(count):
            for array in side.arrays:
                ins.append(array.reshape(before, count, rest, sz.width))
                in_specs.append(
                    pl.BlockSpec(
                        (before // grid, 1, rest, sz.width),
                        lambda g, place, which=which, by=by, count=count: (g, lax.rem(place[which] + by, count), 0, 0),
                    )
                )
            out_specs.append(pl.BlockSpec((before // grid, rest, sz.width), lambda g, place: (g, 0, 0)))
            out_shape.append(jax.ShapeDtypeStruct((before, rest, sz.width), BF16))
    shapes = [(len(side.arrays), count) for side, (_, count, _) in zip(sides, parts)]
    outs = pl.pallas_call(
        lambda *refs: halve_kernel(shapes, *refs),
        grid_spec=pltpu.PrefetchScalarGridSpec(
            num_scalar_prefetch=1, grid=(grid,), in_specs=in_specs, out_specs=out_specs
        ),
        out_shape=out_shape,
        compiler_params=params(sz, 20),
        cost_estimate=cost(4),
        name="halve",
    )(place, *ins)
    sent = []
    for side, (_, count, _) in zip(sides, parts):
        side.arrays = [outs[0]]
        sent.append(list(outs[1:count]))
        outs = outs[count:]
    return sent


def send(sz, label, blocks):
    if label == "dp":
        return [
            lax.ppermute(block, "dp", [(i, (i + by + 1) % sz.m) for i in range(sz.m)])
            for by, block in enumerate(blocks)
        ]
    bit = 2 << label
    return [lax.ppermute(block, "seq", [(i, i ^ bit) for i in range(sz.n)]) for block in blocks]


def swap(sz, block, by):
    return block if by == 0 else lax.ppermute(block, "seq", [(i, i ^ by) for i in range(sz.n)])


def trade_near(sz, blocks):
    me = lax.axis_index("seq")
    blocks = blocks.reshape((sz.n // 4, 4) + blocks.shape[1:])
    return jnp.stack([swap(sz, pick(blocks, 1, me % 4 ^ by), by) for by in range(4)], axis=1)


def trade_far(sz, near):
    me = lax.axis_index("seq")
    return jnp.stack([swap(sz, pick(near, 0, me // 4 ^ by), 4 * by) for by in range(sz.n // 4)], axis=0)


def last_kernel(sz, adds, spans, place, far, gain, offset, weight, *refs):
    ins, outs = refs[: sum(adds)], refs[sum(adds) :]
    totals = []
    for count in adds:
        total = ins[0][...].astype(F32)
        for more in range(1, count):
            total = total + ins[more][...].astype(F32)
        totals.append(total)
        ins = ins[count:]
    wr, we, wo, wt, bias_all, gain_one, offset_one = outs[:7]
    few = sz.width // sz.shards
    wr[...] = totals[0]
    for part in range(sz.ff // sz.width):
        we[:, part * sz.width : (part + 1) * sz.width] = totals[1][part * few : (part + 1) * few]
    wo[...] = totals[2]
    low = place[0] + 2 * place[1]
    high = place[2]
    for bit in range(2, sz.bits):
        high = high + place[1 + bit] * 2 ** (bit - 1)

    def piece(src):
        return far[jnp.bitwise_xor(high, src // 4), jnp.bitwise_xor(low, src % 4)].astype(F32)

    left = lane_index((1, LANES)) < HEAD_DIM
    small = jnp.zeros((1, 2 * LANES), F32)
    along = jnp.zeros((1, 2 * LANES), F32)
    moved = jnp.zeros((few, 1), F32)
    for pair in range(sz.heads // 2):
        a = piece(2 * pair * sz.rep)
        b = piece((2 * pair + 1) * sz.rep)
        along = along + a[few + 1 : few + 2] + b[few + 1 : few + 2]
        kv_a, kv_b, q_a, q_b = a[:few, :LANES], b[:few, :LANES], a[:, LANES:], b[:, LANES:]
        blocks = (
            jnp.where(left, q_a[:few], swap_halves(q_b[:few])),
            jnp.where(left, kv_a, swap_halves(kv_b)),
            jnp.where(left, swap_halves(kv_a), kv_b),
        )
        side = jnp.where(left, swap_halves(q_a[:8]), q_b[:8])
        for part, row in ((0, 2), (1, 0), (2, 1)):
            cols = slice(part * sz.width + pair * LANES, part * sz.width + (pair + 1) * LANES)
            wt[:, cols] = blocks[part]
            bias_all[:, cols] = side[row : row + 1]
            rows = weight[:, cols].astype(F32) * side[row : row + 1]
            moved = moved + jnp.sum(rows, axis=1, keepdims=True)
    for src in range(sz.n):
        small = small + piece(src)[few : few + 1]
    moved = jnp.broadcast_to(moved, (few, LANES)).T[0:1]
    offset_one[...] = moved
    gain_one[...] = (along[:, :few] - offset[0] * moved) / gain[0]
    at = 0
    for out, span in zip(outs[7:], spans):
        out[...] = small[:, at : at + span]
        at += span


def last(sz, place, sides, far, gain, offset, weight, spans):
    few = sz.width // sz.shards
    shard = lambda g, place: (place[2 + sz.bits], 0, 0)
    whole = lambda *shape: pl.BlockSpec(shape, lambda g, place: (0,) * len(shape))
    ins, in_specs = [], []
    for side in sides:
        for array in side.arrays:
            ins.append(array.reshape(side.rows, sz.width))
            in_specs.append(whole(side.rows, sz.width))
    out_dims = [(sides[0].rows, sz.width), (few, sz.ff), (few, sz.width), (few, 3 * sz.width), (1, 3 * sz.width)]
    out_dims = out_dims + [(1, few), (1, few)] + [(1, span) for span in spans]
    return pl.pallas_call(
        lambda *refs: last_kernel(sz, [len(side.arrays) for side in sides], spans, *refs),
        grid_spec=pltpu.PrefetchScalarGridSpec(
            num_scalar_prefetch=1,
            grid=(1,),
            in_specs=[
                whole(*far.shape),
                pl.BlockSpec((1, 1, few), shard),
                pl.BlockSpec((1, 1, few), shard),
                pl.BlockSpec((few, 3 * sz.width), lambda g, place: (place[2 + sz.bits], 0)),
            ]
            + in_specs,
            out_specs=[whole(*dims) for dims in out_dims],
        ),
        out_shape=[jax.ShapeDtypeStruct(dims, F32) for dims in out_dims],
        compiler_params=params(),
        cost_estimate=cost(5),
        name="last",
    )(place, far, gain.reshape(sz.shards, 1, few), offset.reshape(sz.shards, 1, few), weight, *ins)


def per_device(
    tokens,
    clip_start,
    frames,
    positions,
    first_gain,
    first_offset,
    triple_weight,
    triple_bias,
    output_weight,
    output_bias,
    second_gain,
    second_offset,
    expand_weight,
    expand_bias,
    reduce_weight,
    reduce_bias,
    cotangent,
):
    rows, width = tokens.shape[1:]
    ff = expand_weight.shape[1]
    n = lax.axis_size("seq")
    m = lax.axis_size("dp")
    slabs = clip_start.shape[1]
    sz = Sizes(rows, width, ff, n, m, slabs)
    shards = n * m
    group_slabs = n * slabs
    lower, upper = slab_bounds(clip_start[0], frames[0], lax.axis_index("seq") * slabs, group_slabs)
    first_unit = lower[0] // CLIP_MIN
    unit_count = (upper[0] - lower[0]) // CLIP_MIN
    corners = positions[0].reshape(3, slabs, -1)[:, :, 0].T.reshape(-1)
    meta = jnp.concatenate([jnp.stack([first_unit, unit_count]), corners])[:8, None]
    meta = jnp.where(jnp.arange(LANES) < HEAD_DIM, 0, meta).astype(F32)
    cos, sin = lane_tables(positions[0])
    row = lambda vector: vector.reshape(1, -1)
    me, mine_dp = lax.axis_index("seq"), lax.axis_index("dp")
    place = jnp.stack([me % 2] + [me // (2 << bit) % 2 for bit in range(sz.bits)] + [mine_dp, me * m + mine_dp])
    swap_core = lambda block: lax.ppermute(block, "seq", [(i, i ^ 1) for i in range(n)])

    def exchange(message):
        if sz.rep > 1:
            message = jnp.repeat(message, sz.rep, axis=0)
        return lax.all_to_all(message, "seq", 0, 0, tiled=True)

    cot_got = swap_core(cotangent[0])
    head = me // sz.rep * HEAD_DIM
    head_weight = [
        lax.dynamic_slice(triple_weight, (0, k * width + head), (width, HEAD_DIM)) for k in (1, 2, 0)
    ]
    head_weight = jnp.concatenate(head_weight + [jnp.zeros((width, HEAD_DIM), BF16)], axis=1)
    message, normed = project(
        sz, tokens[0], row(first_gain), row(first_offset), triple_weight, row(triple_bias), cos, sin, meta
    )
    recv = exchange(message)
    chips = list(range(0, n // 2, 2)) + list(range(n // 2 - 1, 0, -2))
    ring = [2 * chip + core for chip in chips for core in range(2)]
    normed_all = lax.all_gather(after(normed, recv), "seq", axis=0, tiled=False, axis_index_groups=[ring])
    facts = recv[:, sz.msg - 8 :, LANES - 1].astype(jnp.int32)
    unit_first, unit_span = facts[:: sz.per_unit, 0], facts[:: sz.per_unit, 1]
    turns = all_turns(all_places(sz, facts[:, 2:]))
    out_message, kept, qs, kvs = attend(sz, unit_first, unit_span, recv)
    heads_in = lax.all_to_all(out_message, "seq", 0, 0, tiled=True)[:: sz.rep]
    (
        result,
        grad_hidden,
        grad_message,
        shared,
        act_own,
        grad_be,
        grad_second_gain,
        grad_second_offset,
        grad_bo,
        grad_br,
    ) = feed(
        sz,
        place,
        tokens[0],
        after(heads_in, turns),
        output_weight,
        row(output_bias),
        row(second_gain),
        row(second_offset),
        expand_weight,
        row(expand_bias),
        reduce_weight,
        row(reduce_bias),
        cotangent[0],
    )
    recv_grad = exchange(grad_message)
    half = n // 2
    fan = ff // width
    few = width // shards
    many = ff // shards
    shared_got = swap_core(shared)
    wr_own, wr_sent, we_own, we_sent, *wo_parts = weights(
        sz, place, act_own, cotangent[0], cot_got, shared, shared_got
    )
    bits = list(range(sz.bits - 1, -1, -1))
    side_r = Side(sz, bits[:-1] + ["dp"], many, [wr_own])
    side_e = Side(sz, bits[:-2] + [0, "dp"], many, [we_own])
    side_o = Side(sz, bits, few, [wo_parts[0]])
    sides = [side_r, side_e, side_o]
    sent = [[wr_sent], [we_sent], wo_parts[1:]]
    rounds = [(0, 1, "dp"), (1, 0, 1), ("dp", "dp", 0)] + [(bit,) * 3 for bit in range(2, sz.bits)]

    def move(labels):
        return [send(sz, label, blocks) for label, blocks in zip(labels, sent)]

    def add(got, marker):
        for side, blocks in zip(sides, got):
            side.arrays = side.arrays + list(after(blocks, marker))

    got = move(rounds[0])
    dos, grad_q, grad_kv = attend_back_first(
        sz, unit_first, unit_span, after(recv_grad, wo_parts[0]), qs, kvs, kept
    )
    add(got, grad_kv)
    sent = halve(sz, place, sides, rounds[1])
    got = move(rounds[1])
    back_message = attend_back_last(
        sz, unit_first, unit_span, after(dos, sent), qs, kvs, kept, grad_q, grad_kv, turns
    )
    add(got, back_message)
    sent = halve(sz, place, sides, rounds[2])
    got = move(rounds[2])
    back = lax.all_to_all(after(back_message, sent), "seq", 0, 0, tiled=True)[:: sz.rep]
    head_grad = triple_grad(sz, after(back_message, sent), normed_all)
    columns = [grad_bo, grad_second_gain, grad_second_offset, grad_be, grad_br]
    columns = [column.reshape(shards, -1) for column in after(columns, back_message)]
    spans = [column.shape[1] for column in columns]
    small = jnp.concatenate(columns, axis=1).reshape(n, m, 1, -1)
    small = jnp.pad(small, ((0, 0), (0, 0), (0, 0), (0, 2 * LANES - small.shape[3])))
    along = jnp.sum(head_grad * head_weight.astype(F32), axis=1).reshape(n, m, 1, few)
    along = jnp.pad(along, ((0, 0), (0, 0), (0, 6), (0, 2 * LANES - few)))
    head_parts = jnp.concatenate([head_grad.reshape(n, m, few, 2 * LANES), small, along], axis=2)
    head_sum = pick(head_parts, 1, mine_dp)
    for by in range(1, m):
        block = pick(head_parts, 1, (mine_dp + by) % m).astype(BF16)
        head_sum = head_sum + lax.ppermute(block, "dp", [(i, (i + by) % m) for i in range(m)]).astype(F32)
    near = trade_near(sz, head_sum.astype(BF16))
    back = after(back, near)
    add(got, back)
    for labels in rounds[3:]:
        sent = halve(sz, place, sides, labels)
        got = move(labels)
        if labels != rounds[-1]:
            add(got, back)
    input_grad = finish(
        sz, after(back, sent), triple_weight, tokens[0], row(first_gain), grad_hidden
    )
    add(got, input_grad)
    far = after(trade_far(sz, near), input_grad)
    (
        out_wr,
        out_we,
        out_wo,
        out_wt,
        bias_all,
        gain_one,
        offset_one,
        *vectors,
    ) = last(sz, place, sides, far, first_gain, first_offset, triple_weight, spans)
    shard = me * m + mine_dp
    bias_qk = lax.dynamic_slice(bias_all[0], (shard * 2 * few,), (2 * few,))
    bias_v = lax.dynamic_slice(bias_all[0], (2 * width + shard * few,), (few,))
    gain_one, offset_one = gain_one[0], offset_one[0]
    bias_o, gain_two, offset_two, bias_e, bias_r = [vector[0] for vector in vectors]
    return (
        result[None],
        input_grad[None],
        gain_one,
        offset_one,
        out_wt,
        bias_qk,
        bias_v,
        out_wo,
        bias_o,
        gain_two,
        offset_two,
        out_we,
        bias_e,
        out_wr,
        bias_r,
    )


def solution(mesh):
    sharded = P("dp", "seq", None)
    placed = (
        (sharded, P("dp", "seq"), P("dp", "seq"), P("dp", None, "seq"))
        + (P(),) * 12
        + (sharded,)
    )
    vector = P(("seq", "dp"))
    matrix = P(("seq", "dp"), None)
    return jax.shard_map(
        per_device,
        mesh=mesh,
        in_specs=placed,
        out_specs=(sharded, sharded, vector, vector, matrix, vector, vector, matrix, vector)
        + (vector, vector, matrix, vector, matrix, vector),
        check_vma=False,
    )
```

```python
import jax
import jax.numpy as jnp
from jax import lax
from jax.experimental import pallas as pl
from jax.experimental.pallas import tpu as pltpu
from jax.sharding import PartitionSpec as P

HEAD_DIM = 64
CLIP_MIN = 4
CLIP_MAX = 16
EPSILON = 1e-06
MASKED = 1e30
SECTIONS = ((0, 10), (20, 11), (42, 11))
LANES = 128
F32 = jnp.float32
BF16 = jnp.bfloat16
VMEM_LIMIT = 63 * 2**20
Q_TILE = 256
SAFE_ABOVE = 60.0
BACK_SHARE = (3, 4)


def dot(left, right):
    return jnp.dot(left, right, preferred_element_type=F32)


def dot_cols(left, right):
    return lax.dot_general(left, right, (((1,), (1,)), ((), ())), preferred_element_type=F32)


def dot_rows(left, right):
    return lax.dot_general(left, right, (((0,), (0,)), ((), ())), preferred_element_type=F32)


def cost(micros):
    return pl.CostEstimate(flops=int(micros * 1.15e9), bytes_accessed=2**20, transcendentals=0)


def params(sz=None, mib=0):
    if sz is not None and sz.n <= 16:
        return pltpu.CompilerParams(vmem_limit_bytes=mib * 2**20)
    return pltpu.CompilerParams(vmem_limit_bytes=VMEM_LIMIT)


def lane_index(shape):
    return lax.broadcasted_iota(jnp.int32, shape, len(shape) - 1)


def swap_halves(pair):
    return pltpu.roll(pair, HEAD_DIM, 1)


def rotate_pair(pair, cos_lanes, sin_lanes, inverse):
    lane = lane_index((1, LANES)) % HEAD_DIM
    sign = -1.0 if inverse else 1.0
    total = pair * cos_lanes
    for half in (10, 11):
        first = jnp.zeros(lane.shape, jnp.bool_)
        second = jnp.zeros(lane.shape, jnp.bool_)
        for begin_at, count in SECTIONS:
            if count == half:
                first = first | ((lane >= begin_at) & (lane < begin_at + half))
                second = second | ((lane >= begin_at + half) & (lane < begin_at + 2 * half))
        minus = jnp.where(first, -sign, 0.0)
        plus = jnp.where(second, sign, 0.0)
        total = total + pltpu.roll(pair, LANES - half, 1) * (sin_lanes * minus)
        total = total + pltpu.roll(pair, half, 1) * (sin_lanes * plus)
    return total


def lane_tables(positions):
    angles = jnp.zeros((positions.shape[1], LANES), F32)
    for section, (begin_at, count) in enumerate(SECTIONS):
        frequency = jnp.power(10000.0, -jnp.arange(count, dtype=F32) / count)
        in_head = jnp.zeros((HEAD_DIM,), F32)
        in_head = in_head.at[begin_at : begin_at + count].set(frequency)
        in_head = in_head.at[begin_at + count : begin_at + 2 * count].set(frequency)
        lanes = jnp.tile(in_head, LANES // HEAD_DIM)
        angles = angles + positions[section].astype(F32)[:, None] * lanes[None, :]
    return jnp.cos(angles), jnp.sin(angles)


def all_places(sz, corners):
    slabs = corners.shape[1] // 3
    per_slab = sz.rows // slabs
    side = int(round(per_slab**0.5))
    inside = jnp.arange(per_slab)
    steps = jnp.stack([jnp.zeros_like(inside), inside // side, inside % side])
    places = corners.reshape(sz.n, slabs, 3).transpose(0, 2, 1)[..., None] + steps[None, :, None, :]
    return places.reshape(sz.n, 3, sz.rows)


def all_turns(places):
    spots = jnp.arange(16)
    table = []
    for section in range(len(SECTIONS)):
        only = jnp.where(jnp.arange(len(SECTIONS))[:, None] == section, spots[None, :], 0)
        cos, sin = lane_tables(only)
        lane = jnp.arange(LANES)
        begin_at, count = SECTIONS[section]
        inside = (lane % HEAD_DIM >= begin_at) & (lane % HEAD_DIM < begin_at + 2 * count)
        table.append(jnp.where(inside, jnp.where(lane < HEAD_DIM, cos, sin), 0.0))
    table = jnp.concatenate(table, axis=0)
    hit = places.transpose(0, 2, 1)[..., None] == spots
    hit = hit.reshape(hit.shape[:2] + table.shape[:1]).astype(F32)
    hit = jnp.pad(hit, ((0, 0), (0, -hit.shape[1] % 16), (0, 0))).reshape(-1, table.shape[0])
    return jnp.dot(hit, table, precision=lax.Precision.HIGHEST)


def slab_bounds(clip_start, frames, first_slab, group_slabs):
    slab_index = first_slab + jnp.arange(clip_start.shape[-1], dtype=jnp.int32)
    unit_base = slab_index // CLIP_MIN * CLIP_MIN
    lower_slab = jnp.maximum(
        jnp.maximum(jnp.minimum(clip_start, slab_index), unit_base - (CLIP_MAX - CLIP_MIN)), 0
    )
    upper_slab = jnp.minimum(
        jnp.minimum(jnp.maximum(clip_start + frames // 2, slab_index + 1), unit_base + CLIP_MAX),
        group_slabs,
    )
    return lower_slab, upper_slab


def norm_parts(rows):
    centred = rows - jnp.mean(rows, axis=-1, keepdims=True)
    spread = jnp.mean(centred * centred, axis=-1, keepdims=True)
    scale = lax.rsqrt(spread + EPSILON)
    return centred * scale, scale


def norm_back(grad, rows, gain):
    unit, scale = norm_parts(rows)
    inner = grad * gain
    part = scale * (
        inner
        - jnp.mean(inner, axis=-1, keepdims=True)
        - unit * jnp.mean(inner * unit, axis=-1, keepdims=True)
    )
    return part, jnp.sum(grad * unit, axis=0, keepdims=True), jnp.sum(grad, axis=0, keepdims=True)


class Sizes:
    def __init__(self, rows, width, ff, n, m, slabs):
        self.rows = rows
        self.width = width
        self.ff = ff
        self.n = n
        self.m = m
        self.heads = width // HEAD_DIM
        self.rep = n // self.heads
        self.shards = n * m
        self.bits = (n // 2).bit_length() - 1
        self.per_unit = CLIP_MIN // slabs
        self.units = n // self.per_unit
        self.slot = (rows + 15) // 16 * 16
        self.unit_rows = self.slot * self.per_unit
        self.tokens = self.slot * n
        self.fold = (rows // 2 + 15) // 16 * 16
        self.rest = rows - self.fold
        self.msg = self.slot + self.fold


def pad_rows(block, count):
    if block.shape[0] == count:
        return block
    return jnp.concatenate([block, jnp.zeros((count - block.shape[0], block.shape[1]), F32)], axis=0)


def fold_head(block, sz, right):
    low = block[: sz.fold]
    high = pad_rows(block[sz.fold :], sz.fold)
    left = lane_index(low.shape) < HEAD_DIM
    if right:
        folded = jnp.where(left, swap_halves(low), high)
    else:
        folded = jnp.where(left, low, swap_halves(high))
    return folded


def project_kernel(sz, tok, gain, offset, wq, wk, wv, bq, bk, bv, cos, sin, meta, msg, normed_out):
    step = pl.program_id(0)

    @pl.when(step == 0)
    def _():
        unit, _ = norm_parts(tok[...].astype(F32))
        rows = (unit * gain[...] + offset[...]).astype(BF16)
        normed_out[0 : sz.rows, :] = rows
        normed_out[sz.rows :, :] = jnp.zeros((sz.slot - sz.rows, sz.width), BF16)

    normed = normed_out[0 : sz.rows, :]
    query = dot(normed, wq[...]) + bq[...]
    key = dot(normed, wk[...]) + bk[...]
    value = dot(normed, wv[...]) + bv[...]
    left = lane_index((sz.rows, LANES)) < HEAD_DIM
    spare = sz.slot - sz.rows
    facts = jnp.concatenate([jnp.zeros((sz.fold - 8, LANES), F32), meta[...]], axis=0)
    for pair in range(query.shape[1] // LANES):
        cols = slice(pair * LANES, (pair + 1) * LANES)
        q_pair = rotate_pair(query[:, cols], cos[...], sin[...], False) * 0.125
        k_pair = rotate_pair(key[:, cols], cos[...], sin[...], False)
        v_pair = value[:, cols]
        both = (jnp.where(left, k_pair, swap_halves(v_pair)), jnp.where(left, swap_halves(k_pair), v_pair))
        for head in range(2):
            tail = jnp.where(left[:spare], both[head][sz.rows - spare :], 0.0)
            folded = fold_head(q_pair, sz, head == 1) + facts
            rows = jnp.concatenate([both[head], tail, folded], axis=0)
            msg[2 * pair + head] = rows.astype(BF16)


def project(sz, tokens, gain, offset, weight, bias, cos, sin, meta):
    cols = 256
    steps = sz.width // cols
    whole = lambda shape: pl.BlockSpec(shape, lambda j: (0,) * len(shape))
    part = lambda k: pl.BlockSpec((sz.width, cols), lambda j: (0, k * steps + j))
    part_bias = lambda k: pl.BlockSpec((1, cols), lambda j: (0, k * steps + j))
    heads = cols // HEAD_DIM
    return pl.pallas_call(
        lambda *refs: project_kernel(sz, *refs),
        grid=(steps,),
        in_specs=[whole((sz.rows, sz.width)), whole((1, sz.width)), whole((1, sz.width))]
        + [part(0), part(1), part(2), part_bias(0), part_bias(1), part_bias(2)]
        + [whole((sz.rows, LANES)), whole((sz.rows, LANES)), whole((8, LANES))],
        out_specs=[
            pl.BlockSpec((heads, sz.msg, LANES), lambda j: (j, 0, 0)),
            whole((sz.slot, sz.width)),
        ],
        out_shape=[
            jax.ShapeDtypeStruct((sz.heads, sz.msg, LANES), BF16),
            jax.ShapeDtypeStruct((sz.slot, sz.width), BF16),
        ],
        compiler_params=params(),
        cost_estimate=cost(8),
        name="project",
    )(tokens, gain, offset, weight, weight, weight, bias, bias, bias, cos, sin, meta)


def unfold_slot(folded, sz, right):
    wide = folded.astype(F32)
    left = lane_index(wide.shape) < HEAD_DIM
    keep = ~left if right else left
    swapped = swap_halves(wide)
    low, high = (swapped, wide) if right else (wide, swapped)
    return (
        jnp.where(keep, low, 0.0).astype(BF16),
        jnp.where(keep, high, 0.0)[: sz.slot - sz.fold].astype(BF16),
    )


def unfold_into(target, at, folded, sz, right):
    low, high = unfold_slot(folded, sz, right)
    target[pl.ds(at, sz.fold), :] = low
    target[pl.ds(at + sz.fold, sz.slot - sz.fold), :] = high


def loop(count, body):
    def step(index, carry):
        body(index)
        return carry

    lax.fori_loop(0, count, step, 0)


def attend_kernel(sz, first, count, recv, out, kept, qs, kvs, ones_v):
    def unpack(src):
        at = pl.multiple_of(src * sz.slot, 16)
        unfold_into(qs, at, recv[src, sz.slot :, :], sz, False)
        kv = recv[src, 0 : sz.slot, :]
        kvs[pl.ds(at, sz.slot), :] = kv
        left = lane_index((1, LANES)) < HEAD_DIM
        real = lax.broadcasted_iota(jnp.int32, (sz.slot, 1), 0) < sz.rows
        one = jnp.where(real, 1.0, 0.0)
        ones_v[pl.ds(at, sz.slot), :] = jnp.where(left, one, kv.astype(F32)).astype(BF16)

    loop(sz.n, unpack)
    qs[sz.tokens :, :] = jnp.zeros((Q_TILE, LANES), BF16)
    kept[sz.tokens :, :] = jnp.zeros((Q_TILE, LANES), F32)

    def one(unit):
        rows = pl.ds(pl.multiple_of(unit * sz.unit_rows, 16), sz.unit_rows)
        begin = pl.multiple_of(first[unit] * sz.unit_rows, 16)

        def keep(shift, mixed):
            total = mixed[:, 0:1]
            left = lane_index((1, LANES)) < HEAD_DIM
            kept[rows, :] = jnp.where(left, shift + jnp.log(total), mixed * (1.0 / total))

        for span in (1, 2, 4):

            @pl.when(count[unit] == span)
            def _():
                clip = pl.ds(begin, span * sz.unit_rows)
                some = dot_cols(qs[rows, :], kvs[pl.ds(begin, 2 * LANES), :])
                shift = jnp.max(some, axis=1, keepdims=True)
                scores = dot_cols(qs[rows, :], kvs[clip, :])
                prob = jnp.exp(scores - shift).astype(BF16)
                keep(shift, dot(prob, ones_v[clip, :]))
                above = jnp.max(jnp.max(scores, axis=1, keepdims=True) - shift)

                @pl.when(above > SAFE_ABOVE)
                def _():
                    scores = dot_cols(qs[rows, :], kvs[clip, :])
                    peak = jnp.max(scores, axis=1, keepdims=True)
                    prob = jnp.exp(scores - peak).astype(BF16)
                    keep(peak, dot(prob, ones_v[clip, :]))

    loop(sz.units, one)

    def pack(src):
        at = pl.multiple_of(src * sz.slot, 16)
        out[src] = fold_head(kept[pl.ds(at, sz.slot), :][: sz.rows], sz, True).astype(BF16)
        left = lane_index((sz.slot - sz.rows, LANES)) < HEAD_DIM
        kept[pl.ds(at + sz.rows, sz.slot - sz.rows), :] = jnp.where(left, MASKED, 0.0)

    loop(sz.n, pack)


def attend(sz, first, count, recv):
    smem = pl.BlockSpec(memory_space=pltpu.SMEM)
    vmem = pl.BlockSpec(memory_space=pltpu.VMEM)
    shape = jax.ShapeDtypeStruct
    return pl.pallas_call(
        lambda *refs: attend_kernel(sz, *refs),
        in_specs=[smem, smem, vmem],
        out_specs=[vmem] * 4,
        out_shape=[
            shape((sz.n, sz.fold, LANES), BF16),
            shape((sz.tokens + Q_TILE, LANES), F32),
            shape((sz.tokens + Q_TILE, LANES), BF16),
            shape((sz.tokens, LANES), BF16),
        ],
        scratch_shapes=[pltpu.VMEM((sz.tokens, LANES), BF16)],
        compiler_params=params(),
        cost_estimate=cost(32),
        name="attend",
    )(first, count, recv)


def back_tiles(sz, part, first, count, qs, kvs, dos, kept, grad_q, grad_kv, key_t):
    def one(unit):
        begin = pl.multiple_of(unit * sz.unit_rows, 16)
        for span in (1, 2, 4):

            @pl.when((count[unit] == span) & (first[unit] == unit))
            def _():
                length = span * sz.unit_rows
                clip = pl.ds(begin, length)
                turned = kvs[clip, :].astype(F32).T[:HEAD_DIM]
                real = lax.rem(lane_index((1, length)), sz.slot) < sz.rows
                key_t[:, 0:length] = jnp.where(real, turned, 0.0).astype(BF16)

                def q_tile(t, carry):
                    rows = pl.ds(pl.multiple_of(begin + t * Q_TILE, 16), Q_TILE)
                    query = qs[rows, :]
                    grad = dos[rows, :]
                    kept_rows = kept[rows, :]
                    left = lane_index((Q_TILE, LANES)) < HEAD_DIM
                    turned = jnp.where(left, kept_rows, kept_rows * grad.astype(F32)).T
                    inside = lane_index((1, Q_TILE)) < length - t * Q_TILE
                    log_total = jnp.where(inside, turned[0:1, :], MASKED)
                    delta = jnp.sum(turned[HEAD_DIM:, :], axis=0, keepdims=True)
                    keys = kvs[clip, :]
                    prob = jnp.exp(dot_cols(keys, query) - log_total)
                    grad_prob = dot_cols(keys, grad)
                    grad_scores = (prob * (grad_prob - delta)).astype(BF16)
                    grad_kv[clip, :] += dot(grad_scores, query) + dot(prob.astype(BF16), grad)
                    grad_query = dot(key_t[:, 0:length], grad_scores) * 0.125
                    grad_query = jnp.concatenate([grad_query, jnp.zeros_like(grad_query)], axis=0).T
                    if part == 1:
                        own = lax.broadcasted_iota(jnp.int32, (Q_TILE, 1), 0) < length - t * Q_TILE
                        grad_query = jnp.where(own, grad_query, grad_q[rows, :])
                    grad_q[rows, :] = grad_query
                    return carry

                tiles = (length + Q_TILE - 1) // Q_TILE
                middle = (tiles * BACK_SHARE[0] + BACK_SHARE[1] - 1) // BACK_SHARE[1]
                lax.fori_loop(*((0, middle) if part == 0 else (middle, tiles)), q_tile, 0)

    loop(sz.units, one)


def back_first_kernel(sz, first, count, recv_grad, qs, kvs, kept, dos, grad_q, grad_kv, key_t):
    dos[sz.tokens :, :] = jnp.zeros((Q_TILE, LANES), BF16)

    def unpack(src):
        at = pl.multiple_of(src * sz.slot, 16)
        unfold_into(dos, at, recv_grad[src], sz, True)
        grad_kv[pl.ds(at, sz.slot), :] = jnp.zeros((sz.slot, LANES), F32)

    loop(sz.n, unpack)
    back_tiles(sz, 0, first, count, qs, kvs, dos, kept, grad_q, grad_kv, key_t)


def back_last_kernel(
    sz, first, count, dos, qs, kvs, kept, grad_q_in, grad_kv_in, turns, out, grad_q, grad_kv, key_t
):
    def copy(src):
        rows = pl.ds(pl.multiple_of(src * sz.slot, 16), sz.slot)
        grad_q[rows, :] = grad_q_in[rows, :]
        grad_kv[rows, :] = grad_kv_in[rows, :]

    loop(sz.n, copy)
    back_tiles(sz, 1, first, count, qs, kvs, dos, kept, grad_q, grad_kv, key_t)

    def pack(src):
        rows = pl.ds(pl.multiple_of(src * sz.slot, 16), sz.slot)
        kv = grad_kv[rows, :]
        left = lane_index((1, LANES)) < HEAD_DIM
        real = lax.broadcasted_iota(jnp.int32, (sz.slot, 1), 0) < sz.rows
        both = jnp.where(left, grad_q[rows, :], swap_halves(kv))
        table = turns[rows, :]
        other = swap_halves(table)
        both = rotate_pair(both, jnp.where(left, table, other), jnp.where(left, other, table), True)
        out[src, 0 : sz.slot, :] = jnp.where(real, jnp.where(left, swap_halves(both), kv), 0.0).astype(BF16)
        out[src, sz.slot :, :] = fold_head(both[: sz.rows], sz, False).astype(BF16)

    loop(sz.n, pack)


def attend_back_first(sz, first, count, recv_grad, qs, kvs, kept):
    smem = pl.BlockSpec(memory_space=pltpu.SMEM)
    vmem = pl.BlockSpec(memory_space=pltpu.VMEM)
    shape = jax.ShapeDtypeStruct
    return pl.pallas_call(
        lambda *refs: back_first_kernel(sz, *refs),
        in_specs=[smem, smem] + [vmem] * 4,
        out_specs=[vmem] * 3,
        out_shape=[
            shape((sz.tokens + Q_TILE, LANES), BF16),
            shape((sz.tokens + Q_TILE, LANES), F32),
            shape((sz.tokens, LANES), F32),
        ],
        scratch_shapes=[pltpu.VMEM((HEAD_DIM, CLIP_MAX // CLIP_MIN * sz.unit_rows), BF16)],
        compiler_params=params(sz, 18),
        cost_estimate=cost(40),
        name="attend_back_first",
    )(first, count, recv_grad, qs, kvs, kept)


def attend_back_last(sz, first, count, dos, qs, kvs, kept, grad_q, grad_kv, turns):
    smem = pl.BlockSpec(memory_space=pltpu.SMEM)
    vmem = pl.BlockSpec(memory_space=pltpu.VMEM)
    shape = jax.ShapeDtypeStruct
    return pl.pallas_call(
        lambda *refs: back_last_kernel(sz, *refs),
        in_specs=[smem, smem] + [vmem] * 7,
        out_specs=vmem,
        out_shape=shape((sz.n, sz.msg, LANES), BF16),
        scratch_shapes=[
            pltpu.VMEM((sz.tokens + Q_TILE, LANES), F32),
            pltpu.VMEM((sz.tokens, LANES), F32),
            pltpu.VMEM((HEAD_DIM, CLIP_MAX // CLIP_MIN * sz.unit_rows), BF16),
        ],
        compiler_params=params(sz, 18),
        cost_estimate=cost(20),
        name="attend_back_last",
    )(first, count, dos, qs, kvs, kept, grad_q, grad_kv, turns)


def triple_grad_kernel(sz, grads, normed, out, total):
    step = pl.program_id(0)
    high = sz.slot - sz.fold
    part_kv = jnp.zeros((LANES, sz.width), F32)
    part_q = jnp.zeros((HEAD_DIM, sz.width), F32)
    sums = jnp.zeros((1, 2 * LANES), F32)
    for src in range(grads.shape[0]):
        key_value = grads[src, 0 : sz.slot, :]
        query = grads[src, sz.slot :, :]
        part_kv = part_kv + dot_rows(key_value, normed[src])
        part_q = part_q + dot_rows(query, normed[src, 0 : sz.fold, :])[:HEAD_DIM]
        part_q = part_q + dot_rows(query[:high], normed[src, sz.fold :, :])[HEAD_DIM:]
        sum_kv = jnp.sum(key_value.astype(F32), axis=0, keepdims=True)
        sum_q = jnp.sum(query.astype(F32), axis=0, keepdims=True)
        sums = sums + jnp.concatenate([sum_kv, sum_q + swap_halves(sum_q)], axis=1)

    @pl.when(step == 0)
    def _():
        total[...] = jnp.zeros_like(total)

    total[0:LANES, :] += part_kv
    total[LANES : LANES + HEAD_DIM, :] += part_q
    total[2 * LANES :, 0 : 2 * LANES] += jnp.broadcast_to(sums, (8, 2 * LANES))

    @pl.when(step == pl.num_programs(0) - 1)
    def _():
        few = sz.width // sz.shards
        bias = total[2 * LANES : 2 * LANES + 1, 0 : 2 * LANES]
        place = lax.broadcasted_iota(jnp.int32, (sz.width, 1), 0) % few
        left = lane_index((1, LANES)) < HEAD_DIM
        out[:, 0:LANES] = total[0:LANES, :].T
        queries = total[LANES : 2 * LANES, :].T
        kv_row, q_row = bias[:, 0:LANES], bias[:, LANES:]
        side = jnp.where(place == 0, swap_halves(kv_row), jnp.where(place == 1, kv_row, 0.0))
        side = jnp.where(place == 2, q_row, side)
        out[:, LANES:] = jnp.where(left, queries, side)


def triple_grad(sz, grads, normed_all):
    shape = jax.ShapeDtypeStruct
    last = sz.n // 2 - 1
    return pl.pallas_call(
        lambda *refs: triple_grad_kernel(sz, *refs),
        grid=(sz.n // 2,),
        in_specs=[
            pl.BlockSpec((2, sz.msg, LANES), lambda j: (j, 0, 0)),
            pl.BlockSpec((2, sz.slot, sz.width), lambda j: (jnp.where(j % 2 == 0, j // 2, last - j // 2), 0, 0)),
        ],
        out_specs=pl.BlockSpec((sz.width, 2 * LANES), lambda j: (0, 0)),
        out_shape=shape((sz.width, 2 * LANES), F32),
        scratch_shapes=[pltpu.VMEM((2 * LANES + 8, sz.width), F32)],
        compiler_params=params(sz, 54),
        cost_estimate=cost(1),
        name="triple_grad",
    )(grads, normed_all)


def choose(pieces, index):
    picked = pieces[0]
    for at in range(1, len(pieces)):
        picked = jnp.where(index == at, pieces[at], picked)
    return picked


def core_cols(block, width, side):
    count = block.shape[1] // (2 * width)
    groups = [block[:, g * width : (g + 1) * width] for g in range(2 * count)]
    return jnp.concatenate([choose(groups[2 * g : 2 * g + 2], side) for g in range(count)], axis=1)


def feed_kernel(sz, place, tok, heads_in, wo, bo, gain, offset, we, be, wr, br, cot, *refs):
    result, grad_hidden, msg, shared, grad_exp, act_sent, act_own = refs[:7]
    grad_be, grad_gain, grad_offset, grad_bo, grad_br = refs[7:12]
    hidden, reduced, grad_normed = refs[12:]
    step = pl.program_id(0)
    core = place[0]
    left = lane_index((sz.fold, LANES)) < HEAD_DIM
    normed = shared.at[:, 0 : sz.width]
    attended = shared.at[:, sz.width : 2 * sz.width]

    @pl.when(step == 0)
    def _():
        for pair in range(sz.heads // 2):
            a = heads_in[2 * pair, 0 : sz.fold, :].astype(F32)
            b = heads_in[2 * pair + 1, 0 : sz.fold, :].astype(F32)
            low = jnp.where(left, a, swap_halves(b))
            high = jnp.where(left, swap_halves(a), b)[: sz.rest]
            both = jnp.concatenate([low, high], axis=0)
            attended[:, pair * LANES : (pair + 1) * LANES] = both.astype(BF16)
        rows = tok[...].astype(F32) + (dot(attended[...], wo[...]) + bo[...])
        hidden[...] = rows
        unit, _ = norm_parts(rows)
        normed[...] = (unit * gain[...] + offset[...]).astype(BF16)
        reduced[...] = jnp.zeros_like(reduced)
        grad_normed[...] = jnp.zeros_like(grad_normed)

    expanded = dot(normed[...], we[...]) + be[...]
    below = 0.5 * (1.0 + lax.erf(expanded * 0.7071067811865476))
    bell = jnp.exp(expanded * expanded * -0.5) * 0.3989422804014327
    activated = expanded * below
    slope = below + expanded * bell
    act_low = activated.astype(BF16)
    reduced[...] += dot(act_low, wr[...])
    grad_expanded = (dot_cols(cot[...], wr[...]) * slope).astype(BF16)
    grad_be[...] = jnp.sum(grad_expanded.astype(F32), axis=0, keepdims=True)
    grad_normed[...] += dot_cols(grad_expanded, we[...])
    act_own[...] = core_cols(activated, sz.ff // sz.n, core).astype(BF16)
    act_sent[...] = core_cols(activated, sz.ff // sz.n, 1 - core).astype(BF16)
    grad_exp[...] = grad_expanded

    @pl.when(step == pl.num_programs(0) - 1)
    def _():
        rows = hidden[...]
        out_grad = cot[...].astype(F32)
        result[...] = (rows + (reduced[...] + br[...])).astype(BF16)
        part, gain_part, offset_part = norm_back(grad_normed[...], rows, gain[...])
        total = out_grad + part
        grad_hidden[...] = total
        grad_gain[...] = gain_part
        grad_offset[...] = offset_part
        grad_br[...] = jnp.sum(out_grad, axis=0, keepdims=True)
        low = total.astype(BF16)
        shared[:, 2 * sz.width : 3 * sz.width] = low
        grad_bo[...] = jnp.sum(low.astype(F32), axis=0, keepdims=True)
        for quarter in range(4):
            wide = sz.width // 4
            grad_attended = dot_cols(low, wo[quarter * wide : (quarter + 1) * wide, :])
            for pair in range(wide // LANES):
                both = grad_attended[:, pair * LANES : (pair + 1) * LANES]
                head = 2 * (quarter * (wide // LANES) + pair)
                msg[head] = fold_head(both, sz, False).astype(BF16)
                msg[head + 1] = fold_head(both, sz, True).astype(BF16)


def feed(sz, place, tokens, heads_in, wo, bo, gain, offset, we, be, wr, br, cot):
    span = 512
    steps = sz.ff // span
    whole = lambda *shape: pl.BlockSpec(shape, lambda j: (0,) * len(shape), pipeline_mode=pl.Buffered(1))
    shape = jax.ShapeDtypeStruct
    vector = whole(1, sz.width)
    vector_out = shape((1, sz.width), F32)
    return pl.pallas_call(
        lambda *refs: feed_kernel(sz, *refs),
        grid=(steps,),
        in_specs=[
            pl.BlockSpec(memory_space=pltpu.SMEM),
            whole(sz.rows, sz.width),
            whole(sz.heads, sz.fold, LANES),
            whole(sz.width, sz.width),
            vector,
            vector,
            vector,
            pl.BlockSpec((sz.width, span), lambda j: (0, j)),
            pl.BlockSpec((1, span), lambda j: (0, j)),
            pl.BlockSpec((span, sz.width), lambda j: (j, 0)),
            vector,
            whole(sz.rows, sz.width),
        ],
        out_specs=[
            whole(sz.rows, sz.width),
            whole(sz.rows, sz.width),
            whole(sz.heads, sz.fold, LANES),
            whole(sz.rows, 3 * sz.width),
            pl.BlockSpec((sz.rows, span), lambda j: (0, j)),
            pl.BlockSpec((sz.rows, span // 2), lambda j: (0, j)),
            pl.BlockSpec((sz.rows, span // 2), lambda j: (0, j)),
            pl.BlockSpec((1, span), lambda j: (0, j)),
            vector,
            vector,
            vector,
            vector,
        ],
        out_shape=[
            shape((sz.rows, sz.width), BF16),
            shape((sz.rows, sz.width), F32),
            shape((sz.heads, sz.fold, LANES), BF16),
            shape((sz.rows, 3 * sz.width), BF16),
            shape((sz.rows, sz.ff), BF16),
            shape((sz.rows, sz.ff // 2), BF16),
            shape((sz.rows, sz.ff // 2), BF16),
            shape((1, sz.ff), F32),
            vector_out,
            vector_out,
            vector_out,
            vector_out,
        ],
        scratch_shapes=[pltpu.VMEM((sz.rows, sz.width), F32)] * 3,
        compiler_params=params(),
        cost_estimate=cost(28),
        name="feed",
    )(place, tokens, heads_in, wo, bo, gain, offset, we, be, wr, br, cot)


def weights_kernel(sz, place, act, act_got, cot, cot_got, back, back_got, norm, norm_got, *refs):
    att, att_got, low, low_got = refs[:4]
    wr_own, wr_sent, first_own, first_sent, next_own, next_sent = refs[4:10]
    wo_out = refs[10 : 10 + sz.m]
    norm_t, norm_t_got = refs[10 + sz.m :]
    step = pl.program_id(0)
    core, low_bit, mine_dp = place[0], place[1], place[1 + sz.bits]
    per = sz.width // sz.n

    def core_rows(block):
        turned = block[...].astype(F32).T.reshape(sz.n // 2, 2, per, sz.rows)
        return choose([turned[:, 0], turned[:, 1]], core).reshape(sz.width // 2, sz.rows).astype(BF16)

    @pl.when(step == 0)
    def _():
        norm_t[...] = core_rows(norm)
        norm_t_got[...] = core_rows(norm_got)
        grad_wo = dot(core_rows(att), low[...]) + dot(core_rows(att_got), low_got[...])
        grad_wo = grad_wo.reshape(sz.n // 2, sz.m, per // sz.m, sz.width)
        sides = [grad_wo[:, q] for q in range(sz.m)]
        for by in range(sz.m):
            wo_out[by][...] = choose(sides, lax.rem(mine_dp + by, sz.m)).astype(BF16)

    groups = act.shape[1] // (sz.ff // sz.n)
    grad_wr = (dot_rows(act[...], cot[...]) + dot_rows(act_got[...], cot_got[...])).astype(BF16)
    grad_wr = grad_wr.reshape(groups, sz.ff // sz.n, sz.width)
    if groups == 1:

        @pl.when(step % 2 == low_bit)
        def _():
            wr_own[...] = grad_wr

        @pl.when(step % 2 != low_bit)
        def _():
            wr_sent[...] = grad_wr

    else:
        wr_own[...] = choose([grad_wr[0:1], grad_wr[1:2]], low_bit)
        wr_sent[...] = choose([grad_wr[0:1], grad_wr[1:2]], 1 - low_bit)
    grad_we = dot(norm_t[...], back[...]) + dot(norm_t_got[...], back_got[...])

    def split(bit, own, sent):
        above, below = sz.n // 4 >> bit, (1 << bit) * sz.m
        parts = grad_we.reshape(above, 2, below, per // sz.m, grad_we.shape[1])
        sides = [parts[:, 0], parts[:, 1]]
        own[...] = choose(sides, place[1 + bit]).astype(BF16).reshape(own.shape)
        sent[...] = choose(sides, 1 - place[1 + bit]).astype(BF16).reshape(sent.shape)

    @pl.when(step < pl.num_programs(0) // 2)
    def _():
        split(2, first_own, first_sent)

    @pl.when(step >= pl.num_programs(0) // 2)
    def _():
        split(1, next_own, next_sent)


def weights(sz, place, act, act_got, cot, cot_got, back, back_got, shared, shared_got):
    span = sz.width
    steps = sz.ff // span
    fan = sz.ff // sz.width
    half = sz.n // 2
    few = sz.width // sz.shards
    whole = lambda *shape: pl.BlockSpec(shape, lambda j: (0,) * len(shape))
    column = lambda k: pl.BlockSpec((sz.rows, sz.width), lambda j: (0, k))
    block = pl.BlockSpec((sz.rows, span), lambda j: (0, j))
    act_block = pl.BlockSpec((sz.rows, span // 2), lambda j: (0, j))
    shape = jax.ShapeDtypeStruct
    groups = half // steps
    wr_block = pl.BlockSpec((1, sz.ff // sz.n, sz.width), lambda j: (j * groups // 2, 0, 0))
    wr_out = shape((half // 2, sz.ff // sz.n, sz.width), BF16)
    wo_dims = (half, few, sz.width)
    last_j = steps // 2 - 1
    first_block = pl.BlockSpec((half // 2 * sz.m, 1, few, span), lambda j: (0, jnp.minimum(j, last_j), 0, 0))
    next_block = pl.BlockSpec((half // 2 * sz.m, 1, few, span), lambda j: (0, jnp.maximum(j - last_j - 1, 0), 0, 0))
    we_out = shape((half // 2 * sz.m, fan // 2, few, sz.width), BF16)
    return pl.pallas_call(
        lambda *refs: weights_kernel(sz, *refs),
        grid=(steps,),
        in_specs=[
            pl.BlockSpec(memory_space=pltpu.SMEM),
            act_block,
            act_block,
            whole(sz.rows, sz.width),
            whole(sz.rows, sz.width),
            block,
            block,
        ]
        + [column(k // 2) for k in range(6)],
        out_specs=[wr_block] * 2 + [first_block] * 2 + [next_block] * 2 + [whole(*wo_dims)] * sz.m,
        out_shape=[wr_out] * 2 + [we_out] * 4 + [shape(wo_dims, BF16)] * sz.m,
        scratch_shapes=[pltpu.VMEM((sz.width // 2, sz.rows), BF16)] * 2,
        compiler_params=params(),
        cost_estimate=cost(10),
        name="weights",
    )(place, act, act_got, cot, cot_got, back, back_got, *([shared, shared_got] * 3))


def finish_kernel(sz, back, wq, wk, wv, tok, gain, grad_hidden, input_grad, grad_normed):
    step = pl.program_id(0)
    left = lane_index((sz.rows, LANES)) < HEAD_DIM
    left_fold = lane_index((sz.fold, LANES)) < HEAD_DIM
    queries, keys, values = [], [], []
    for pair in range(wq.shape[1] // LANES):
        kv_a = back[2 * pair, 0 : sz.rows, :].astype(F32)
        kv_b = back[2 * pair + 1, 0 : sz.rows, :].astype(F32)
        q_a = back[2 * pair, sz.slot : sz.slot + sz.fold, :].astype(F32)
        q_b = back[2 * pair + 1, sz.slot : sz.slot + sz.fold, :].astype(F32)
        low = jnp.where(left_fold, q_a, swap_halves(q_b))
        high = jnp.where(left_fold, swap_halves(q_a), q_b)[: sz.rest]
        queries.append(jnp.concatenate([low, high], axis=0).astype(BF16))
        keys.append(jnp.where(left, kv_a, swap_halves(kv_b)).astype(BF16))
        values.append(jnp.where(left, swap_halves(kv_a), kv_b).astype(BF16))
    total = jnp.zeros((sz.rows, sz.width), F32)
    for parts, weight in ((queries, wq), (keys, wk), (values, wv)):
        total = total + dot_cols(jnp.concatenate(parts, axis=1), weight[...])

    @pl.when(step == 0)
    def _():
        grad_normed[...] = total

    @pl.when(step > 0)
    def _():
        grad_normed[...] += total

    @pl.when(step == pl.num_programs(0) - 1)
    def _():
        part, _, _ = norm_back(grad_normed[...], tok[...].astype(F32), gain[...])
        input_grad[...] = grad_hidden[...] + part


def finish(sz, back, weight, tokens, gain, grad_hidden):
    cols = 512
    steps = sz.width // cols
    whole = lambda *shape: pl.BlockSpec(shape, lambda j: (0,) * len(shape))
    part = lambda k: pl.BlockSpec((sz.width, cols), lambda j: (0, k * steps + j))
    return pl.pallas_call(
        lambda *refs: finish_kernel(sz, *refs),
        grid=(steps,),
        in_specs=[
            pl.BlockSpec((cols // HEAD_DIM, sz.msg, LANES), lambda j: (j, 0, 0)),
            part(0),
            part(1),
            part(2),
            whole(sz.rows, sz.width),
            whole(1, sz.width),
            whole(sz.rows, sz.width),
        ],
        out_specs=whole(sz.rows, sz.width),
        out_shape=jax.ShapeDtypeStruct((sz.rows, sz.width), F32),
        scratch_shapes=[pltpu.VMEM((sz.rows, sz.width), F32)],
        compiler_params=params(sz, 54),
        cost_estimate=cost(10),
        name="finish",
    )(back, weight, weight, weight, tokens, gain, grad_hidden)


def pick(array, axis, index):
    return lax.dynamic_index_in_dim(array, index, axis, keepdims=False)


def after(value, *others):
    return lax.optimization_barrier((value,) + others)[0]


class Side:
    def __init__(self, sz, labels, rows, arrays):
        self.dims = [(label, sz.m if label == "dp" else 2) for label in labels]
        self.rows = rows
        self.width = sz.width
        self.arrays = list(arrays)

    def split(self, label):
        at = [name for name, _ in self.dims].index(label)
        before, after_it = 1, self.rows
        for _, size in self.dims[:at]:
            before *= size
        for _, size in self.dims[at + 1 :]:
            after_it *= size
        count = self.dims[at][1]
        self.dims = self.dims[:at] + self.dims[at + 1 :]
        return before, count, after_it

    def total(self):
        return sum(array.astype(F32) for array in self.arrays).reshape(self.rows, self.width)


def halve_kernel(shapes, place, *refs):
    at = 0
    outs = sum(adds * count for adds, count in shapes)
    for adds, count in shapes:
        for _ in range(count):
            total = refs[at][:, 0].astype(F32)
            for more in range(1, adds):
                total = total + refs[at + more][:, 0].astype(F32)
            refs[outs][...] = total.astype(BF16)
            at += adds
            outs += 1


def halve(sz, place, sides, labels):
    parts = [side.split(label) for side, label in zip(sides, labels)]
    grid = 2 if all(before % 2 == 0 for before, _, _ in parts) else 1
    ins, in_specs, out_specs, out_shape = [], [], [], []
    for side, label, (before, count, rest) in zip(sides, labels, parts):
        which = 1 + sz.bits if label == "dp" else 1 + label
        for by in range(count):
            for array in side.arrays:
                ins.append(array.reshape(before, count, rest, sz.width))
                in_specs.append(
                    pl.BlockSpec(
                        (before // grid, 1, rest, sz.width),
                        lambda g, place, which=which, by=by, count=count: (g, lax.rem(place[which] + by, count), 0, 0),
                    )
                )
            out_specs.append(pl.BlockSpec((before // grid, rest, sz.width), lambda g, place: (g, 0, 0)))
            out_shape.append(jax.ShapeDtypeStruct((before, rest, sz.width), BF16))
    shapes = [(len(side.arrays), count) for side, (_, count, _) in zip(sides, parts)]
    outs = pl.pallas_call(
        lambda *refs: halve_kernel(shapes, *refs),
        grid_spec=pltpu.PrefetchScalarGridSpec(
            num_scalar_prefetch=1, grid=(grid,), in_specs=in_specs, out_specs=out_specs
        ),
        out_shape=out_shape,
        compiler_params=params(sz, 20),
        cost_estimate=cost(4),
        name="halve",
    )(place, *ins)
    sent = []
    for side, (_, count, _) in zip(sides, parts):
        side.arrays = [outs[0]]
        sent.append(list(outs[1:count]))
        outs = outs[count:]
    return sent


def send(sz, label, blocks):
    if label == "dp":
        return [
            lax.ppermute(block, "dp", [(i, (i + by + 1) % sz.m) for i in range(sz.m)])
            for by, block in enumerate(blocks)
        ]
    bit = 2 << label
    return [lax.ppermute(block, "seq", [(i, i ^ bit) for i in range(sz.n)]) for block in blocks]


def swap(sz, block, by):
    return block if by == 0 else lax.ppermute(block, "seq", [(i, i ^ by) for i in range(sz.n)])


def trade_near(sz, blocks):
    me = lax.axis_index("seq")
    blocks = blocks.reshape((sz.n // 4, 4) + blocks.shape[1:])
    return jnp.stack([swap(sz, pick(blocks, 1, me % 4 ^ by), by) for by in range(4)], axis=1)


def trade_far(sz, near):
    me = lax.axis_index("seq")
    return jnp.stack([swap(sz, pick(near, 0, me // 4 ^ by), 4 * by) for by in range(sz.n // 4)], axis=0)


def last_kernel(sz, adds, spans, place, far, gain, offset, weight, *refs):
    ins, outs = refs[: sum(adds)], refs[sum(adds) :]
    totals = []
    for count in adds:
        total = ins[0][...].astype(F32)
        for more in range(1, count):
            total = total + ins[more][...].astype(F32)
        totals.append(total)
        ins = ins[count:]
    wr, we, wo, wt, bias_all, gain_one, offset_one = outs[:7]
    few = sz.width // sz.shards
    wr[...] = totals[0]
    half = sz.ff // sz.width // 2
    for part in range(2 * half):
        rows = totals[1 + part // half][part % half * few : (part % half + 1) * few]
        we[:, part * sz.width : (part + 1) * sz.width] = rows
    wo[...] = totals[3]
    low = place[0] + 2 * place[1]
    high = place[2]
    for bit in range(2, sz.bits):
        high = high + place[1 + bit] * 2 ** (bit - 1)

    def piece(src):
        return far[jnp.bitwise_xor(high, src // 4), jnp.bitwise_xor(low, src % 4)].astype(F32)

    left = lane_index((1, LANES)) < HEAD_DIM
    small = jnp.zeros((8, LANES), F32)
    along = jnp.zeros((8, LANES), F32)
    moved = jnp.zeros((few, 1), F32)
    for pair in range(sz.heads // 2):
        a = piece(2 * pair * sz.rep)
        b = piece((2 * pair + 1) * sz.rep)
        kv_a, kv_b, q_a, q_b = a[:, :LANES], b[:, :LANES], a[:, LANES:], b[:, LANES:]
        along = along + q_a[:8] + q_b[:8]
        blocks = (
            jnp.where(left, q_a, swap_halves(q_b)),
            jnp.where(left, kv_a, swap_halves(kv_b)),
            jnp.where(left, swap_halves(kv_a), kv_b),
        )
        side = jnp.where(left, swap_halves(q_a[:8]), q_b[:8])
        for part, row in ((0, 2), (1, 0), (2, 1)):
            cols = slice(part * sz.width + pair * LANES, part * sz.width + (pair + 1) * LANES)
            wt[:, cols] = blocks[part]
            bias_all[:, cols] = side[row : row + 1]
            rows = weight[:, cols].astype(F32) * side[row : row + 1]
            moved = moved + jnp.sum(rows, axis=1, keepdims=True)
    for src in range(sz.n):
        small = small + piece(src)[:8, LANES:]
    along = swap_halves(along)[7:8]
    small = swap_halves(small)
    small = jnp.concatenate([small[3 + row : 4 + row, :HEAD_DIM] for row in range(4)], axis=1)
    moved = jnp.broadcast_to(moved, (few, LANES)).T[0:1]
    offset_one[...] = moved
    gain_one[...] = (along[:, :few] - offset[0] * moved) / gain[0]
    at = 0
    for out, span in zip(outs[7:], spans):
        out[...] = small[:, at : at + span]
        at += span


def last(sz, place, sides, far, gain, offset, weight, spans):
    few = sz.width // sz.shards
    shard = lambda g, place: (place[2 + sz.bits], 0, 0)
    whole = lambda *shape: pl.BlockSpec(shape, lambda g, place: (0,) * len(shape))
    ins, in_specs = [], []
    for side in sides:
        for array in side.arrays:
            ins.append(array.reshape(side.rows, sz.width))
            in_specs.append(whole(side.rows, sz.width))
    out_dims = [(sides[0].rows, sz.width), (few, sz.ff), (few, sz.width), (few, 3 * sz.width), (1, 3 * sz.width)]
    out_dims = out_dims + [(1, few), (1, few)] + [(1, span) for span in spans]
    return pl.pallas_call(
        lambda *refs: last_kernel(sz, [len(side.arrays) for side in sides], spans, *refs),
        grid_spec=pltpu.PrefetchScalarGridSpec(
            num_scalar_prefetch=1,
            grid=(1,),
            in_specs=[
                whole(*far.shape),
                pl.BlockSpec((1, 1, few), shard),
                pl.BlockSpec((1, 1, few), shard),
                pl.BlockSpec((few, 3 * sz.width), lambda g, place: (place[2 + sz.bits], 0)),
            ]
            + in_specs,
            out_specs=[whole(*dims) for dims in out_dims],
        ),
        out_shape=[jax.ShapeDtypeStruct(dims, F32) for dims in out_dims],
        compiler_params=params(sz, 50),
        cost_estimate=cost(5),
        name="last",
    )(place, far, gain.reshape(sz.shards, 1, few), offset.reshape(sz.shards, 1, few), weight, *ins)


def per_device(
    tokens,
    clip_start,
    frames,
    positions,
    first_gain,
    first_offset,
    triple_weight,
    triple_bias,
    output_weight,
    output_bias,
    second_gain,
    second_offset,
    expand_weight,
    expand_bias,
    reduce_weight,
    reduce_bias,
    cotangent,
):
    rows, width = tokens.shape[1:]
    ff = expand_weight.shape[1]
    n = lax.axis_size("seq")
    m = lax.axis_size("dp")
    slabs = clip_start.shape[1]
    sz = Sizes(rows, width, ff, n, m, slabs)
    shards = n * m
    group_slabs = n * slabs
    lower, upper = slab_bounds(clip_start[0], frames[0], lax.axis_index("seq") * slabs, group_slabs)
    first_unit = lower[0] // CLIP_MIN
    unit_count = (upper[0] - lower[0]) // CLIP_MIN
    corners = positions[0].reshape(3, slabs, -1)[:, :, 0].T.reshape(-1)
    meta = jnp.concatenate([jnp.stack([first_unit, unit_count]), corners])[:8, None]
    meta = jnp.where(jnp.arange(LANES) < HEAD_DIM, 0, meta).astype(F32)
    cos, sin = lane_tables(positions[0])
    row = lambda vector: vector.reshape(1, -1)
    me, mine_dp = lax.axis_index("seq"), lax.axis_index("dp")
    place = jnp.stack([me % 2] + [me // (2 << bit) % 2 for bit in range(sz.bits)] + [mine_dp, me * m + mine_dp])
    swap_core = lambda block: lax.ppermute(block, "seq", [(i, i ^ 1) for i in range(n)])

    def exchange(message):
        if sz.rep > 1:
            message = jnp.repeat(message, sz.rep, axis=0)
        return lax.all_to_all(message, "seq", 0, 0, tiled=True)

    cot_got = swap_core(cotangent[0])
    head = me // sz.rep * HEAD_DIM
    head_weight = [
        lax.dynamic_slice(triple_weight, (0, k * width + head), (width, HEAD_DIM)) for k in (1, 2, 0)
    ]
    head_weight = jnp.concatenate(head_weight + [jnp.zeros((width, HEAD_DIM), BF16)], axis=1)
    message, normed = project(
        sz, tokens[0], row(first_gain), row(first_offset), triple_weight, row(triple_bias), cos, sin, meta
    )
    recv = exchange(message)
    chips = list(range(0, n // 2, 2)) + list(range(n // 2 - 1, 0, -2))
    ring = [2 * chip + core for chip in chips for core in range(2)]
    normed_all = lax.all_gather(after(normed, recv), "seq", axis=0, tiled=False, axis_index_groups=[ring])
    facts = recv[:, sz.msg - 8 :, LANES - 1].astype(jnp.int32)
    unit_first, unit_span = facts[:: sz.per_unit, 0], facts[:: sz.per_unit, 1]
    turns = all_turns(all_places(sz, facts[:, 2:]))
    out_message, kept, qs, kvs = attend(sz, unit_first, unit_span, recv)
    heads_in = lax.all_to_all(out_message, "seq", 0, 0, tiled=True)[:: sz.rep]
    (
        result,
        grad_hidden,
        grad_message,
        shared,
        grad_exp,
        act_sent,
        act_own,
        grad_be,
        grad_second_gain,
        grad_second_offset,
        grad_bo,
        grad_br,
    ) = feed(
        sz,
        place,
        tokens[0],
        after(heads_in, turns),
        output_weight,
        row(output_bias),
        row(second_gain),
        row(second_offset),
        expand_weight,
        row(expand_bias),
        reduce_weight,
        row(reduce_bias),
        cotangent[0],
    )
    recv_grad = exchange(grad_message)
    half = n // 2
    fan = ff // width
    few = width // shards
    many = ff // shards
    wr_own, wr_sent, first_own, first_sent, next_own, next_sent, *wo_parts = weights(
        sz,
        place,
        act_own,
        swap_core(act_sent),
        cotangent[0],
        cot_got,
        grad_exp,
        swap_core(grad_exp),
        shared,
        swap_core(shared),
    )
    bits = list(range(sz.bits - 1, -1, -1))
    side_r = Side(sz, bits[:-1] + ["dp"], many, [wr_own])
    without = lambda label: [bit for bit in bits if bit != label] + ["dp"]
    side_e = Side(sz, without(2), many // 2, [first_own])
    side_f = Side(sz, without(1), many // 2, [next_own])
    side_o = Side(sz, bits, few, [wo_parts[0]])
    sides = [side_r, side_e, side_f, side_o]
    sent = [[wr_sent], [first_sent], [next_sent], wo_parts[1:]]
    rounds = [(0, 2, 1, "dp"), (1, "dp", 0, 2), ("dp", 0, "dp", 0), (2, 1, 2, 1)]
    rounds = rounds + [(bit,) * 4 for bit in range(3, sz.bits)]

    def move(labels):
        return [send(sz, label, blocks) for label, blocks in zip(labels, sent)]

    def add(got, marker):
        for side, blocks in zip(sides, got):
            side.arrays = side.arrays + list(after(blocks, marker))

    got = move(rounds[0])
    dos, grad_q, grad_kv = attend_back_first(
        sz, unit_first, unit_span, after(recv_grad, wo_parts[0]), qs, kvs, kept
    )
    add(got, grad_kv)
    sent = halve(sz, place, sides, rounds[1])
    got = move(rounds[1])
    back_message = attend_back_last(
        sz, unit_first, unit_span, after(dos, sent), qs, kvs, kept, grad_q, grad_kv, turns
    )
    back = lax.all_to_all(after(back_message, got), "seq", 0, 0, tiled=True)[:: sz.rep]
    add(got, back_message)
    sent = halve(sz, place, sides, rounds[2])
    got = move(rounds[2])
    head_grad = triple_grad(sz, after(back_message, sent), normed_all)
    columns = [grad_bo, grad_second_gain, grad_second_offset, grad_be, grad_br]
    columns = [column.reshape(shards, -1) for column in after(columns, back_message)]
    spans = [column.shape[1] for column in columns]
    head_grad = after(head_grad, got)
    small = jnp.concatenate(columns, axis=1)
    small = jnp.pad(small, ((0, 0), (0, 4 * HEAD_DIM - small.shape[1]))).reshape(shards, 4, HEAD_DIM)
    along = jnp.sum(head_grad * head_weight.astype(F32), axis=1).reshape(shards, 1, few)
    along = jnp.pad(along, ((0, 0), (0, 0), (0, HEAD_DIM - few)))
    spare = jnp.concatenate([small, along], axis=1)
    spare = jnp.pad(spare, ((0, 0), (3, few - 8), (3 * HEAD_DIM, 0)))
    head_parts = (head_grad.reshape(shards, few, 4 * HEAD_DIM) + spare).reshape(n, m, few, 4 * HEAD_DIM)
    head_sum = pick(head_parts, 1, mine_dp)
    for by in range(1, m):
        block = pick(head_parts, 1, (mine_dp + by) % m).astype(BF16)
        head_sum = head_sum + lax.ppermute(block, "dp", [(i, (i + by) % m) for i in range(m)]).astype(F32)
    near = trade_near(sz, head_sum.astype(BF16))
    back = after(back, near)
    add(got, back_message)
    for step, labels in enumerate(rounds[3:]):
        if step > 0:
            add(got, back)
        sent = after(halve(sz, place, sides, labels), back)
        got = move(labels)
    far = trade_far(sz, near)
    input_grad = finish(
        sz, after(back, sent, far), triple_weight, tokens[0], row(first_gain), grad_hidden
    )
    add(got, input_grad)
    (
        out_wr,
        out_we,
        out_wo,
        out_wt,
        bias_all,
        gain_one,
        offset_one,
        *vectors,
    ) = last(sz, place, sides, far, first_gain, first_offset, triple_weight, spans)
    shard = me * m + mine_dp
    bias_qk = lax.dynamic_slice(bias_all[0], (shard * 2 * few,), (2 * few,))
    bias_v = lax.dynamic_slice(bias_all[0], (2 * width + shard * few,), (few,))
    gain_one, offset_one = gain_one[0], offset_one[0]
    bias_o, gain_two, offset_two, bias_e, bias_r = [vector[0] for vector in vectors]
    return (
        result[None],
        input_grad[None],
        gain_one,
        offset_one,
        out_wt,
        bias_qk,
        bias_v,
        out_wo,
        bias_o,
        gain_two,
        offset_two,
        out_we,
        bias_e,
        out_wr,
        bias_r,
    )


def solution(mesh):
    sharded = P("dp", "seq", None)
    placed = (
        (sharded, P("dp", "seq"), P("dp", "seq"), P("dp", None, "seq"))
        + (P(),) * 12
        + (sharded,)
    )
    vector = P(("seq", "dp"))
    matrix = P(("seq", "dp"), None)
    return jax.shard_map(
        per_device,
        mesh=mesh,
        in_specs=placed,
        out_specs=(sharded, sharded, vector, vector, matrix, vector, vector, matrix, vector)
        + (vector, vector, matrix, vector, matrix, vector),
        check_vma=False,
    )
```

```python
import jax
import jax.numpy as jnp
import numpy as np
from jax import lax
from jax.experimental import pallas as pl
from jax.experimental.pallas import tpu as pltpu
from jax.sharding import PartitionSpec as P

HEAD_DIM = 64
CLIP_MIN = 4
CLIP_MAX = 16
EPSILON = 1e-06
MASKED = 1e30
SECTIONS = ((0, 10), (20, 11), (42, 11))
LANES = 128
F32 = jnp.float32
BF16 = jnp.bfloat16
VMEM_LIMIT = 63 * 2**20
Q_TILE = 256
SAFE_ABOVE = 60.0
BACK_SHARE = (3, 4)


def dot(left, right):
    return jnp.dot(left, right, preferred_element_type=F32)


def dot_cols(left, right):
    return lax.dot_general(left, right, (((1,), (1,)), ((), ())), preferred_element_type=F32)


def dot_rows(left, right):
    return lax.dot_general(left, right, (((0,), (0,)), ((), ())), preferred_element_type=F32)


def cost(micros):
    return pl.CostEstimate(flops=int(micros * 1.15e9), bytes_accessed=2**20, transcendentals=0)


def params(sz=None, mib=0):
    if sz is not None and sz.n <= 16:
        return pltpu.CompilerParams(vmem_limit_bytes=mib * 2**20)
    return pltpu.CompilerParams(vmem_limit_bytes=VMEM_LIMIT)


def lane_index(shape):
    return lax.broadcasted_iota(jnp.int32, shape, len(shape) - 1)


def swap_halves(pair):
    return pltpu.roll(pair, HEAD_DIM, 1)


def rotate_pair(pair, cos_lanes, sin_lanes, inverse):
    lane = lane_index((1, LANES)) % HEAD_DIM
    sign = -1.0 if inverse else 1.0
    total = pair * cos_lanes
    for half in (10, 11):
        first = jnp.zeros(lane.shape, jnp.bool_)
        second = jnp.zeros(lane.shape, jnp.bool_)
        for begin_at, count in SECTIONS:
            if count == half:
                first = first | ((lane >= begin_at) & (lane < begin_at + half))
                second = second | ((lane >= begin_at + half) & (lane < begin_at + 2 * half))
        minus = jnp.where(first, -sign, 0.0)
        plus = jnp.where(second, sign, 0.0)
        total = total + pltpu.roll(pair, LANES - half, 1) * (sin_lanes * minus)
        total = total + pltpu.roll(pair, half, 1) * (sin_lanes * plus)
    return total


def lane_tables(positions):
    angles = jnp.zeros((positions.shape[1], LANES), F32)
    for section, (begin_at, count) in enumerate(SECTIONS):
        frequency = jnp.power(10000.0, -jnp.arange(count, dtype=F32) / count)
        in_head = jnp.zeros((HEAD_DIM,), F32)
        in_head = in_head.at[begin_at : begin_at + count].set(frequency)
        in_head = in_head.at[begin_at + count : begin_at + 2 * count].set(frequency)
        lanes = jnp.tile(in_head, LANES // HEAD_DIM)
        angles = angles + positions[section].astype(F32)[:, None] * lanes[None, :]
    return jnp.cos(angles), jnp.sin(angles)


def all_places(sz, corners):
    slabs = corners.shape[1] // 3
    per_slab = sz.rows // slabs
    side = int(round(per_slab**0.5))
    inside = jnp.arange(per_slab)
    steps = jnp.stack([jnp.zeros_like(inside), inside // side, inside % side])
    places = corners.reshape(sz.n, slabs, 3).transpose(0, 2, 1)[..., None] + steps[None, :, None, :]
    return places.reshape(sz.n, 3, sz.rows)


def all_turns(places):
    spots = jnp.arange(16)
    table = []
    for section in range(len(SECTIONS)):
        only = jnp.where(jnp.arange(len(SECTIONS))[:, None] == section, spots[None, :], 0)
        cos, sin = lane_tables(only)
        lane = jnp.arange(LANES)
        begin_at, count = SECTIONS[section]
        inside = (lane % HEAD_DIM >= begin_at) & (lane % HEAD_DIM < begin_at + 2 * count)
        table.append(jnp.where(inside, jnp.where(lane < HEAD_DIM, cos, sin), 0.0))
    table = jnp.concatenate(table, axis=0)
    hit = places.transpose(0, 2, 1)[..., None] == spots
    hit = hit.reshape(hit.shape[:2] + table.shape[:1]).astype(F32)
    hit = jnp.pad(hit, ((0, 0), (0, -hit.shape[1] % 16), (0, 0))).reshape(-1, table.shape[0])
    return jnp.dot(hit, table, precision=lax.Precision.HIGHEST)


def slab_bounds(clip_start, frames, first_slab, group_slabs):
    slab_index = first_slab + jnp.arange(clip_start.shape[-1], dtype=jnp.int32)
    unit_base = slab_index // CLIP_MIN * CLIP_MIN
    lower_slab = jnp.maximum(
        jnp.maximum(jnp.minimum(clip_start, slab_index), unit_base - (CLIP_MAX - CLIP_MIN)), 0
    )
    upper_slab = jnp.minimum(
        jnp.minimum(jnp.maximum(clip_start + frames // 2, slab_index + 1), unit_base + CLIP_MAX),
        group_slabs,
    )
    return lower_slab, upper_slab


def norm_parts(rows):
    centred = rows - jnp.mean(rows, axis=-1, keepdims=True)
    spread = jnp.mean(centred * centred, axis=-1, keepdims=True)
    scale = lax.rsqrt(spread + EPSILON)
    return centred * scale, scale


def norm_back(grad, rows, gain):
    unit, scale = norm_parts(rows)
    inner = grad * gain
    part = scale * (
        inner
        - jnp.mean(inner, axis=-1, keepdims=True)
        - unit * jnp.mean(inner * unit, axis=-1, keepdims=True)
    )
    return part, jnp.sum(grad * unit, axis=0, keepdims=True), jnp.sum(grad, axis=0, keepdims=True)


class Sizes:
    def __init__(self, rows, width, ff, n, m, slabs):
        self.rows = rows
        self.width = width
        self.ff = ff
        self.n = n
        self.m = m
        self.heads = width // HEAD_DIM
        self.rep = n // self.heads
        self.slabs = slabs
        self.shards = n * m
        self.bits = (n // 2).bit_length() - 1
        self.per_unit = CLIP_MIN // slabs
        self.units = n // self.per_unit
        self.slot = (rows + 15) // 16 * 16
        self.unit_rows = self.slot * self.per_unit
        self.tokens = self.slot * n
        self.fold = (rows // 2 + 15) // 16 * 16
        self.rest = rows - self.fold
        self.msg = self.slot + self.fold


def pad_rows(block, count):
    if block.shape[0] == count:
        return block
    return jnp.concatenate([block, jnp.zeros((count - block.shape[0], block.shape[1]), F32)], axis=0)


def fold_head(block, sz, right):
    low = block[: sz.fold]
    high = pad_rows(block[sz.fold :], sz.fold)
    left = lane_index(low.shape) < HEAD_DIM
    if right:
        folded = jnp.where(left, swap_halves(low), high)
    else:
        folded = jnp.where(left, low, swap_halves(high))
    return folded


def turn_table():
    table = np.zeros((LANES, 2 * LANES), np.float32)
    for section, (begin_at, count) in enumerate(SECTIONS):
        frequency = np.power(10000.0, -np.arange(count) / count)
        for place in range(16):
            for head in range(LANES // HEAD_DIM):
                for half in range(2):
                    at = head * HEAD_DIM + begin_at + half * count
                    table[16 * section + place, at : at + count] = np.cos(place * frequency)
                    at = at + LANES
                    table[16 * section + place, at : at + count] = np.sin(place * frequency)
    return jnp.asarray(table)


def own_turns(sz, facts, table):
    slabs = sz.slabs
    per_slab = sz.rows // slabs
    side = int(round(per_slab**0.5))
    row = lax.broadcasted_iota(jnp.int32, (sz.rows, 1), 0)
    inside = row
    first = [jnp.full((sz.rows, 1), facts[2 + section]) for section in range(3)]
    for slab in range(1, slabs):
        here = row >= slab * per_slab
        inside = jnp.where(here, row - slab * per_slab, inside)
        first = [jnp.where(here, facts[2 + 3 * slab + section], first[section]) for section in range(3)]
    down = jnp.floor((inside.astype(F32) + 0.5) * (1.0 / side)).astype(jnp.int32)
    lane = lane_index((1, LANES))
    place = jnp.where(lane < 16, first[0], jnp.where(lane < 32, first[1] + down, first[2] + inside - down * side))
    hit = jnp.where((place == lane % 16) & (lane < 48), 1.0, 0.0)
    return jnp.dot(hit, table, precision=lax.Precision.HIGHEST, preferred_element_type=F32)


def project_kernel(sz, facts, tok, gain, offset, wq, wk, wv, bq, bk, bv, table, msg, normed_out, turns):
    step = pl.program_id(0)

    @pl.when(step == 0)
    def _():
        unit, _ = norm_parts(tok[...].astype(F32))
        rows = (unit * gain[...] + offset[...]).astype(BF16)
        normed_out[0 : sz.rows, :] = rows
        normed_out[sz.rows :, :] = jnp.zeros((sz.slot - sz.rows, sz.width), BF16)
        turns[...] = own_turns(sz, facts, table[...])

    cos = turns.at[:, 0:LANES]
    sin = turns.at[:, LANES:]
    row = lax.broadcasted_iota(jnp.int32, (8, LANES), 0)
    meta = jnp.zeros((8, LANES), F32)
    for place in range(8):
        right = (row == place) & (lane_index((8, LANES)) >= HEAD_DIM)
        meta = jnp.where(right, facts[place].astype(F32), meta)
    normed = normed_out[0 : sz.rows, :]
    query = dot(normed, wq[...]) + bq[...]
    key = dot(normed, wk[...]) + bk[...]
    value = dot(normed, wv[...]) + bv[...]
    left = lane_index((sz.rows, LANES)) < HEAD_DIM
    spare = sz.slot - sz.rows
    spare_facts = jnp.concatenate([jnp.zeros((sz.fold - 8, LANES), F32), meta], axis=0)
    for pair in range(query.shape[1] // LANES):
        cols = slice(pair * LANES, (pair + 1) * LANES)
        q_pair = rotate_pair(query[:, cols], cos[...], sin[...], False) * 0.125
        k_pair = rotate_pair(key[:, cols], cos[...], sin[...], False)
        v_pair = value[:, cols]
        both = (jnp.where(left, k_pair, swap_halves(v_pair)), jnp.where(left, swap_halves(k_pair), v_pair))
        for head in range(2):
            tail = jnp.where(left[:spare], both[head][sz.rows - spare :], 0.0)
            folded = fold_head(q_pair, sz, head == 1) + spare_facts
            rows = jnp.concatenate([both[head], tail, folded], axis=0)
            msg[2 * pair + head] = rows.astype(BF16)


def project(sz, facts, tokens, gain, offset, weight, bias):
    cols = 256
    steps = sz.width // cols
    whole = lambda shape: pl.BlockSpec(shape, lambda j: (0,) * len(shape))
    part = lambda k: pl.BlockSpec((sz.width, cols), lambda j: (0, k * steps + j))
    part_bias = lambda k: pl.BlockSpec((1, cols), lambda j: (0, k * steps + j))
    heads = cols // HEAD_DIM
    return pl.pallas_call(
        lambda *refs: project_kernel(sz, *refs),
        grid=(steps,),
        in_specs=[pl.BlockSpec(memory_space=pltpu.SMEM)]
        + [whole((sz.rows, sz.width)), whole((1, sz.width)), whole((1, sz.width))]
        + [part(0), part(1), part(2), part_bias(0), part_bias(1), part_bias(2)]
        + [whole((LANES, 2 * LANES))],
        out_specs=[
            pl.BlockSpec((heads, sz.msg, LANES), lambda j: (j, 0, 0)),
            whole((sz.slot, sz.width)),
        ],
        out_shape=[
            jax.ShapeDtypeStruct((sz.heads, sz.msg, LANES), BF16),
            jax.ShapeDtypeStruct((sz.slot, sz.width), BF16),
        ],
        scratch_shapes=[pltpu.VMEM((sz.rows, 2 * LANES), F32)],
        compiler_params=params(),
        cost_estimate=cost(8),
        name="project",
    )(facts, tokens, gain, offset, weight, weight, weight, bias, bias, bias, turn_table())


def unfold_slot(folded, sz, right):
    wide = folded.astype(F32)
    left = lane_index(wide.shape) < HEAD_DIM
    keep = ~left if right else left
    swapped = swap_halves(wide)
    low, high = (swapped, wide) if right else (wide, swapped)
    return (
        jnp.where(keep, low, 0.0).astype(BF16),
        jnp.where(keep, high, 0.0)[: sz.slot - sz.fold].astype(BF16),
    )


def unfold_into(target, at, folded, sz, right):
    low, high = unfold_slot(folded, sz, right)
    target[pl.ds(at, sz.fold), :] = low
    target[pl.ds(at + sz.fold, sz.slot - sz.fold), :] = high


def loop(count, body):
    def step(index, carry):
        body(index)
        return carry

    lax.fori_loop(0, count, step, 0)


def attend_kernel(sz, first, count, recv, out, kept, qs, kvs, ones_v):
    def unpack(src):
        at = pl.multiple_of(src * sz.slot, 16)
        unfold_into(qs, at, recv[src, sz.slot :, :], sz, False)
        kv = recv[src, 0 : sz.slot, :]
        kvs[pl.ds(at, sz.slot), :] = kv
        left = lane_index((1, LANES)) < HEAD_DIM
        real = lax.broadcasted_iota(jnp.int32, (sz.slot, 1), 0) < sz.rows
        one = jnp.where(real, 1.0, 0.0)
        ones_v[pl.ds(at, sz.slot), :] = jnp.where(left, one, kv.astype(F32)).astype(BF16)

    loop(sz.n, unpack)
    qs[sz.tokens :, :] = jnp.zeros((Q_TILE, LANES), BF16)
    kept[sz.tokens :, :] = jnp.zeros((Q_TILE, LANES), F32)

    def one(unit):
        rows = pl.ds(pl.multiple_of(unit * sz.unit_rows, 16), sz.unit_rows)
        begin = pl.multiple_of(first[unit] * sz.unit_rows, 16)

        def keep(shift, mixed):
            total = mixed[:, 0:1]
            left = lane_index((1, LANES)) < HEAD_DIM
            kept[rows, :] = jnp.where(left, shift + jnp.log(total), mixed * (1.0 / total))

        for span in (1, 2, 4):

            @pl.when(count[unit] == span)
            def _():
                clip = pl.ds(begin, span * sz.unit_rows)
                some = dot_cols(qs[rows, :], kvs[pl.ds(begin, 2 * LANES), :])
                shift = jnp.max(some, axis=1, keepdims=True)
                scores = dot_cols(qs[rows, :], kvs[clip, :])
                prob = jnp.exp(scores - shift).astype(BF16)
                keep(shift, dot(prob, ones_v[clip, :]))
                above = jnp.max(jnp.max(scores, axis=1, keepdims=True) - shift)

                @pl.when(above > SAFE_ABOVE)
                def _():
                    scores = dot_cols(qs[rows, :], kvs[clip, :])
                    peak = jnp.max(scores, axis=1, keepdims=True)
                    prob = jnp.exp(scores - peak).astype(BF16)
                    keep(peak, dot(prob, ones_v[clip, :]))

    loop(sz.units, one)

    def pack(src):
        at = pl.multiple_of(src * sz.slot, 16)
        out[src] = fold_head(kept[pl.ds(at, sz.slot), :][: sz.rows], sz, True).astype(BF16)
        left = lane_index((sz.slot - sz.rows, LANES)) < HEAD_DIM
        kept[pl.ds(at + sz.rows, sz.slot - sz.rows), :] = jnp.where(left, MASKED, 0.0)

    loop(sz.n, pack)


def attend(sz, first, count, recv):
    smem = pl.BlockSpec(memory_space=pltpu.SMEM)
    vmem = pl.BlockSpec(memory_space=pltpu.VMEM)
    shape = jax.ShapeDtypeStruct
    return pl.pallas_call(
        lambda *refs: attend_kernel(sz, *refs),
        in_specs=[smem, smem, vmem],
        out_specs=[vmem] * 4,
        out_shape=[
            shape((sz.n, sz.fold, LANES), BF16),
            shape((sz.tokens + Q_TILE, LANES), F32),
            shape((sz.tokens + Q_TILE, LANES), BF16),
            shape((sz.tokens, LANES), BF16),
        ],
        scratch_shapes=[pltpu.VMEM((sz.tokens, LANES), BF16)],
        compiler_params=params(),
        cost_estimate=cost(32),
        name="attend",
    )(first, count, recv)


def back_tiles(sz, part, first, count, qs, kvs, dos, kept, grad_q, grad_kv, key_t):
    def one(unit):
        begin = pl.multiple_of(unit * sz.unit_rows, 16)
        for span in (1, 2, 4):

            @pl.when((count[unit] == span) & (first[unit] == unit))
            def _():
                length = span * sz.unit_rows
                clip = pl.ds(begin, length)
                turned = kvs[clip, :].astype(F32).T[:HEAD_DIM]
                real = lax.rem(lane_index((1, length)), sz.slot) < sz.rows
                key_t[:, 0:length] = jnp.where(real, turned, 0.0).astype(BF16)

                def q_tile(t, carry):
                    rows = pl.ds(pl.multiple_of(begin + t * Q_TILE, 16), Q_TILE)
                    query = qs[rows, :]
                    grad = dos[rows, :]
                    kept_rows = kept[rows, :]
                    left = lane_index((Q_TILE, LANES)) < HEAD_DIM
                    turned = jnp.where(left, kept_rows, kept_rows * grad.astype(F32)).T
                    inside = lane_index((1, Q_TILE)) < length - t * Q_TILE
                    log_total = jnp.where(inside, turned[0:1, :], MASKED)
                    delta = jnp.sum(turned[HEAD_DIM:, :], axis=0, keepdims=True)
                    keys = kvs[clip, :]
                    prob = jnp.exp(dot_cols(keys, query) - log_total)
                    grad_prob = dot_cols(keys, grad)
                    grad_scores = (prob * (grad_prob - delta)).astype(BF16)
                    grad_kv[clip, :] += dot(grad_scores, query) + dot(prob.astype(BF16), grad)
                    grad_query = dot(key_t[:, 0:length], grad_scores) * 0.125
                    grad_query = jnp.concatenate([grad_query, jnp.zeros_like(grad_query)], axis=0).T
                    if part == 1:
                        own = lax.broadcasted_iota(jnp.int32, (Q_TILE, 1), 0) < length - t * Q_TILE
                        grad_query = jnp.where(own, grad_query, grad_q[rows, :])
                    grad_q[rows, :] = grad_query
                    return carry

                tiles = (length + Q_TILE - 1) // Q_TILE
                middle = (tiles * BACK_SHARE[0] + BACK_SHARE[1] - 1) // BACK_SHARE[1]
                lax.fori_loop(*((0, middle) if part == 0 else (middle, tiles)), q_tile, 0)

    loop(sz.units, one)


def back_first_kernel(sz, first, count, recv_grad, qs, kvs, kept, dos, grad_q, grad_kv, key_t):
    dos[sz.tokens :, :] = jnp.zeros((Q_TILE, LANES), BF16)

    def unpack(src):
        at = pl.multiple_of(src * sz.slot, 16)
        unfold_into(dos, at, recv_grad[src], sz, True)
        grad_kv[pl.ds(at, sz.slot), :] = jnp.zeros((sz.slot, LANES), F32)

    loop(sz.n, unpack)
    back_tiles(sz, 0, first, count, qs, kvs, dos, kept, grad_q, grad_kv, key_t)


def back_last_kernel(
    sz, first, count, dos, qs, kvs, kept, grad_q_in, grad_kv_in, turns, out, grad_q, grad_kv, key_t
):
    def copy(src):
        rows = pl.ds(pl.multiple_of(src * sz.slot, 16), sz.slot)
        grad_q[rows, :] = grad_q_in[rows, :]
        grad_kv[rows, :] = grad_kv_in[rows, :]

    loop(sz.n, copy)
    back_tiles(sz, 1, first, count, qs, kvs, dos, kept, grad_q, grad_kv, key_t)

    def pack(src):
        rows = pl.ds(pl.multiple_of(src * sz.slot, 16), sz.slot)
        kv = grad_kv[rows, :]
        left = lane_index((1, LANES)) < HEAD_DIM
        real = lax.broadcasted_iota(jnp.int32, (sz.slot, 1), 0) < sz.rows
        both = jnp.where(left, grad_q[rows, :], swap_halves(kv))
        table = turns[rows, :]
        other = swap_halves(table)
        both = rotate_pair(both, jnp.where(left, table, other), jnp.where(left, other, table), True)
        out[src, 0 : sz.slot, :] = jnp.where(real, jnp.where(left, swap_halves(both), kv), 0.0).astype(BF16)
        out[src, sz.slot :, :] = fold_head(both[: sz.rows], sz, False).astype(BF16)

    loop(sz.n, pack)


def attend_back_first(sz, first, count, recv_grad, qs, kvs, kept):
    smem = pl.BlockSpec(memory_space=pltpu.SMEM)
    vmem = pl.BlockSpec(memory_space=pltpu.VMEM)
    shape = jax.ShapeDtypeStruct
    return pl.pallas_call(
        lambda *refs: back_first_kernel(sz, *refs),
        in_specs=[smem, smem] + [vmem] * 4,
        out_specs=[vmem] * 3,
        out_shape=[
            shape((sz.tokens + Q_TILE, LANES), BF16),
            shape((sz.tokens + Q_TILE, LANES), F32),
            shape((sz.tokens, LANES), F32),
        ],
        scratch_shapes=[pltpu.VMEM((HEAD_DIM, CLIP_MAX // CLIP_MIN * sz.unit_rows), BF16)],
        compiler_params=params(sz, 18),
        cost_estimate=cost(40),
        name="attend_back_first",
    )(first, count, recv_grad, qs, kvs, kept)


def attend_back_last(sz, first, count, dos, qs, kvs, kept, grad_q, grad_kv, turns):
    smem = pl.BlockSpec(memory_space=pltpu.SMEM)
    vmem = pl.BlockSpec(memory_space=pltpu.VMEM)
    shape = jax.ShapeDtypeStruct
    return pl.pallas_call(
        lambda *refs: back_last_kernel(sz, *refs),
        in_specs=[smem, smem] + [vmem] * 7,
        out_specs=vmem,
        out_shape=shape((sz.n, sz.msg, LANES), BF16),
        scratch_shapes=[
            pltpu.VMEM((sz.tokens + Q_TILE, LANES), F32),
            pltpu.VMEM((sz.tokens, LANES), F32),
            pltpu.VMEM((HEAD_DIM, CLIP_MAX // CLIP_MIN * sz.unit_rows), BF16),
        ],
        compiler_params=params(sz, 18),
        cost_estimate=cost(20),
        name="attend_back_last",
    )(first, count, dos, qs, kvs, kept, grad_q, grad_kv, turns)


def triple_grad_kernel(sz, grads, normed, out, total):
    step = pl.program_id(0)
    high = sz.slot - sz.fold
    part_kv = jnp.zeros((LANES, sz.width), F32)
    part_q = jnp.zeros((HEAD_DIM, sz.width), F32)
    sums = jnp.zeros((1, 2 * LANES), F32)
    for src in range(grads.shape[0]):
        key_value = grads[src, 0 : sz.slot, :]
        query = grads[src, sz.slot :, :]
        part_kv = part_kv + dot_rows(key_value, normed[src])
        part_q = part_q + dot_rows(query, normed[src, 0 : sz.fold, :])[:HEAD_DIM]
        part_q = part_q + dot_rows(query[:high], normed[src, sz.fold :, :])[HEAD_DIM:]
        sum_kv = jnp.sum(key_value.astype(F32), axis=0, keepdims=True)
        sum_q = jnp.sum(query.astype(F32), axis=0, keepdims=True)
        sums = sums + jnp.concatenate([sum_kv, sum_q + swap_halves(sum_q)], axis=1)

    @pl.when(step == 0)
    def _():
        total[...] = jnp.zeros_like(total)

    total[0:LANES, :] += part_kv
    total[LANES : LANES + HEAD_DIM, :] += part_q
    total[2 * LANES :, 0 : 2 * LANES] += jnp.broadcast_to(sums, (8, 2 * LANES))

    @pl.when(step == pl.num_programs(0) - 1)
    def _():
        few = sz.width // sz.shards
        bias = total[2 * LANES : 2 * LANES + 1, 0 : 2 * LANES]
        place = lax.broadcasted_iota(jnp.int32, (sz.width, 1), 0) % few
        left = lane_index((1, LANES)) < HEAD_DIM
        out[:, 0:LANES] = total[0:LANES, :].T
        queries = total[LANES : 2 * LANES, :].T
        kv_row, q_row = bias[:, 0:LANES], bias[:, LANES:]
        side = jnp.where(place == 0, swap_halves(kv_row), jnp.where(place == 1, kv_row, 0.0))
        side = jnp.where(place == 2, q_row, side)
        out[:, LANES:] = jnp.where(left, queries, side)


def triple_grad(sz, grads, normed_all):
    shape = jax.ShapeDtypeStruct
    last = sz.n // 2 - 1
    return pl.pallas_call(
        lambda *refs: triple_grad_kernel(sz, *refs),
        grid=(sz.n // 2,),
        in_specs=[
            pl.BlockSpec((2, sz.msg, LANES), lambda j: (j, 0, 0)),
            pl.BlockSpec((2, sz.slot, sz.width), lambda j: (jnp.where(j % 2 == 0, j // 2, last - j // 2), 0, 0)),
        ],
        out_specs=pl.BlockSpec((sz.width, 2 * LANES), lambda j: (0, 0)),
        out_shape=shape((sz.width, 2 * LANES), F32),
        scratch_shapes=[pltpu.VMEM((2 * LANES + 8, sz.width), F32)],
        compiler_params=params(sz, 54),
        cost_estimate=cost(1),
        name="triple_grad",
    )(grads, normed_all)


def choose(pieces, index):
    picked = pieces[0]
    for at in range(1, len(pieces)):
        picked = jnp.where(index == at, pieces[at], picked)
    return picked


def core_cols(block, width, side):
    count = block.shape[1] // (2 * width)
    groups = [block[:, g * width : (g + 1) * width] for g in range(2 * count)]
    return jnp.concatenate([choose(groups[2 * g : 2 * g + 2], side) for g in range(count)], axis=1)


def feed_kernel(sz, place, tok, heads_in, wo, bo, gain, offset, we, be, wr, br, cot, *refs):
    result, grad_hidden, msg, shared, grad_exp, act_sent, act_own = refs[:7]
    small = refs[7]
    hidden, reduced, grad_normed = refs[8:]
    step = pl.program_id(0)
    core = place[0]
    left = lane_index((sz.fold, LANES)) < HEAD_DIM
    normed = shared.at[:, 0 : sz.width]
    attended = shared.at[:, sz.width : 2 * sz.width]

    @pl.when(step == 0)
    def _():
        for pair in range(sz.heads // 2):
            a = heads_in[2 * pair, 0 : sz.fold, :].astype(F32)
            b = heads_in[2 * pair + 1, 0 : sz.fold, :].astype(F32)
            low = jnp.where(left, a, swap_halves(b))
            high = jnp.where(left, swap_halves(a), b)[: sz.rest]
            both = jnp.concatenate([low, high], axis=0)
            attended[:, pair * LANES : (pair + 1) * LANES] = both.astype(BF16)
        rows = tok[...].astype(F32) + (dot(attended[...], wo[...]) + bo[...])
        hidden[...] = rows
        unit, _ = norm_parts(rows)
        normed[...] = (unit * gain[...] + offset[...]).astype(BF16)
        reduced[...] = jnp.zeros_like(reduced)
        grad_normed[...] = jnp.zeros_like(grad_normed)

    expanded = dot(normed[...], we[...]) + be[...]
    below = 0.5 * (1.0 + lax.erf(expanded * 0.7071067811865476))
    bell = jnp.exp(expanded * expanded * -0.5) * 0.3989422804014327
    activated = expanded * below
    slope = below + expanded * bell
    act_low = activated.astype(BF16)
    reduced[...] += dot(act_low, wr[...])
    grad_expanded = (dot_cols(cot[...], wr[...]) * slope).astype(BF16)
    span = act_low.shape[1]
    per = sz.width // span
    lanes = pl.ds(pl.multiple_of(lax.rem(step, per) * span, LANES), span)
    small[pl.ds(4 + step // per, 1), lanes] = jnp.sum(grad_expanded.astype(F32), axis=0, keepdims=True)
    grad_normed[...] += dot_cols(grad_expanded, we[...])
    act_own[...] = core_cols(activated, sz.ff // sz.n, core).astype(BF16)
    act_sent[...] = core_cols(activated, sz.ff // sz.n, 1 - core).astype(BF16)
    grad_exp[...] = grad_expanded

    @pl.when(step == pl.num_programs(0) - 1)
    def _():
        rows = hidden[...]
        out_grad = cot[...].astype(F32)
        result[...] = (rows + (reduced[...] + br[...])).astype(BF16)
        part, gain_part, offset_part = norm_back(grad_normed[...], rows, gain[...])
        total = out_grad + part
        grad_hidden[...] = total
        low = total.astype(BF16)
        small[0:1, :] = jnp.sum(low.astype(F32), axis=0, keepdims=True)
        small[1:2, :] = gain_part
        small[2:3, :] = offset_part
        small[3:4, :] = jnp.sum(out_grad, axis=0, keepdims=True)
        shared[:, 2 * sz.width : 3 * sz.width] = low
        for quarter in range(4):
            wide = sz.width // 4
            grad_attended = dot_cols(low, wo[quarter * wide : (quarter + 1) * wide, :])
            for pair in range(wide // LANES):
                both = grad_attended[:, pair * LANES : (pair + 1) * LANES]
                head = 2 * (quarter * (wide // LANES) + pair)
                msg[head] = fold_head(both, sz, False).astype(BF16)
                msg[head + 1] = fold_head(both, sz, True).astype(BF16)


def feed(sz, place, tokens, heads_in, wo, bo, gain, offset, we, be, wr, br, cot):
    span = 512
    steps = sz.ff // span
    whole = lambda *shape: pl.BlockSpec(shape, lambda j: (0,) * len(shape), pipeline_mode=pl.Buffered(1))
    shape = jax.ShapeDtypeStruct
    vector = whole(1, sz.width)
    return pl.pallas_call(
        lambda *refs: feed_kernel(sz, *refs),
        grid=(steps,),
        in_specs=[
            pl.BlockSpec(memory_space=pltpu.SMEM),
            whole(sz.rows, sz.width),
            whole(sz.heads, sz.fold, LANES),
            whole(sz.width, sz.width),
            vector,
            vector,
            vector,
            pl.BlockSpec((sz.width, span), lambda j: (0, j)),
            pl.BlockSpec((1, span), lambda j: (0, j)),
            pl.BlockSpec((span, sz.width), lambda j: (j, 0)),
            vector,
            whole(sz.rows, sz.width),
        ],
        out_specs=[
            whole(sz.rows, sz.width),
            whole(sz.rows, sz.width),
            whole(sz.heads, sz.fold, LANES),
            whole(sz.rows, 3 * sz.width),
            pl.BlockSpec((sz.rows, span), lambda j: (0, j)),
            pl.BlockSpec((sz.rows, span // 2), lambda j: (0, j)),
            pl.BlockSpec((sz.rows, span // 2), lambda j: (0, j)),
            whole(4 + sz.ff // sz.width, sz.width),
        ],
        out_shape=[
            shape((sz.rows, sz.width), BF16),
            shape((sz.rows, sz.width), F32),
            shape((sz.heads, sz.fold, LANES), BF16),
            shape((sz.rows, 3 * sz.width), BF16),
            shape((sz.rows, sz.ff), BF16),
            shape((sz.rows, sz.ff // 2), BF16),
            shape((sz.rows, sz.ff // 2), BF16),
            shape((4 + sz.ff // sz.width, sz.width), F32),
        ],
        scratch_shapes=[pltpu.VMEM((sz.rows, sz.width), F32)] * 3,
        compiler_params=params(),
        cost_estimate=cost(28),
        name="feed",
    )(place, tokens, heads_in, wo, bo, gain, offset, we, be, wr, br, cot)


def weights_kernel(sz, place, act, act_got, cot, cot_got, back, back_got, norm, norm_got, *refs):
    att, att_got, low, low_got = refs[:4]
    wr_own, wr_sent, first_own, first_sent, next_own, next_sent = refs[4:10]
    wo_out = refs[10 : 10 + sz.m]
    norm_t, norm_t_got = refs[10 + sz.m :]
    step = pl.program_id(0)
    core, low_bit, mine_dp = place[0], place[1], place[1 + sz.bits]
    per = sz.width // sz.n

    def core_rows(block):
        turned = block[...].astype(F32).T.reshape(sz.n // 2, 2, per, sz.rows)
        return choose([turned[:, 0], turned[:, 1]], core).reshape(sz.width // 2, sz.rows).astype(BF16)

    @pl.when(step == 0)
    def _():
        norm_t[...] = core_rows(norm)
        norm_t_got[...] = core_rows(norm_got)
        grad_wo = dot(core_rows(att), low[...]) + dot(core_rows(att_got), low_got[...])
        grad_wo = grad_wo.reshape(sz.n // 2, sz.m, per // sz.m, sz.width)
        sides = [grad_wo[:, q] for q in range(sz.m)]
        for by in range(sz.m):
            wo_out[by][...] = choose(sides, lax.rem(mine_dp + by, sz.m)).astype(BF16)

    groups = act.shape[1] // (sz.ff // sz.n)
    grad_wr = (dot_rows(act[...], cot[...]) + dot_rows(act_got[...], cot_got[...])).astype(BF16)
    grad_wr = grad_wr.reshape(groups, sz.ff // sz.n, sz.width)
    if groups == 1:

        @pl.when(step % 2 == low_bit)
        def _():
            wr_own[...] = grad_wr

        @pl.when(step % 2 != low_bit)
        def _():
            wr_sent[...] = grad_wr

    else:
        wr_own[...] = choose([grad_wr[0:1], grad_wr[1:2]], low_bit)
        wr_sent[...] = choose([grad_wr[0:1], grad_wr[1:2]], 1 - low_bit)
    grad_we = dot(norm_t[...], back[...]) + dot(norm_t_got[...], back_got[...])

    def split(bit, own, sent):
        above, below = sz.n // 4 >> bit, (1 << bit) * sz.m
        parts = grad_we.reshape(above, 2, below, per // sz.m, grad_we.shape[1])
        sides = [parts[:, 0], parts[:, 1]]
        own[...] = choose(sides, place[1 + bit]).astype(BF16).reshape(own.shape)
        sent[...] = choose(sides, 1 - place[1 + bit]).astype(BF16).reshape(sent.shape)

    @pl.when(step < pl.num_programs(0) // 2)
    def _():
        split(2, first_own, first_sent)

    @pl.when(step >= pl.num_programs(0) // 2)
    def _():
        split(1, next_own, next_sent)


def weights(sz, place, act, act_got, cot, cot_got, back, back_got, shared, shared_got):
    span = sz.width
    steps = sz.ff // span
    fan = sz.ff // sz.width
    half = sz.n // 2
    few = sz.width // sz.shards
    whole = lambda *shape: pl.BlockSpec(shape, lambda j: (0,) * len(shape))
    column = lambda k: pl.BlockSpec((sz.rows, sz.width), lambda j: (0, k))
    block = pl.BlockSpec((sz.rows, span), lambda j: (0, j))
    act_block = pl.BlockSpec((sz.rows, span // 2), lambda j: (0, j))
    shape = jax.ShapeDtypeStruct
    groups = half // steps
    wr_block = pl.BlockSpec((1, sz.ff // sz.n, sz.width), lambda j: (j * groups // 2, 0, 0))
    wr_out = shape((half // 2, sz.ff // sz.n, sz.width), BF16)
    wo_dims = (half, few, sz.width)
    last_j = steps // 2 - 1
    first_block = pl.BlockSpec((half // 2 * sz.m, 1, few, span), lambda j: (0, jnp.minimum(j, last_j), 0, 0))
    next_block = pl.BlockSpec((half // 2 * sz.m, 1, few, span), lambda j: (0, jnp.maximum(j - last_j - 1, 0), 0, 0))
    we_out = shape((half // 2 * sz.m, fan // 2, few, sz.width), BF16)
    return pl.pallas_call(
        lambda *refs: weights_kernel(sz, *refs),
        grid=(steps,),
        in_specs=[
            pl.BlockSpec(memory_space=pltpu.SMEM),
            act_block,
            act_block,
            whole(sz.rows, sz.width),
            whole(sz.rows, sz.width),
            block,
            block,
        ]
        + [column(k // 2) for k in range(6)],
        out_specs=[wr_block] * 2 + [first_block] * 2 + [next_block] * 2 + [whole(*wo_dims)] * sz.m,
        out_shape=[wr_out] * 2 + [we_out] * 4 + [shape(wo_dims, BF16)] * sz.m,
        scratch_shapes=[pltpu.VMEM((sz.width // 2, sz.rows), BF16)] * 2,
        compiler_params=params(),
        cost_estimate=cost(10),
        name="weights",
    )(place, act, act_got, cot, cot_got, back, back_got, *([shared, shared_got] * 3))


def finish_kernel(sz, back, wq, wk, wv, tok, gain, grad_hidden, input_grad, grad_normed):
    step = pl.program_id(0)
    left = lane_index((sz.rows, LANES)) < HEAD_DIM
    left_fold = lane_index((sz.fold, LANES)) < HEAD_DIM
    queries, keys, values = [], [], []
    for pair in range(wq.shape[1] // LANES):
        kv_a = back[2 * pair, 0 : sz.rows, :].astype(F32)
        kv_b = back[2 * pair + 1, 0 : sz.rows, :].astype(F32)
        q_a = back[2 * pair, sz.slot : sz.slot + sz.fold, :].astype(F32)
        q_b = back[2 * pair + 1, sz.slot : sz.slot + sz.fold, :].astype(F32)
        low = jnp.where(left_fold, q_a, swap_halves(q_b))
        high = jnp.where(left_fold, swap_halves(q_a), q_b)[: sz.rest]
        queries.append(jnp.concatenate([low, high], axis=0).astype(BF16))
        keys.append(jnp.where(left, kv_a, swap_halves(kv_b)).astype(BF16))
        values.append(jnp.where(left, swap_halves(kv_a), kv_b).astype(BF16))
    total = jnp.zeros((sz.rows, sz.width), F32)
    for parts, weight in ((queries, wq), (keys, wk), (values, wv)):
        total = total + dot_cols(jnp.concatenate(parts, axis=1), weight[...])

    @pl.when(step == 0)
    def _():
        grad_normed[...] = total

    @pl.when(step > 0)
    def _():
        grad_normed[...] += total

    @pl.when(step == pl.num_programs(0) - 1)
    def _():
        part, _, _ = norm_back(grad_normed[...], tok[...].astype(F32), gain[...])
        input_grad[...] = grad_hidden[...] + part


def finish(sz, back, weight, tokens, gain, grad_hidden):
    cols = 512
    steps = sz.width // cols
    whole = lambda *shape: pl.BlockSpec(shape, lambda j: (0,) * len(shape))
    part = lambda k: pl.BlockSpec((sz.width, cols), lambda j: (0, k * steps + j))
    return pl.pallas_call(
        lambda *refs: finish_kernel(sz, *refs),
        grid=(steps,),
        in_specs=[
            pl.BlockSpec((cols // HEAD_DIM, sz.msg, LANES), lambda j: (j, 0, 0)),
            part(0),
            part(1),
            part(2),
            whole(sz.rows, sz.width),
            whole(1, sz.width),
            whole(sz.rows, sz.width),
        ],
        out_specs=whole(sz.rows, sz.width),
        out_shape=jax.ShapeDtypeStruct((sz.rows, sz.width), F32),
        scratch_shapes=[pltpu.VMEM((sz.rows, sz.width), F32)],
        compiler_params=params(sz, 54),
        cost_estimate=cost(10),
        name="finish",
    )(back, weight, weight, weight, tokens, gain, grad_hidden)


def pick(array, axis, index):
    return lax.dynamic_index_in_dim(array, index, axis, keepdims=False)


def after(value, *others):
    return lax.optimization_barrier((value,) + others)[0]


class Side:
    def __init__(self, sz, labels, rows, arrays):
        self.dims = [(label, sz.m if label == "dp" else 2) for label in labels]
        self.rows = rows
        self.width = sz.width
        self.arrays = list(arrays)

    def split(self, label):
        at = [name for name, _ in self.dims].index(label)
        before, after_it = 1, self.rows
        for _, size in self.dims[:at]:
            before *= size
        for _, size in self.dims[at + 1 :]:
            after_it *= size
        count = self.dims[at][1]
        self.dims = self.dims[:at] + self.dims[at + 1 :]
        return before, count, after_it

    def total(self):
        return sum(array.astype(F32) for array in self.arrays).reshape(self.rows, self.width)


def halve_kernel(shapes, place, *refs):
    at = 0
    outs = sum(adds * count for adds, count in shapes)
    for adds, count in shapes:
        for _ in range(count):
            total = refs[at][:, 0].astype(F32)
            for more in range(1, adds):
                total = total + refs[at + more][:, 0].astype(F32)
            refs[outs][...] = total.astype(BF16)
            at += adds
            outs += 1


def halve(sz, place, sides, labels, mib=63):
    parts = [side.split(label) for side, label in zip(sides, labels)]
    grid = 2 if all(before % 2 == 0 for before, _, _ in parts) else 1
    ins, in_specs, out_specs, out_shape = [], [], [], []
    for side, label, (before, count, rest) in zip(sides, labels, parts):
        which = 1 + sz.bits if label == "dp" else 1 + label
        for by in range(count):
            for array in side.arrays:
                ins.append(array.reshape(before, count, rest, sz.width))
                in_specs.append(
                    pl.BlockSpec(
                        (before // grid, 1, rest, sz.width),
                        lambda g, place, which=which, by=by, count=count: (g, lax.rem(place[which] + by, count), 0, 0),
                    )
                )
            out_specs.append(pl.BlockSpec((before // grid, rest, sz.width), lambda g, place: (g, 0, 0)))
            out_shape.append(jax.ShapeDtypeStruct((before, rest, sz.width), BF16))
    shapes = [(len(side.arrays), count) for side, (_, count, _) in zip(sides, parts)]
    outs = pl.pallas_call(
        lambda *refs: halve_kernel(shapes, *refs),
        grid_spec=pltpu.PrefetchScalarGridSpec(
            num_scalar_prefetch=1, grid=(grid,), in_specs=in_specs, out_specs=out_specs
        ),
        out_shape=out_shape,
        compiler_params=params(sz, mib),
        cost_estimate=cost(4),
        name="halve",
    )(place, *ins)
    sent = []
    for side, (_, count, _) in zip(sides, parts):
        side.arrays = [outs[0]]
        sent.append(list(outs[1:count]))
        outs = outs[count:]
    return sent


def send(sz, label, blocks):
    if label == "dp":
        return [
            lax.ppermute(block, "dp", [(i, (i + by + 1) % sz.m) for i in range(sz.m)])
            for by, block in enumerate(blocks)
        ]
    bit = 2 << label
    return [lax.ppermute(block, "seq", [(i, i ^ bit) for i in range(sz.n)]) for block in blocks]


def swap(sz, block, by):
    return block if by == 0 else lax.ppermute(block, "seq", [(i, i ^ by) for i in range(sz.n)])


def trade_near(sz, blocks):
    me = lax.axis_index("seq")
    blocks = blocks.reshape((sz.n // 4, 4) + blocks.shape[1:])
    return jnp.stack([swap(sz, pick(blocks, 1, me % 4 ^ by), by) for by in range(4)], axis=1)


def trade_far(sz, near):
    me = lax.axis_index("seq")
    return jnp.stack([swap(sz, pick(near, 0, me // 4 ^ by), 4 * by) for by in range(sz.n // 4)], axis=0)


def last_kernel(sz, adds, spans, place, far, gain, offset, weight, *refs):
    ins, outs = refs[: sum(adds)], refs[sum(adds) :]
    totals = []
    for count in adds:
        total = ins[0][...].astype(F32)
        for more in range(1, count):
            total = total + ins[more][...].astype(F32)
        totals.append(total)
        ins = ins[count:]
    wr, we, wo, wt, bias_all, gain_one, offset_one = outs[:7]
    few = sz.width // sz.shards
    wr[...] = totals[0]
    half = sz.ff // sz.width // 2
    for part in range(2 * half):
        rows = totals[1 + part // half][part % half * few : (part % half + 1) * few]
        we[:, part * sz.width : (part + 1) * sz.width] = rows
    wo[...] = totals[3]
    low = place[0] + 2 * place[1]
    high = place[2]
    for bit in range(2, sz.bits):
        high = high + place[1 + bit] * 2 ** (bit - 1)

    def piece(src):
        return far[jnp.bitwise_xor(high, src // 4), jnp.bitwise_xor(low, src % 4)].astype(F32)

    left = lane_index((1, LANES)) < HEAD_DIM
    small = jnp.zeros((8, LANES), F32)
    along = jnp.zeros((8, LANES), F32)
    moved = jnp.zeros((few, 1), F32)
    for pair in range(sz.heads // 2):
        a = piece(2 * pair * sz.rep)
        b = piece((2 * pair + 1) * sz.rep)
        kv_a, kv_b, q_a, q_b = a[:, :LANES], b[:, :LANES], a[:, LANES:], b[:, LANES:]
        along = along + q_a[:8] + q_b[:8]
        blocks = (
            jnp.where(left, q_a, swap_halves(q_b)),
            jnp.where(left, kv_a, swap_halves(kv_b)),
            jnp.where(left, swap_halves(kv_a), kv_b),
        )
        side = jnp.where(left, swap_halves(q_a[:8]), q_b[:8])
        for part, row in ((0, 2), (1, 0), (2, 1)):
            cols = slice(part * sz.width + pair * LANES, part * sz.width + (pair + 1) * LANES)
            wt[:, cols] = blocks[part]
            bias_all[:, cols] = side[row : row + 1]
            rows = weight[:, cols].astype(F32) * side[row : row + 1]
            moved = moved + jnp.sum(rows, axis=1, keepdims=True)
    for src in range(sz.n):
        small = small + piece(src)[:8, LANES:]
    along = swap_halves(along)[7:8]
    small = swap_halves(small)
    small = jnp.concatenate([small[3 + row : 4 + row, :HEAD_DIM] for row in range(4)], axis=1)
    moved = jnp.broadcast_to(moved, (few, LANES)).T[0:1]
    offset_one[...] = moved
    gain_one[...] = (along[:, :few] - offset[0] * moved) / gain[0]
    at = 0
    for out, span in zip(outs[7:], spans):
        out[...] = small[:, at : at + span]
        at += span


def last(sz, place, sides, far, gain, offset, weight, spans):
    few = sz.width // sz.shards
    shard = lambda g, place: (place[2 + sz.bits], 0, 0)
    whole = lambda *shape: pl.BlockSpec(shape, lambda g, place: (0,) * len(shape))
    ins, in_specs = [], []
    for side in sides:
        for array in side.arrays:
            ins.append(array.reshape(side.rows, sz.width))
            in_specs.append(whole(side.rows, sz.width))
    out_dims = [(sides[0].rows, sz.width), (few, sz.ff), (few, sz.width), (few, 3 * sz.width), (1, 3 * sz.width)]
    out_dims = out_dims + [(1, few), (1, few)] + [(1, span) for span in spans]
    return pl.pallas_call(
        lambda *refs: last_kernel(sz, [len(side.arrays) for side in sides], spans, *refs),
        grid_spec=pltpu.PrefetchScalarGridSpec(
            num_scalar_prefetch=1,
            grid=(1,),
            in_specs=[
                whole(*far.shape),
                pl.BlockSpec((1, 1, few), shard),
                pl.BlockSpec((1, 1, few), shard),
                pl.BlockSpec((few, 3 * sz.width), lambda g, place: (place[2 + sz.bits], 0)),
            ]
            + in_specs,
            out_specs=[whole(*dims) for dims in out_dims],
        ),
        out_shape=[jax.ShapeDtypeStruct(dims, F32) for dims in out_dims],
        compiler_params=params(sz, 50),
        cost_estimate=cost(5),
        name="last",
    )(place, far, gain.reshape(sz.shards, 1, few), offset.reshape(sz.shards, 1, few), weight, *ins)


def per_device(
    tokens,
    clip_start,
    frames,
    positions,
    first_gain,
    first_offset,
    triple_weight,
    triple_bias,
    output_weight,
    output_bias,
    second_gain,
    second_offset,
    expand_weight,
    expand_bias,
    reduce_weight,
    reduce_bias,
    cotangent,
):
    rows, width = tokens.shape[1:]
    ff = expand_weight.shape[1]
    n = lax.axis_size("seq")
    m = lax.axis_size("dp")
    slabs = clip_start.shape[1]
    sz = Sizes(rows, width, ff, n, m, slabs)
    shards = n * m
    group_slabs = n * slabs
    lower, upper = slab_bounds(clip_start[0], frames[0], lax.axis_index("seq") * slabs, group_slabs)
    first_unit = lower[0] // CLIP_MIN
    unit_count = (upper[0] - lower[0]) // CLIP_MIN
    corners = positions[0].reshape(3, slabs, -1)[:, :, 0].T.reshape(-1)
    own_facts = jnp.concatenate([jnp.stack([first_unit, unit_count]), corners]).astype(jnp.int32)
    row = lambda vector: vector.reshape(1, -1)
    me, mine_dp = lax.axis_index("seq"), lax.axis_index("dp")
    place = jnp.stack([me % 2] + [me // (2 << bit) % 2 for bit in range(sz.bits)] + [mine_dp, me * m + mine_dp])
    swap_core = lambda block: lax.ppermute(block, "seq", [(i, i ^ 1) for i in range(n)])

    def exchange(message):
        if sz.rep > 1:
            message = jnp.repeat(message, sz.rep, axis=0)
        return lax.all_to_all(message, "seq", 0, 0, tiled=True)

    cot_got = swap_core(cotangent[0])
    head = me // sz.rep * HEAD_DIM
    head_weight = [
        lax.dynamic_slice(triple_weight, (0, k * width + head), (width, HEAD_DIM)) for k in (1, 2, 0)
    ]
    head_weight = jnp.concatenate(head_weight + [jnp.zeros((width, HEAD_DIM), BF16)], axis=1)
    message, normed = project(
        sz, own_facts, tokens[0], row(first_gain), row(first_offset), triple_weight, row(triple_bias)
    )
    recv = exchange(message)
    chips = list(range(0, n // 2, 2)) + list(range(n // 2 - 1, 0, -2))
    ring = [2 * chip + core for chip in chips for core in range(2)]
    normed_all = lax.all_gather(after(normed, recv), "seq", axis=0, tiled=False, axis_index_groups=[ring])
    facts = recv[:, sz.msg - 8 :, LANES - 1].astype(jnp.int32)
    unit_first, unit_span = facts[:: sz.per_unit, 0], facts[:: sz.per_unit, 1]
    turns = all_turns(all_places(sz, facts[:, 2:]))
    out_message, kept, qs, kvs = attend(sz, unit_first, unit_span, recv)
    heads_in = lax.all_to_all(out_message, "seq", 0, 0, tiled=True)[:: sz.rep]
    (
        result,
        grad_hidden,
        grad_message,
        shared,
        grad_exp,
        act_sent,
        act_own,
        small,
    ) = feed(
        sz,
        place,
        tokens[0],
        after(heads_in, turns, head_weight),
        output_weight,
        row(output_bias),
        row(second_gain),
        row(second_offset),
        expand_weight,
        row(expand_bias),
        reduce_weight,
        row(reduce_bias),
        cotangent[0],
    )
    recv_grad = exchange(grad_message)
    half = n // 2
    fan = ff // width
    few = width // shards
    many = ff // shards
    wr_own, wr_sent, first_own, first_sent, next_own, next_sent, *wo_parts = weights(
        sz,
        place,
        act_own,
        swap_core(act_sent),
        cotangent[0],
        cot_got,
        grad_exp,
        swap_core(grad_exp),
        shared,
        swap_core(shared),
    )
    bits = list(range(sz.bits - 1, -1, -1))
    side_r = Side(sz, bits[:-1] + ["dp"], many, [wr_own])
    without = lambda label: [bit for bit in bits if bit != label] + ["dp"]
    side_e = Side(sz, without(2), many // 2, [first_own])
    side_f = Side(sz, without(1), many // 2, [next_own])
    side_o = Side(sz, bits, few, [wo_parts[0]])
    sides = [side_r, side_e, side_f, side_o]
    sent = [[wr_sent], [first_sent], [next_sent], wo_parts[1:]]
    rounds = [(0, 2, 1, "dp"), (1, "dp", 0, 2), ("dp", 0, "dp", 0), (2, 1, 2, 1)]
    rounds = rounds + [(bit,) * 4 for bit in range(3, sz.bits)]

    def move(labels):
        return [send(sz, label, blocks) for label, blocks in zip(labels, sent)]

    def add(got, marker):
        for side, blocks in zip(sides, got):
            side.arrays = side.arrays + list(after(blocks, marker))

    got = move(rounds[0])
    dos, grad_q, grad_kv = attend_back_first(
        sz, unit_first, unit_span, after(recv_grad, wo_parts[0]), qs, kvs, kept
    )
    add(got, grad_kv)
    sent = halve(sz, place, sides, rounds[1], 20)
    got = move(rounds[1])
    back_message = attend_back_last(
        sz, unit_first, unit_span, after(dos, sent), qs, kvs, kept, grad_q, grad_kv, turns
    )
    back = lax.all_to_all(after(back_message, got), "seq", 0, 0, tiled=True)[:: sz.rep]
    add(got, back_message)
    sent = halve(sz, place, sides, rounds[2], 20)
    got = move(rounds[2])
    head_grad = triple_grad(sz, after(back_message, sent), normed_all)
    small = after(small, back_message)
    small = [small[:4].reshape(4, shards, few).transpose(1, 0, 2).reshape(shards, -1), small[4:].reshape(shards, -1)]
    small = jnp.concatenate(small, axis=1)
    spans = [few] * 4 + [fan * few]
    small = jnp.pad(small, ((0, 0), (0, 4 * HEAD_DIM - small.shape[1]))).reshape(shards, 4, HEAD_DIM)
    head_grad = after(head_grad, got)
    along = jnp.sum(head_grad * head_weight.astype(F32), axis=1).reshape(shards, 1, few)
    along = jnp.pad(along, ((0, 0), (0, 0), (0, HEAD_DIM - few)))
    spare = jnp.concatenate([small, along], axis=1)
    spare = jnp.pad(spare, ((0, 0), (3, few - 8), (3 * HEAD_DIM, 0)))
    head_parts = (head_grad.reshape(shards, few, 4 * HEAD_DIM) + spare).reshape(n, m, few, 4 * HEAD_DIM)
    head_sum = pick(head_parts, 1, mine_dp)
    for by in range(1, m):
        block = pick(head_parts, 1, (mine_dp + by) % m).astype(BF16)
        head_sum = head_sum + lax.ppermute(block, "dp", [(i, (i + by) % m) for i in range(m)]).astype(F32)
    near = trade_near(sz, head_sum.astype(BF16))
    back = after(back, near)
    add(got, back_message)
    for step, labels in enumerate(rounds[3:]):
        if step > 0:
            add(got, back)
        sent = after(halve(sz, place, sides, labels), back)
        got = move(labels)
    far = trade_far(sz, near)
    input_grad = finish(
        sz, after(back, sent, far), triple_weight, tokens[0], row(first_gain), grad_hidden
    )
    add(got, input_grad)
    (
        out_wr,
        out_we,
        out_wo,
        out_wt,
        bias_all,
        gain_one,
        offset_one,
        *vectors,
    ) = last(sz, place, sides, far, first_gain, first_offset, triple_weight, spans)
    shard = me * m + mine_dp
    bias_qk = lax.dynamic_slice(bias_all[0], (shard * 2 * few,), (2 * few,))
    bias_v = lax.dynamic_slice(bias_all[0], (2 * width + shard * few,), (few,))
    gain_one, offset_one = gain_one[0], offset_one[0]
    bias_o, gain_two, offset_two, bias_r, bias_e = [vector[0] for vector in vectors]
    return (
        result[None],
        input_grad[None],
        gain_one,
        offset_one,
        out_wt,
        bias_qk,
        bias_v,
        out_wo,
        bias_o,
        gain_two,
        offset_two,
        out_we,
        bias_e,
        out_wr,
        bias_r,
    )


def solution(mesh):
    sharded = P("dp", "seq", None)
    placed = (
        (sharded, P("dp", "seq"), P("dp", "seq"), P("dp", None, "seq"))
        + (P(),) * 12
        + (sharded,)
    )
    vector = P(("seq", "dp"))
    matrix = P(("seq", "dp"), None)
    return jax.shard_map(
        per_device,
        mesh=mesh,
        in_specs=placed,
        out_specs=(sharded, sharded, vector, vector, matrix, vector, vector, matrix, vector)
        + (vector, vector, matrix, vector, matrix, vector),
        check_vma=False,
    )
```

```python
import jax
import jax.numpy as jnp
import numpy as np
from jax import lax
from jax.experimental import pallas as pl
from jax.experimental.pallas import tpu as pltpu
from jax.sharding import PartitionSpec as P

HEAD_DIM = 64
CLIP_MIN = 4
CLIP_MAX = 16
EPSILON = 1e-06
MASKED = 1e30
SECTIONS = ((0, 10), (20, 11), (42, 11))
LANES = 128
F32 = jnp.float32
BF16 = jnp.bfloat16
VMEM_LIMIT = 63 * 2**20
Q_TILE = 256
SAFE_ABOVE = 60.0
BACK_SHARE = (3, 4)


def dot(left, right):
    return jnp.dot(left, right, preferred_element_type=F32)


def dot_cols(left, right):
    return lax.dot_general(left, right, (((1,), (1,)), ((), ())), preferred_element_type=F32)


def dot_rows(left, right):
    return lax.dot_general(left, right, (((0,), (0,)), ((), ())), preferred_element_type=F32)


def cost(micros):
    return pl.CostEstimate(flops=int(micros * 1.15e9), bytes_accessed=2**20, transcendentals=0)


def params(sz=None, mib=0):
    if sz is not None and sz.n <= 16:
        return pltpu.CompilerParams(vmem_limit_bytes=mib * 2**20)
    return pltpu.CompilerParams(vmem_limit_bytes=VMEM_LIMIT)


def lane_index(shape):
    return lax.broadcasted_iota(jnp.int32, shape, len(shape) - 1)


def swap_halves(pair):
    return pltpu.roll(pair, HEAD_DIM, 1)


def rotate_pair(pair, cos_lanes, sin_lanes, inverse):
    lane = lane_index((1, LANES)) % HEAD_DIM
    sign = -1.0 if inverse else 1.0
    total = pair * cos_lanes
    for half in (10, 11):
        first = jnp.zeros(lane.shape, jnp.bool_)
        second = jnp.zeros(lane.shape, jnp.bool_)
        for begin_at, count in SECTIONS:
            if count == half:
                first = first | ((lane >= begin_at) & (lane < begin_at + half))
                second = second | ((lane >= begin_at + half) & (lane < begin_at + 2 * half))
        minus = jnp.where(first, -sign, 0.0)
        plus = jnp.where(second, sign, 0.0)
        total = total + pltpu.roll(pair, LANES - half, 1) * (sin_lanes * minus)
        total = total + pltpu.roll(pair, half, 1) * (sin_lanes * plus)
    return total


def lane_tables(positions):
    angles = jnp.zeros((positions.shape[1], LANES), F32)
    for section, (begin_at, count) in enumerate(SECTIONS):
        frequency = jnp.power(10000.0, -jnp.arange(count, dtype=F32) / count)
        in_head = jnp.zeros((HEAD_DIM,), F32)
        in_head = in_head.at[begin_at : begin_at + count].set(frequency)
        in_head = in_head.at[begin_at + count : begin_at + 2 * count].set(frequency)
        lanes = jnp.tile(in_head, LANES // HEAD_DIM)
        angles = angles + positions[section].astype(F32)[:, None] * lanes[None, :]
    return jnp.cos(angles), jnp.sin(angles)


def all_places(sz, corners):
    slabs = corners.shape[1] // 3
    per_slab = sz.rows // slabs
    side = int(round(per_slab**0.5))
    inside = jnp.arange(per_slab)
    steps = jnp.stack([jnp.zeros_like(inside), inside // side, inside % side])
    places = corners.reshape(sz.n, slabs, 3).transpose(0, 2, 1)[..., None] + steps[None, :, None, :]
    return places.reshape(sz.n, 3, sz.rows)


def all_turns(places):
    spots = jnp.arange(16)
    table = []
    for section in range(len(SECTIONS)):
        only = jnp.where(jnp.arange(len(SECTIONS))[:, None] == section, spots[None, :], 0)
        cos, sin = lane_tables(only)
        lane = jnp.arange(LANES)
        begin_at, count = SECTIONS[section]
        inside = (lane % HEAD_DIM >= begin_at) & (lane % HEAD_DIM < begin_at + 2 * count)
        table.append(jnp.where(inside, jnp.where(lane < HEAD_DIM, cos, sin), 0.0))
    table = jnp.concatenate(table, axis=0)
    hit = places.transpose(0, 2, 1)[..., None] == spots
    hit = hit.reshape(hit.shape[:2] + table.shape[:1]).astype(F32)
    hit = jnp.pad(hit, ((0, 0), (0, -hit.shape[1] % 16), (0, 0))).reshape(-1, table.shape[0])
    return jnp.dot(hit, table, precision=lax.Precision.HIGHEST)


def slab_bounds(clip_start, frames, first_slab, group_slabs):
    slab_index = first_slab + jnp.arange(clip_start.shape[-1], dtype=jnp.int32)
    unit_base = slab_index // CLIP_MIN * CLIP_MIN
    lower_slab = jnp.maximum(
        jnp.maximum(jnp.minimum(clip_start, slab_index), unit_base - (CLIP_MAX - CLIP_MIN)), 0
    )
    upper_slab = jnp.minimum(
        jnp.minimum(jnp.maximum(clip_start + frames // 2, slab_index + 1), unit_base + CLIP_MAX),
        group_slabs,
    )
    return lower_slab, upper_slab


def norm_parts(rows):
    centred = rows - jnp.mean(rows, axis=-1, keepdims=True)
    spread = jnp.mean(centred * centred, axis=-1, keepdims=True)
    scale = lax.rsqrt(spread + EPSILON)
    return centred * scale, scale


def norm_back(grad, rows, gain):
    unit, scale = norm_parts(rows)
    inner = grad * gain
    part = scale * (
        inner
        - jnp.mean(inner, axis=-1, keepdims=True)
        - unit * jnp.mean(inner * unit, axis=-1, keepdims=True)
    )
    return part, jnp.sum(grad * unit, axis=0, keepdims=True), jnp.sum(grad, axis=0, keepdims=True)


class Sizes:
    def __init__(self, rows, width, ff, n, m, slabs):
        self.rows = rows
        self.width = width
        self.ff = ff
        self.n = n
        self.m = m
        self.heads = width // HEAD_DIM
        self.rep = n // self.heads
        self.slabs = slabs
        self.shards = n * m
        self.bits = (n // 2).bit_length() - 1
        self.per_unit = CLIP_MIN // slabs
        self.units = n // self.per_unit
        self.slot = (rows + 15) // 16 * 16
        self.unit_rows = self.slot * self.per_unit
        self.tokens = self.slot * n
        self.fold = (rows // 2 + 15) // 16 * 16
        self.rest = rows - self.fold
        self.msg = self.slot + self.fold


def pad_rows(block, count):
    if block.shape[0] == count:
        return block
    return jnp.concatenate([block, jnp.zeros((count - block.shape[0], block.shape[1]), F32)], axis=0)


def fold_head(block, sz, right):
    low = block[: sz.fold]
    high = pad_rows(block[sz.fold :], sz.fold)
    left = lane_index(low.shape) < HEAD_DIM
    if right:
        folded = jnp.where(left, swap_halves(low), high)
    else:
        folded = jnp.where(left, low, swap_halves(high))
    return folded


def turn_table():
    table = np.zeros((LANES, 2 * LANES), np.float32)
    for section, (begin_at, count) in enumerate(SECTIONS):
        frequency = np.power(10000.0, -np.arange(count) / count)
        for place in range(16):
            for head in range(LANES // HEAD_DIM):
                for half in range(2):
                    at = head * HEAD_DIM + begin_at + half * count
                    table[16 * section + place, at : at + count] = np.cos(place * frequency)
                    at = at + LANES
                    table[16 * section + place, at : at + count] = np.sin(place * frequency)
    return jnp.asarray(table)


def own_turns(sz, facts, table):
    slabs = sz.slabs
    per_slab = sz.rows // slabs
    side = int(round(per_slab**0.5))
    row = lax.broadcasted_iota(jnp.int32, (sz.rows, 1), 0)
    inside = row
    first = [jnp.full((sz.rows, 1), facts[2 + section]) for section in range(3)]
    for slab in range(1, slabs):
        here = row >= slab * per_slab
        inside = jnp.where(here, row - slab * per_slab, inside)
        first = [jnp.where(here, facts[2 + 3 * slab + section], first[section]) for section in range(3)]
    down = jnp.floor((inside.astype(F32) + 0.5) * (1.0 / side)).astype(jnp.int32)
    lane = lane_index((1, LANES))
    place = jnp.where(lane < 16, first[0], jnp.where(lane < 32, first[1] + down, first[2] + inside - down * side))
    hit = jnp.where((place == lane % 16) & (lane < 48), 1.0, 0.0)
    return jnp.dot(hit, table, precision=lax.Precision.HIGHEST, preferred_element_type=F32)


def project_kernel(sz, facts, tok, gain, offset, wq, wk, wv, bq, bk, bv, table, msg, normed_out, turns):
    step = pl.program_id(0)

    @pl.when(step == 0)
    def _():
        unit, _ = norm_parts(tok[...].astype(F32))
        rows = (unit * gain[...] + offset[...]).astype(BF16)
        normed_out[0 : sz.rows, :] = rows
        normed_out[sz.rows :, :] = jnp.zeros((sz.slot - sz.rows, sz.width), BF16)
        turns[...] = own_turns(sz, facts, table[...])

    cos = turns.at[:, 0:LANES]
    sin = turns.at[:, LANES:]
    row = lax.broadcasted_iota(jnp.int32, (8, LANES), 0)
    meta = jnp.zeros((8, LANES), F32)
    for place in range(8):
        right = (row == place) & (lane_index((8, LANES)) >= HEAD_DIM)
        meta = jnp.where(right, facts[place].astype(F32), meta)
    normed = normed_out[0 : sz.rows, :]
    query = dot(normed, wq[...]) + bq[...]
    key = dot(normed, wk[...]) + bk[...]
    value = dot(normed, wv[...]) + bv[...]
    left = lane_index((sz.rows, LANES)) < HEAD_DIM
    spare = sz.slot - sz.rows
    spare_facts = jnp.concatenate([jnp.zeros((sz.fold - 8, LANES), F32), meta], axis=0)
    for pair in range(query.shape[1] // LANES):
        cols = slice(pair * LANES, (pair + 1) * LANES)
        q_pair = rotate_pair(query[:, cols], cos[...], sin[...], False) * 0.125
        k_pair = rotate_pair(key[:, cols], cos[...], sin[...], False)
        v_pair = value[:, cols]
        both = (jnp.where(left, k_pair, swap_halves(v_pair)), jnp.where(left, swap_halves(k_pair), v_pair))
        for head in range(2):
            tail = jnp.where(left[:spare], both[head][sz.rows - spare :], 0.0)
            folded = fold_head(q_pair, sz, head == 1) + spare_facts
            rows = jnp.concatenate([both[head], tail, folded], axis=0)
            msg[2 * pair + head] = rows.astype(BF16)


def project(sz, facts, tokens, gain, offset, weight, bias):
    cols = 256
    steps = sz.width // cols
    whole = lambda shape: pl.BlockSpec(shape, lambda j: (0,) * len(shape))
    part = lambda k: pl.BlockSpec((sz.width, cols), lambda j: (0, k * steps + j))
    part_bias = lambda k: pl.BlockSpec((1, cols), lambda j: (0, k * steps + j))
    heads = cols // HEAD_DIM
    return pl.pallas_call(
        lambda *refs: project_kernel(sz, *refs),
        grid=(steps,),
        in_specs=[pl.BlockSpec(memory_space=pltpu.SMEM)]
        + [whole((sz.rows, sz.width)), whole((1, sz.width)), whole((1, sz.width))]
        + [part(0), part(1), part(2), part_bias(0), part_bias(1), part_bias(2)]
        + [whole((LANES, 2 * LANES))],
        out_specs=[
            pl.BlockSpec((heads, sz.msg, LANES), lambda j: (j, 0, 0)),
            whole((sz.slot, sz.width)),
        ],
        out_shape=[
            jax.ShapeDtypeStruct((sz.heads, sz.msg, LANES), BF16),
            jax.ShapeDtypeStruct((sz.slot, sz.width), BF16),
        ],
        scratch_shapes=[pltpu.VMEM((sz.rows, 2 * LANES), F32)],
        compiler_params=params(),
        cost_estimate=cost(8),
        name="project",
    )(facts, tokens, gain, offset, weight, weight, weight, bias, bias, bias, turn_table())


def unfold_slot(folded, sz, right):
    wide = folded.astype(F32)
    left = lane_index(wide.shape) < HEAD_DIM
    keep = ~left if right else left
    swapped = swap_halves(wide)
    low, high = (swapped, wide) if right else (wide, swapped)
    return (
        jnp.where(keep, low, 0.0).astype(BF16),
        jnp.where(keep, high, 0.0)[: sz.slot - sz.fold].astype(BF16),
    )


def unfold_into(target, at, folded, sz, right):
    low, high = unfold_slot(folded, sz, right)
    target[pl.ds(at, sz.fold), :] = low
    target[pl.ds(at + sz.fold, sz.slot - sz.fold), :] = high


def loop(count, body, unroll=1):
    def step(index, carry):
        body(index)
        return carry

    lax.fori_loop(0, count, step, 0, unroll=unroll)


def attend_kernel(sz, first, count, recv, out, kept, qs, kvs, ones_v):
    def unpack(src):
        at = pl.multiple_of(src * sz.slot, 16)
        unfold_into(qs, at, recv[src, sz.slot :, :], sz, False)
        kv = recv[src, 0 : sz.slot, :]
        kvs[pl.ds(at, sz.slot), :] = kv
        left = lane_index((1, LANES)) < HEAD_DIM
        real = lax.broadcasted_iota(jnp.int32, (sz.slot, 1), 0) < sz.rows
        one = jnp.where(real, 1.0, 0.0)
        ones_v[pl.ds(at, sz.slot), :] = jnp.where(left, one, kv.astype(F32)).astype(BF16)

    loop(sz.n, unpack, 4)
    qs[sz.tokens :, :] = jnp.zeros((Q_TILE, LANES), BF16)
    kept[sz.tokens :, :] = jnp.zeros((Q_TILE, LANES), F32)

    def one(unit):
        rows = pl.ds(pl.multiple_of(unit * sz.unit_rows, 16), sz.unit_rows)
        begin = pl.multiple_of(first[unit] * sz.unit_rows, 16)

        def keep(shift, mixed):
            total = mixed[:, 0:1]
            left = lane_index((1, LANES)) < HEAD_DIM
            kept[rows, :] = jnp.where(left, shift + jnp.log(total), mixed * (1.0 / total))

        for span in (1, 2, 4):

            @pl.when(count[unit] == span)
            def _():
                clip = pl.ds(begin, span * sz.unit_rows)
                some = dot_cols(qs[rows, :], kvs[pl.ds(begin, 2 * LANES), :])
                shift = jnp.max(some, axis=1, keepdims=True)
                scores = dot_cols(qs[rows, :], kvs[clip, :])
                prob = jnp.exp(scores - shift).astype(BF16)
                keep(shift, dot(prob, ones_v[clip, :]))
                above = jnp.max(jnp.max(scores, axis=1, keepdims=True) - shift)

                @pl.when(above > SAFE_ABOVE)
                def _():
                    scores = dot_cols(qs[rows, :], kvs[clip, :])
                    peak = jnp.max(scores, axis=1, keepdims=True)
                    prob = jnp.exp(scores - peak).astype(BF16)
                    keep(peak, dot(prob, ones_v[clip, :]))

    loop(sz.units, one)

    def pack(src):
        at = pl.multiple_of(src * sz.slot, 16)
        out[src] = fold_head(kept[pl.ds(at, sz.slot), :][: sz.rows], sz, True).astype(BF16)
        left = lane_index((sz.slot - sz.rows, LANES)) < HEAD_DIM
        kept[pl.ds(at + sz.rows, sz.slot - sz.rows), :] = jnp.where(left, MASKED, 0.0)

    loop(sz.n, pack, 4)


def attend(sz, first, count, recv):
    smem = pl.BlockSpec(memory_space=pltpu.SMEM)
    vmem = pl.BlockSpec(memory_space=pltpu.VMEM)
    shape = jax.ShapeDtypeStruct
    return pl.pallas_call(
        lambda *refs: attend_kernel(sz, *refs),
        in_specs=[smem, smem, vmem],
        out_specs=[vmem] * 4,
        out_shape=[
            shape((sz.n, sz.fold, LANES), BF16),
            shape((sz.tokens + Q_TILE, LANES), F32),
            shape((sz.tokens + Q_TILE, LANES), BF16),
            shape((sz.tokens, LANES), BF16),
        ],
        scratch_shapes=[pltpu.VMEM((sz.tokens, LANES), BF16)],
        compiler_params=params(),
        cost_estimate=cost(32),
        name="attend",
    )(first, count, recv)


def back_tiles(sz, part, first, count, qs, kvs, dos, kept, grad_q, grad_kv, key_t):
    def one(unit):
        begin = pl.multiple_of(unit * sz.unit_rows, 16)
        for span in (1, 2, 4):

            @pl.when((count[unit] == span) & (first[unit] == unit))
            def _():
                length = span * sz.unit_rows
                clip = pl.ds(begin, length)
                turned = kvs[clip, :].astype(F32).T[:HEAD_DIM]
                real = lax.rem(lane_index((1, length)), sz.slot) < sz.rows
                key_t[:, 0:length] = jnp.where(real, turned, 0.0).astype(BF16)

                def q_tile(t, carry):
                    rows = pl.ds(pl.multiple_of(begin + t * Q_TILE, 16), Q_TILE)
                    query = qs[rows, :]
                    grad = dos[rows, :]
                    kept_rows = kept[rows, :]
                    left = lane_index((Q_TILE, LANES)) < HEAD_DIM
                    turned = jnp.where(left, kept_rows, kept_rows * grad.astype(F32)).T
                    inside = lane_index((1, Q_TILE)) < length - t * Q_TILE
                    log_total = jnp.where(inside, turned[0:1, :], MASKED)
                    delta = jnp.sum(turned[HEAD_DIM:, :], axis=0, keepdims=True)
                    keys = kvs[clip, :]
                    prob = jnp.exp(dot_cols(keys, query) - log_total)
                    grad_prob = dot_cols(keys, grad)
                    grad_scores = (prob * (grad_prob - delta)).astype(BF16)
                    grad_kv[clip, :] += dot(grad_scores, query) + dot(prob.astype(BF16), grad)
                    grad_query = dot(key_t[:, 0:length], grad_scores) * 0.125
                    grad_query = jnp.concatenate([grad_query, jnp.zeros_like(grad_query)], axis=0).T
                    if part == 1:
                        own = lax.broadcasted_iota(jnp.int32, (Q_TILE, 1), 0) < length - t * Q_TILE
                        grad_query = jnp.where(own, grad_query, grad_q[rows, :])
                    grad_q[rows, :] = grad_query
                    return carry

                tiles = (length + Q_TILE - 1) // Q_TILE
                middle = (tiles * BACK_SHARE[0] + BACK_SHARE[1] - 1) // BACK_SHARE[1]
                lax.fori_loop(*((0, middle) if part == 0 else (middle, tiles)), q_tile, 0)

    loop(sz.units, one)


def back_first_kernel(sz, first, count, recv_grad, qs, kvs, kept, dos, grad_q, grad_kv, key_t):
    dos[sz.tokens :, :] = jnp.zeros((Q_TILE, LANES), BF16)

    def unpack(src):
        at = pl.multiple_of(src * sz.slot, 16)
        unfold_into(dos, at, recv_grad[src], sz, True)
        grad_kv[pl.ds(at, sz.slot), :] = jnp.zeros((sz.slot, LANES), F32)

    loop(sz.n, unpack, 4)
    back_tiles(sz, 0, first, count, qs, kvs, dos, kept, grad_q, grad_kv, key_t)


def back_last_kernel(
    sz, first, count, dos, qs, kvs, kept, grad_q_in, grad_kv_in, turns, out, grad_q, grad_kv, key_t
):
    def copy(src):
        rows = pl.ds(pl.multiple_of(src * sz.slot, 16), sz.slot)
        grad_q[rows, :] = grad_q_in[rows, :]
        grad_kv[rows, :] = grad_kv_in[rows, :]

    loop(sz.n, copy)
    back_tiles(sz, 1, first, count, qs, kvs, dos, kept, grad_q, grad_kv, key_t)

    def pack(src):
        rows = pl.ds(pl.multiple_of(src * sz.slot, 16), sz.slot)
        kv = grad_kv[rows, :]
        left = lane_index((1, LANES)) < HEAD_DIM
        real = lax.broadcasted_iota(jnp.int32, (sz.slot, 1), 0) < sz.rows
        both = jnp.where(left, grad_q[rows, :], swap_halves(kv))
        table = turns[rows, :]
        other = swap_halves(table)
        both = rotate_pair(both, jnp.where(left, table, other), jnp.where(left, other, table), True)
        out[src, 0 : sz.slot, :] = jnp.where(real, jnp.where(left, swap_halves(both), kv), 0.0).astype(BF16)
        out[src, sz.slot :, :] = fold_head(both[: sz.rows], sz, False).astype(BF16)

    loop(sz.n, pack, 4)


def attend_back_first(sz, first, count, recv_grad, qs, kvs, kept):
    smem = pl.BlockSpec(memory_space=pltpu.SMEM)
    vmem = pl.BlockSpec(memory_space=pltpu.VMEM)
    shape = jax.ShapeDtypeStruct
    return pl.pallas_call(
        lambda *refs: back_first_kernel(sz, *refs),
        in_specs=[smem, smem] + [vmem] * 4,
        out_specs=[vmem] * 3,
        out_shape=[
            shape((sz.tokens + Q_TILE, LANES), BF16),
            shape((sz.tokens + Q_TILE, LANES), F32),
            shape((sz.tokens, LANES), F32),
        ],
        scratch_shapes=[pltpu.VMEM((HEAD_DIM, CLIP_MAX // CLIP_MIN * sz.unit_rows), BF16)],
        compiler_params=params(sz, 18),
        cost_estimate=cost(40),
        name="attend_back_first",
    )(first, count, recv_grad, qs, kvs, kept)


def attend_back_last(sz, first, count, dos, qs, kvs, kept, grad_q, grad_kv, turns):
    smem = pl.BlockSpec(memory_space=pltpu.SMEM)
    vmem = pl.BlockSpec(memory_space=pltpu.VMEM)
    shape = jax.ShapeDtypeStruct
    return pl.pallas_call(
        lambda *refs: back_last_kernel(sz, *refs),
        in_specs=[smem, smem] + [vmem] * 7,
        out_specs=vmem,
        out_shape=shape((sz.n, sz.msg, LANES), BF16),
        scratch_shapes=[
            pltpu.VMEM((sz.tokens + Q_TILE, LANES), F32),
            pltpu.VMEM((sz.tokens, LANES), F32),
            pltpu.VMEM((HEAD_DIM, CLIP_MAX // CLIP_MIN * sz.unit_rows), BF16),
        ],
        compiler_params=params(sz, 18),
        cost_estimate=cost(20),
        name="attend_back_last",
    )(first, count, dos, qs, kvs, kept, grad_q, grad_kv, turns)


def triple_grad_kernel(sz, grads, normed, out, total):
    step = pl.program_id(0)
    high = sz.slot - sz.fold
    part_kv = jnp.zeros((LANES, sz.width), F32)
    part_q = jnp.zeros((HEAD_DIM, sz.width), F32)
    sums = jnp.zeros((1, 2 * LANES), F32)
    for src in range(grads.shape[0]):
        key_value = grads[src, 0 : sz.slot, :]
        query = grads[src, sz.slot :, :]
        part_kv = part_kv + dot_rows(key_value, normed[src])
        part_q = part_q + dot_rows(query, normed[src, 0 : sz.fold, :])[:HEAD_DIM]
        part_q = part_q + dot_rows(query[:high], normed[src, sz.fold :, :])[HEAD_DIM:]
        sum_kv = jnp.sum(key_value.astype(F32), axis=0, keepdims=True)
        sum_q = jnp.sum(query.astype(F32), axis=0, keepdims=True)
        sums = sums + jnp.concatenate([sum_kv, sum_q + swap_halves(sum_q)], axis=1)

    @pl.when(step == 0)
    def _():
        total[...] = jnp.zeros_like(total)

    total[0:LANES, :] += part_kv
    total[LANES : LANES + HEAD_DIM, :] += part_q
    total[2 * LANES :, 0 : 2 * LANES] += jnp.broadcast_to(sums, (8, 2 * LANES))

    @pl.when(step == pl.num_programs(0) - 1)
    def _():
        few = sz.width // sz.shards
        bias = total[2 * LANES : 2 * LANES + 1, 0 : 2 * LANES]
        place = lax.broadcasted_iota(jnp.int32, (sz.width, 1), 0) % few
        left = lane_index((1, LANES)) < HEAD_DIM
        out[:, 0:LANES] = total[0:LANES, :].T
        queries = total[LANES : 2 * LANES, :].T
        kv_row, q_row = bias[:, 0:LANES], bias[:, LANES:]
        side = jnp.where(place == 0, swap_halves(kv_row), jnp.where(place == 1, kv_row, 0.0))
        side = jnp.where(place == 2, q_row, side)
        out[:, LANES:] = jnp.where(left, queries, side)


def triple_grad(sz, grads, normed_all):
    shape = jax.ShapeDtypeStruct
    last = sz.n // 2 - 1
    return pl.pallas_call(
        lambda *refs: triple_grad_kernel(sz, *refs),
        grid=(sz.n // 2,),
        in_specs=[
            pl.BlockSpec((2, sz.msg, LANES), lambda j: (j, 0, 0)),
            pl.BlockSpec((2, sz.slot, sz.width), lambda j: (jnp.where(j % 2 == 0, j // 2, last - j // 2), 0, 0)),
        ],
        out_specs=pl.BlockSpec((sz.width, 2 * LANES), lambda j: (0, 0)),
        out_shape=shape((sz.width, 2 * LANES), F32),
        scratch_shapes=[pltpu.VMEM((2 * LANES + 8, sz.width), F32)],
        compiler_params=params(sz, 54),
        cost_estimate=cost(1),
        name="triple_grad",
    )(grads, normed_all)


def choose(pieces, index):
    picked = pieces[0]
    for at in range(1, len(pieces)):
        picked = jnp.where(index == at, pieces[at], picked)
    return picked


def core_cols(block, width, side):
    count = block.shape[1] // (2 * width)
    groups = [block[:, g * width : (g + 1) * width] for g in range(2 * count)]
    return jnp.concatenate([choose(groups[2 * g : 2 * g + 2], side) for g in range(count)], axis=1)


def feed_kernel(sz, place, tok, heads_in, wo, bo, gain, offset, we, be, wr, br, cot, *refs):
    result, grad_hidden, msg, shared, grad_exp, act_sent, act_own = refs[:7]
    small = refs[7]
    hidden, reduced, grad_normed = refs[8:]
    step = pl.program_id(0)
    core = place[0]
    left = lane_index((sz.fold, LANES)) < HEAD_DIM
    normed = shared.at[:, 0 : sz.width]
    attended = shared.at[:, sz.width : 2 * sz.width]

    @pl.when(step == 0)
    def _():
        for pair in range(sz.heads // 2):
            a = heads_in[2 * pair, 0 : sz.fold, :].astype(F32)
            b = heads_in[2 * pair + 1, 0 : sz.fold, :].astype(F32)
            low = jnp.where(left, a, swap_halves(b))
            high = jnp.where(left, swap_halves(a), b)[: sz.rest]
            both = jnp.concatenate([low, high], axis=0)
            attended[:, pair * LANES : (pair + 1) * LANES] = both.astype(BF16)
        rows = tok[...].astype(F32) + (dot(attended[...], wo[...]) + bo[...])
        hidden[...] = rows
        unit, _ = norm_parts(rows)
        normed[...] = (unit * gain[...] + offset[...]).astype(BF16)
        reduced[...] = jnp.zeros_like(reduced)
        grad_normed[...] = jnp.zeros_like(grad_normed)

    expanded = dot(normed[...], we[...]) + be[...]
    below = 0.5 * (1.0 + lax.erf(expanded * 0.7071067811865476))
    bell = jnp.exp(expanded * expanded * -0.5) * 0.3989422804014327
    activated = expanded * below
    slope = below + expanded * bell
    act_low = activated.astype(BF16)
    reduced[...] += dot(act_low, wr[...])
    grad_expanded = (dot_cols(cot[...], wr[...]) * slope).astype(BF16)
    span = act_low.shape[1]
    per = sz.width // span
    lanes = pl.ds(pl.multiple_of(lax.rem(step, per) * span, LANES), span)
    small[pl.ds(4 + step // per, 1), lanes] = jnp.sum(grad_expanded.astype(F32), axis=0, keepdims=True)
    grad_normed[...] += dot_cols(grad_expanded, we[...])
    act_own[...] = core_cols(activated, sz.ff // sz.n, core).astype(BF16)
    act_sent[...] = core_cols(activated, sz.ff // sz.n, 1 - core).astype(BF16)
    grad_exp[...] = grad_expanded

    @pl.when(step == pl.num_programs(0) - 1)
    def _():
        rows = hidden[...]
        out_grad = cot[...].astype(F32)
        result[...] = (rows + (reduced[...] + br[...])).astype(BF16)
        part, gain_part, offset_part = norm_back(grad_normed[...], rows, gain[...])
        total = out_grad + part
        grad_hidden[...] = total
        low = total.astype(BF16)
        small[0:1, :] = jnp.sum(low.astype(F32), axis=0, keepdims=True)
        small[1:2, :] = gain_part
        small[2:3, :] = offset_part
        small[3:4, :] = jnp.sum(out_grad, axis=0, keepdims=True)
        shared[:, 2 * sz.width : 3 * sz.width] = low
        for quarter in range(4):
            wide = sz.width // 4
            grad_attended = dot_cols(low, wo[quarter * wide : (quarter + 1) * wide, :])
            for pair in range(wide // LANES):
                both = grad_attended[:, pair * LANES : (pair + 1) * LANES]
                head = 2 * (quarter * (wide // LANES) + pair)
                msg[head] = fold_head(both, sz, False).astype(BF16)
                msg[head + 1] = fold_head(both, sz, True).astype(BF16)


def feed(sz, place, tokens, heads_in, wo, bo, gain, offset, we, be, wr, br, cot):
    span = 512
    steps = sz.ff // span
    whole = lambda *shape: pl.BlockSpec(shape, lambda j: (0,) * len(shape), pipeline_mode=pl.Buffered(1))
    shape = jax.ShapeDtypeStruct
    vector = whole(1, sz.width)
    return pl.pallas_call(
        lambda *refs: feed_kernel(sz, *refs),
        grid=(steps,),
        in_specs=[
            pl.BlockSpec(memory_space=pltpu.SMEM),
            whole(sz.rows, sz.width),
            whole(sz.heads, sz.fold, LANES),
            whole(sz.width, sz.width),
            vector,
            vector,
            vector,
            pl.BlockSpec((sz.width, span), lambda j: (0, j)),
            pl.BlockSpec((1, span), lambda j: (0, j)),
            pl.BlockSpec((span, sz.width), lambda j: (j, 0)),
            vector,
            whole(sz.rows, sz.width),
        ],
        out_specs=[
            whole(sz.rows, sz.width),
            whole(sz.rows, sz.width),
            whole(sz.heads, sz.fold, LANES),
            whole(sz.rows, 3 * sz.width),
            pl.BlockSpec((sz.rows, span), lambda j: (0, j)),
            pl.BlockSpec((sz.rows, span // 2), lambda j: (0, j)),
            pl.BlockSpec((sz.rows, span // 2), lambda j: (0, j)),
            whole(4 + sz.ff // sz.width, sz.width),
        ],
        out_shape=[
            shape((sz.rows, sz.width), BF16),
            shape((sz.rows, sz.width), F32),
            shape((sz.heads, sz.fold, LANES), BF16),
            shape((sz.rows, 3 * sz.width), BF16),
            shape((sz.rows, sz.ff), BF16),
            shape((sz.rows, sz.ff // 2), BF16),
            shape((sz.rows, sz.ff // 2), BF16),
            shape((4 + sz.ff // sz.width, sz.width), F32),
        ],
        scratch_shapes=[pltpu.VMEM((sz.rows, sz.width), F32)] * 3,
        compiler_params=params(),
        cost_estimate=cost(28),
        name="feed",
    )(place, tokens, heads_in, wo, bo, gain, offset, we, be, wr, br, cot)


def weights_kernel(sz, place, act, act_got, cot, cot_got, back, back_got, norm, norm_got, *refs):
    att, att_got, low, low_got = refs[:4]
    wr_own, wr_sent, first_own, first_sent, next_own, next_sent = refs[4:10]
    wo_out = refs[10 : 10 + sz.m]
    norm_t, norm_t_got = refs[10 + sz.m :]
    step = pl.program_id(0)
    core, low_bit, mine_dp = place[0], place[1], place[1 + sz.bits]
    per = sz.width // sz.n

    def core_rows(block):
        turned = block[...].astype(F32).T.reshape(sz.n // 2, 2, per, sz.rows)
        return choose([turned[:, 0], turned[:, 1]], core).reshape(sz.width // 2, sz.rows).astype(BF16)

    @pl.when(step == 0)
    def _():
        norm_t[...] = core_rows(norm)
        norm_t_got[...] = core_rows(norm_got)
        grad_wo = dot(core_rows(att), low[...]) + dot(core_rows(att_got), low_got[...])
        grad_wo = grad_wo.reshape(sz.n // 2, sz.m, per // sz.m, sz.width)
        sides = [grad_wo[:, q] for q in range(sz.m)]
        for by in range(sz.m):
            wo_out[by][...] = choose(sides, lax.rem(mine_dp + by, sz.m)).astype(BF16)

    groups = act.shape[1] // (sz.ff // sz.n)
    grad_wr = (dot_rows(act[...], cot[...]) + dot_rows(act_got[...], cot_got[...])).astype(BF16)
    grad_wr = grad_wr.reshape(groups, sz.ff // sz.n, sz.width)
    if groups == 1:

        @pl.when(step % 2 == low_bit)
        def _():
            wr_own[...] = grad_wr

        @pl.when(step % 2 != low_bit)
        def _():
            wr_sent[...] = grad_wr

    else:
        wr_own[...] = choose([grad_wr[0:1], grad_wr[1:2]], low_bit)
        wr_sent[...] = choose([grad_wr[0:1], grad_wr[1:2]], 1 - low_bit)
    grad_we = dot(norm_t[...], back[...]) + dot(norm_t_got[...], back_got[...])

    def split(bit, own, sent):
        above, below = sz.n // 4 >> bit, (1 << bit) * sz.m
        parts = grad_we.reshape(above, 2, below, per // sz.m, grad_we.shape[1])
        sides = [parts[:, 0], parts[:, 1]]
        own[...] = choose(sides, place[1 + bit]).astype(BF16).reshape(own.shape)
        sent[...] = choose(sides, 1 - place[1 + bit]).astype(BF16).reshape(sent.shape)

    @pl.when(step < pl.num_programs(0) // 2)
    def _():
        split(2, first_own, first_sent)

    @pl.when(step >= pl.num_programs(0) // 2)
    def _():
        split(1, next_own, next_sent)


def weights(sz, place, act, act_got, cot, cot_got, back, back_got, shared, shared_got):
    span = sz.width
    steps = sz.ff // span
    fan = sz.ff // sz.width
    half = sz.n // 2
    few = sz.width // sz.shards
    whole = lambda *shape: pl.BlockSpec(shape, lambda j: (0,) * len(shape))
    column = lambda k: pl.BlockSpec((sz.rows, sz.width), lambda j: (0, k))
    block = pl.BlockSpec((sz.rows, span), lambda j: (0, j))
    act_block = pl.BlockSpec((sz.rows, span // 2), lambda j: (0, j))
    shape = jax.ShapeDtypeStruct
    groups = half // steps
    wr_block = pl.BlockSpec((1, sz.ff // sz.n, sz.width), lambda j: (j * groups // 2, 0, 0))
    wr_out = shape((half // 2, sz.ff // sz.n, sz.width), BF16)
    wo_dims = (half, few, sz.width)
    last_j = steps // 2 - 1
    first_block = pl.BlockSpec((half // 2 * sz.m, 1, few, span), lambda j: (0, jnp.minimum(j, last_j), 0, 0))
    next_block = pl.BlockSpec((half // 2 * sz.m, 1, few, span), lambda j: (0, jnp.maximum(j - last_j - 1, 0), 0, 0))
    we_out = shape((half // 2 * sz.m, fan // 2, few, sz.width), BF16)
    return pl.pallas_call(
        lambda *refs: weights_kernel(sz, *refs),
        grid=(steps,),
        in_specs=[
            pl.BlockSpec(memory_space=pltpu.SMEM),
            act_block,
            act_block,
            whole(sz.rows, sz.width),
            whole(sz.rows, sz.width),
            block,
            block,
        ]
        + [column(k // 2) for k in range(6)],
        out_specs=[wr_block] * 2 + [first_block] * 2 + [next_block] * 2 + [whole(*wo_dims)] * sz.m,
        out_shape=[wr_out] * 2 + [we_out] * 4 + [shape(wo_dims, BF16)] * sz.m,
        scratch_shapes=[pltpu.VMEM((sz.width // 2, sz.rows), BF16)] * 2,
        compiler_params=params(),
        cost_estimate=cost(10),
        name="weights",
    )(place, act, act_got, cot, cot_got, back, back_got, *([shared, shared_got] * 3))


def finish_kernel(sz, back, wq, wk, wv, tok, gain, grad_hidden, input_grad, grad_normed):
    step = pl.program_id(0)
    left = lane_index((sz.rows, LANES)) < HEAD_DIM
    left_fold = lane_index((sz.fold, LANES)) < HEAD_DIM
    queries, keys, values = [], [], []
    for pair in range(wq.shape[1] // LANES):
        kv_a = back[2 * pair, 0 : sz.rows, :].astype(F32)
        kv_b = back[2 * pair + 1, 0 : sz.rows, :].astype(F32)
        q_a = back[2 * pair, sz.slot : sz.slot + sz.fold, :].astype(F32)
        q_b = back[2 * pair + 1, sz.slot : sz.slot + sz.fold, :].astype(F32)
        low = jnp.where(left_fold, q_a, swap_halves(q_b))
        high = jnp.where(left_fold, swap_halves(q_a), q_b)[: sz.rest]
        queries.append(jnp.concatenate([low, high], axis=0).astype(BF16))
        keys.append(jnp.where(left, kv_a, swap_halves(kv_b)).astype(BF16))
        values.append(jnp.where(left, swap_halves(kv_a), kv_b).astype(BF16))
    total = jnp.zeros((sz.rows, sz.width), F32)
    for parts, weight in ((queries, wq), (keys, wk), (values, wv)):
        total = total + dot_cols(jnp.concatenate(parts, axis=1), weight[...])

    @pl.when(step == 0)
    def _():
        grad_normed[...] = total

    @pl.when(step > 0)
    def _():
        grad_normed[...] += total

    @pl.when(step == pl.num_programs(0) - 1)
    def _():
        part, _, _ = norm_back(grad_normed[...], tok[...].astype(F32), gain[...])
        input_grad[...] = grad_hidden[...] + part


def finish(sz, back, weight, tokens, gain, grad_hidden):
    cols = 512
    steps = sz.width // cols
    whole = lambda *shape: pl.BlockSpec(shape, lambda j: (0,) * len(shape))
    part = lambda k: pl.BlockSpec((sz.width, cols), lambda j: (0, k * steps + j))
    return pl.pallas_call(
        lambda *refs: finish_kernel(sz, *refs),
        grid=(steps,),
        in_specs=[
            pl.BlockSpec((cols // HEAD_DIM, sz.msg, LANES), lambda j: (j, 0, 0)),
            part(0),
            part(1),
            part(2),
            whole(sz.rows, sz.width),
            whole(1, sz.width),
            whole(sz.rows, sz.width),
        ],
        out_specs=whole(sz.rows, sz.width),
        out_shape=jax.ShapeDtypeStruct((sz.rows, sz.width), F32),
        scratch_shapes=[pltpu.VMEM((sz.rows, sz.width), F32)],
        compiler_params=params(sz, 54),
        cost_estimate=cost(10),
        name="finish",
    )(back, weight, weight, weight, tokens, gain, grad_hidden)


def pick(array, axis, index):
    return lax.dynamic_index_in_dim(array, index, axis, keepdims=False)


def after(value, *others):
    return lax.optimization_barrier((value,) + others)[0]


class Side:
    def __init__(self, sz, labels, rows, arrays):
        self.dims = [(label, sz.m if label == "dp" else 2) for label in labels]
        self.rows = rows
        self.width = sz.width
        self.arrays = list(arrays)

    def split(self, label):
        at = [name for name, _ in self.dims].index(label)
        before, after_it = 1, self.rows
        for _, size in self.dims[:at]:
            before *= size
        for _, size in self.dims[at + 1 :]:
            after_it *= size
        count = self.dims[at][1]
        self.dims = self.dims[:at] + self.dims[at + 1 :]
        return before, count, after_it

    def total(self):
        return sum(array.astype(F32) for array in self.arrays).reshape(self.rows, self.width)


def halve_kernel(shapes, place, *refs):
    at = 0
    outs = sum(adds * count for adds, count in shapes)
    for adds, count in shapes:
        for _ in range(count):
            total = refs[at][:, 0].astype(F32)
            for more in range(1, adds):
                total = total + refs[at + more][:, 0].astype(F32)
            refs[outs][...] = total.astype(BF16)
            at += adds
            outs += 1


def halve(sz, place, sides, labels, mib=63):
    parts = [side.split(label) for side, label in zip(sides, labels)]
    grid = 2 if all(before % 2 == 0 for before, _, _ in parts) else 1
    ins, in_specs, out_specs, out_shape = [], [], [], []
    for side, label, (before, count, rest) in zip(sides, labels, parts):
        which = 1 + sz.bits if label == "dp" else 1 + label
        for by in range(count):
            for array in side.arrays:
                ins.append(array.reshape(before, count, rest, sz.width))
                in_specs.append(
                    pl.BlockSpec(
                        (before // grid, 1, rest, sz.width),
                        lambda g, place, which=which, by=by, count=count: (g, lax.rem(place[which] + by, count), 0, 0),
                    )
                )
            out_specs.append(pl.BlockSpec((before // grid, rest, sz.width), lambda g, place: (g, 0, 0)))
            out_shape.append(jax.ShapeDtypeStruct((before, rest, sz.width), BF16))
    shapes = [(len(side.arrays), count) for side, (_, count, _) in zip(sides, parts)]
    outs = pl.pallas_call(
        lambda *refs: halve_kernel(shapes, *refs),
        grid_spec=pltpu.PrefetchScalarGridSpec(
            num_scalar_prefetch=1, grid=(grid,), in_specs=in_specs, out_specs=out_specs
        ),
        out_shape=out_shape,
        compiler_params=params(sz, mib),
        cost_estimate=cost(4),
        name="halve",
    )(place, *ins)
    sent = []
    for side, (_, count, _) in zip(sides, parts):
        side.arrays = [outs[0]]
        sent.append(list(outs[1:count]))
        outs = outs[count:]
    return sent


def send(sz, label, blocks):
    if label == "dp":
        return [
            lax.ppermute(block, "dp", [(i, (i + by + 1) % sz.m) for i in range(sz.m)])
            for by, block in enumerate(blocks)
        ]
    bit = 2 << label
    return [lax.ppermute(block, "seq", [(i, i ^ bit) for i in range(sz.n)]) for block in blocks]


def swap(sz, block, by):
    return block if by == 0 else lax.ppermute(block, "seq", [(i, i ^ by) for i in range(sz.n)])


def trade_near(sz, blocks):
    me = lax.axis_index("seq")
    blocks = blocks.reshape((sz.n // 4, 4) + blocks.shape[1:])
    return jnp.stack([swap(sz, pick(blocks, 1, me % 4 ^ by), by) for by in range(4)], axis=1)


def trade_far(sz, near):
    me = lax.axis_index("seq")
    return jnp.stack([swap(sz, pick(near, 0, me // 4 ^ by), 4 * by) for by in range(sz.n // 4)], axis=0)


def last_kernel(sz, adds, spans, place, far, gain, offset, weight, *refs):
    ins, outs = refs[: sum(adds)], refs[sum(adds) :]
    totals = []
    for count in adds:
        total = ins[0][...].astype(F32)
        for more in range(1, count):
            total = total + ins[more][...].astype(F32)
        totals.append(total)
        ins = ins[count:]
    wr, we, wo, wt, bias_all, gain_one, offset_one = outs[:7]
    few = sz.width // sz.shards
    wr[...] = totals[0]
    half = sz.ff // sz.width // 2
    for part in range(2 * half):
        rows = totals[1 + part // half][part % half * few : (part % half + 1) * few]
        we[:, part * sz.width : (part + 1) * sz.width] = rows
    wo[...] = totals[3]
    low = place[0] + 2 * place[1]
    high = place[2]
    for bit in range(2, sz.bits):
        high = high + place[1 + bit] * 2 ** (bit - 1)

    def piece(src):
        return far[jnp.bitwise_xor(high, src // 4), jnp.bitwise_xor(low, src % 4)].astype(F32)

    left = lane_index((1, LANES)) < HEAD_DIM
    small = jnp.zeros((8, LANES), F32)
    along = jnp.zeros((8, LANES), F32)
    moved = jnp.zeros((few, 1), F32)
    for pair in range(sz.heads // 2):
        a = piece(2 * pair * sz.rep)
        b = piece((2 * pair + 1) * sz.rep)
        kv_a, kv_b, q_a, q_b = a[:, :LANES], b[:, :LANES], a[:, LANES:], b[:, LANES:]
        along = along + q_a[:8] + q_b[:8]
        blocks = (
            jnp.where(left, q_a, swap_halves(q_b)),
            jnp.where(left, kv_a, swap_halves(kv_b)),
            jnp.where(left, swap_halves(kv_a), kv_b),
        )
        side = jnp.where(left, swap_halves(q_a[:8]), q_b[:8])
        for part, row in ((0, 2), (1, 0), (2, 1)):
            cols = slice(part * sz.width + pair * LANES, part * sz.width + (pair + 1) * LANES)
            wt[:, cols] = blocks[part]
            bias_all[:, cols] = side[row : row + 1]
            rows = weight[:, cols].astype(F32) * side[row : row + 1]
            moved = moved + jnp.sum(rows, axis=1, keepdims=True)
    for src in range(sz.n):
        small = small + piece(src)[:8, LANES:]
    along = swap_halves(along)[7:8]
    small = swap_halves(small)
    small = jnp.concatenate([small[3 + row : 4 + row, :HEAD_DIM] for row in range(4)], axis=1)
    moved = jnp.broadcast_to(moved, (few, LANES)).T[0:1]
    offset_one[...] = moved
    gain_one[...] = (along[:, :few] - offset[0] * moved) / gain[0]
    at = 0
    for out, span in zip(outs[7:], spans):
        out[...] = small[:, at : at + span]
        at += span


def last(sz, place, sides, far, gain, offset, weight, spans):
    few = sz.width // sz.shards
    shard = lambda g, place: (place[2 + sz.bits], 0, 0)
    whole = lambda *shape: pl.BlockSpec(shape, lambda g, place: (0,) * len(shape))
    ins, in_specs = [], []
    for side in sides:
        for array in side.arrays:
            ins.append(array.reshape(side.rows, sz.width))
            in_specs.append(whole(side.rows, sz.width))
    out_dims = [(sides[0].rows, sz.width), (few, sz.ff), (few, sz.width), (few, 3 * sz.width), (1, 3 * sz.width)]
    out_dims = out_dims + [(1, few), (1, few)] + [(1, span) for span in spans]
    return pl.pallas_call(
        lambda *refs: last_kernel(sz, [len(side.arrays) for side in sides], spans, *refs),
        grid_spec=pltpu.PrefetchScalarGridSpec(
            num_scalar_prefetch=1,
            grid=(1,),
            in_specs=[
                whole(*far.shape),
                pl.BlockSpec((1, 1, few), shard),
                pl.BlockSpec((1, 1, few), shard),
                pl.BlockSpec((few, 3 * sz.width), lambda g, place: (place[2 + sz.bits], 0)),
            ]
            + in_specs,
            out_specs=[whole(*dims) for dims in out_dims],
        ),
        out_shape=[jax.ShapeDtypeStruct(dims, F32) for dims in out_dims],
        compiler_params=params(sz, 50),
        cost_estimate=cost(5),
        name="last",
    )(place, far, gain.reshape(sz.shards, 1, few), offset.reshape(sz.shards, 1, few), weight, *ins)


def per_device(
    tokens,
    clip_start,
    frames,
    positions,
    first_gain,
    first_offset,
    triple_weight,
    triple_bias,
    output_weight,
    output_bias,
    second_gain,
    second_offset,
    expand_weight,
    expand_bias,
    reduce_weight,
    reduce_bias,
    cotangent,
):
    rows, width = tokens.shape[1:]
    ff = expand_weight.shape[1]
    n = lax.axis_size("seq")
    m = lax.axis_size("dp")
    slabs = clip_start.shape[1]
    sz = Sizes(rows, width, ff, n, m, slabs)
    shards = n * m
    group_slabs = n * slabs
    lower, upper = slab_bounds(clip_start[0], frames[0], lax.axis_index("seq") * slabs, group_slabs)
    first_unit = lower[0] // CLIP_MIN
    unit_count = (upper[0] - lower[0]) // CLIP_MIN
    corners = positions[0].reshape(3, slabs, -1)[:, :, 0].T.reshape(-1)
    own_facts = jnp.concatenate([jnp.stack([first_unit, unit_count]), corners]).astype(jnp.int32)
    row = lambda vector: vector.reshape(1, -1)
    me, mine_dp = lax.axis_index("seq"), lax.axis_index("dp")
    place = jnp.stack([me % 2] + [me // (2 << bit) % 2 for bit in range(sz.bits)] + [mine_dp, me * m + mine_dp])
    swap_core = lambda block: lax.ppermute(block, "seq", [(i, i ^ 1) for i in range(n)])

    def exchange(message):
        if sz.rep > 1:
            message = jnp.repeat(message, sz.rep, axis=0)
        return lax.all_to_all(message, "seq", 0, 0, tiled=True)

    cot_got = swap_core(cotangent[0])
    head = me // sz.rep * HEAD_DIM
    head_weight = [
        lax.dynamic_slice(triple_weight, (0, k * width + head), (width, HEAD_DIM)) for k in (1, 2, 0)
    ]
    head_weight = jnp.concatenate(head_weight + [jnp.zeros((width, HEAD_DIM), BF16)], axis=1)
    message, normed = project(
        sz, own_facts, tokens[0], row(first_gain), row(first_offset), triple_weight, row(triple_bias)
    )
    recv = exchange(message)
    chips = list(range(0, n // 2, 2)) + list(range(n // 2 - 1, 0, -2))
    ring = [2 * chip + core for chip in chips for core in range(2)]
    normed_all = lax.all_gather(after(normed, recv), "seq", axis=0, tiled=False, axis_index_groups=[ring])
    facts = recv[:, sz.msg - 8 :, LANES - 1].astype(jnp.int32)
    unit_first, unit_span = facts[:: sz.per_unit, 0], facts[:: sz.per_unit, 1]
    turns = all_turns(all_places(sz, facts[:, 2:]))
    out_message, kept, qs, kvs = attend(sz, unit_first, unit_span, recv)
    heads_in = lax.all_to_all(out_message, "seq", 0, 0, tiled=True)[:: sz.rep]
    (
        result,
        grad_hidden,
        grad_message,
        shared,
        grad_exp,
        act_sent,
        act_own,
        small,
    ) = feed(
        sz,
        place,
        tokens[0],
        after(heads_in, turns, head_weight),
        output_weight,
        row(output_bias),
        row(second_gain),
        row(second_offset),
        expand_weight,
        row(expand_bias),
        reduce_weight,
        row(reduce_bias),
        cotangent[0],
    )
    recv_grad = exchange(grad_message)
    half = n // 2
    fan = ff // width
    few = width // shards
    many = ff // shards
    wr_own, wr_sent, first_own, first_sent, next_own, next_sent, *wo_parts = weights(
        sz,
        place,
        act_own,
        swap_core(act_sent),
        cotangent[0],
        cot_got,
        grad_exp,
        swap_core(grad_exp),
        shared,
        swap_core(shared),
    )
    bits = list(range(sz.bits - 1, -1, -1))
    side_r = Side(sz, bits[:-1] + ["dp"], many, [wr_own])
    without = lambda label: [bit for bit in bits if bit != label] + ["dp"]
    side_e = Side(sz, without(2), many // 2, [first_own])
    side_f = Side(sz, without(1), many // 2, [next_own])
    side_o = Side(sz, bits, few, [wo_parts[0]])
    sides = [side_r, side_e, side_f, side_o]
    sent = [[wr_sent], [first_sent], [next_sent], wo_parts[1:]]
    rounds = [(0, 2, 1, "dp"), (1, "dp", 0, 2), ("dp", 0, "dp", 0), (2, 1, 2, 1)]
    rounds = rounds + [(bit,) * 4 for bit in range(3, sz.bits)]

    def move(labels):
        return [send(sz, label, blocks) for label, blocks in zip(labels, sent)]

    def add(got, marker):
        for side, blocks in zip(sides, got):
            side.arrays = side.arrays + list(after(blocks, marker))

    got = move(rounds[0])
    dos, grad_q, grad_kv = attend_back_first(
        sz, unit_first, unit_span, after(recv_grad, wo_parts[0]), qs, kvs, kept
    )
    add(got, grad_kv)
    sent = halve(sz, place, sides, rounds[1], 20)
    got = move(rounds[1])
    back_message = attend_back_last(
        sz, unit_first, unit_span, after(dos, sent), qs, kvs, kept, grad_q, grad_kv, turns
    )
    back = lax.all_to_all(after(back_message, got), "seq", 0, 0, tiled=True)[:: sz.rep]
    add(got, back_message)
    sent = halve(sz, place, sides, rounds[2], 20)
    got = move(rounds[2])
    head_grad = triple_grad(sz, after(back_message, sent), normed_all)
    small = after(small, back_message)
    small = [small[:4].reshape(4, shards, few).transpose(1, 0, 2).reshape(shards, -1), small[4:].reshape(shards, -1)]
    small = jnp.concatenate(small, axis=1)
    spans = [few] * 4 + [fan * few]
    small = jnp.pad(small, ((0, 0), (0, 4 * HEAD_DIM - small.shape[1]))).reshape(shards, 4, HEAD_DIM)
    head_grad = after(head_grad, got)
    along = jnp.sum(head_grad * head_weight.astype(F32), axis=1).reshape(shards, 1, few)
    along = jnp.pad(along, ((0, 0), (0, 0), (0, HEAD_DIM - few)))
    spare = jnp.concatenate([small, along], axis=1)
    spare = jnp.pad(spare, ((0, 0), (3, few - 8), (3 * HEAD_DIM, 0)))
    head_parts = (head_grad.reshape(shards, few, 4 * HEAD_DIM) + spare).reshape(n, m, few, 4 * HEAD_DIM)
    head_sum = pick(head_parts, 1, mine_dp)
    for by in range(1, m):
        block = pick(head_parts, 1, (mine_dp + by) % m).astype(BF16)
        head_sum = head_sum + lax.ppermute(block, "dp", [(i, (i + by) % m) for i in range(m)]).astype(F32)
    near = trade_near(sz, head_sum.astype(BF16))
    back = after(back, near)
    add(got, back_message)
    for step, labels in enumerate(rounds[3:]):
        if step > 0:
            add(got, back)
        sent = after(halve(sz, place, sides, labels), back)
        got = move(labels)
    far = trade_far(sz, near)
    input_grad = finish(
        sz, after(back, sent, far), triple_weight, tokens[0], row(first_gain), grad_hidden
    )
    add(got, input_grad)
    (
        out_wr,
        out_we,
        out_wo,
        out_wt,
        bias_all,
        gain_one,
        offset_one,
        *vectors,
    ) = last(sz, place, sides, far, first_gain, first_offset, triple_weight, spans)
    shard = me * m + mine_dp
    bias_qk = lax.dynamic_slice(bias_all[0], (shard * 2 * few,), (2 * few,))
    bias_v = lax.dynamic_slice(bias_all[0], (2 * width + shard * few,), (few,))
    gain_one, offset_one = gain_one[0], offset_one[0]
    bias_o, gain_two, offset_two, bias_r, bias_e = [vector[0] for vector in vectors]
    return (
        result[None],
        input_grad[None],
        gain_one,
        offset_one,
        out_wt,
        bias_qk,
        bias_v,
        out_wo,
        bias_o,
        gain_two,
        offset_two,
        out_we,
        bias_e,
        out_wr,
        bias_r,
    )


def solution(mesh):
    sharded = P("dp", "seq", None)
    placed = (
        (sharded, P("dp", "seq"), P("dp", "seq"), P("dp", None, "seq"))
        + (P(),) * 12
        + (sharded,)
    )
    vector = P(("seq", "dp"))
    matrix = P(("seq", "dp"), None)
    return jax.shard_map(
        per_device,
        mesh=mesh,
        in_specs=placed,
        out_specs=(sharded, sharded, vector, vector, matrix, vector, vector, matrix, vector)
        + (vector, vector, matrix, vector, matrix, vector),
        check_vma=False,
    )
```
